32 devices in a mesh: dp: 16 (over z, x, core), rep: 2 (over y).
Axes of the slice: x: 2, y: 2, z: 4, core: 2. Of those that a mesh axis runs over, the one named last changes fastest.
Arguments:
- block_input: float32 [65536, 384], P(('dp', 'rep')), may hold values from -6 to 6
- expert_out: float32 [65536, 207], P(('dp', 'rep')), may hold values from -6 to 6
- upstream: float32 [65536, 69], P(('dp', 'rep')), may hold values from -6 to 6
- lead_index: int32 [32], P(('dp', 'rep')), may hold values from 0 to 39
- lead_frames: int32 [40], replicated, may hold values from 1000 to 7999
- lead_embed: float32 [40, 384], replicated, may hold values from -3 to 3
- first_gain: float32 [384], replicated, may hold values from 0.5 to 1.5
- first_shift: float32 [384], replicated, may hold values from -0.625 to 0.625
- attend_weight: bfloat16 [384, 1152], replicated, may hold values from -0.3125 to 0.3125
- query_bias: float32 [384], replicated, may hold values from -0.625 to 0.625
- value_bias: float32 [384], replicated, may hold values from -0.125 to 0.125
- merge_weight: bfloat16 [384, 384], replicated, may hold values from -6 to 6
- merge_bias: float32 [384], replicated, may hold values from -0.625 to 0.625
- second_gain: float32 [384], replicated, may hold values from 0.5 to 1.5
- second_shift: float32 [384], replicated, may hold values from -0.625 to 0.625
- expand_weight: bfloat16 [384, 1536], replicated, may hold values from -0.3125 to 0.3125
- expand_bias: float32 [1536], replicated, may hold values from -0.625 to 0.625
- shrink_weight: bfloat16 [1536, 384], replicated, may hold values from -0.15625 to 0.15625
- shrink_bias: float32 [384], replicated, may hold values from -0.625 to 0.625
- router_weight: bfloat16 [384, 207], replicated, may hold values from -0.15625 to 0.15625
- router_bias: float32 [207], replicated, may hold values from -0.4375 to 0.4375
- correction: float32 [69], replicated, may hold values from -1.75 to 1.75
Outputs:
- blended: float32 [65536, 69], P(('dp', 'rep'))
- grad_input: float32 [65536, 384], P(('dp', 'rep'))
- grad_lead_embed: float32 [40, 384], replicated
- grad_first_gain: float32 [384], replicated
- grad_first_shift: float32 [384], replicated
- grad_attend_weight: float32 [384, 1152], replicated
- grad_query_bias: float32 [384], replicated
- grad_value_bias: float32 [384], replicated
- grad_merge_weight: float32 [384, 384], replicated
- grad_merge_bias: float32 [384], replicated
- grad_second_gain: float32 [384], replicated
- grad_second_shift: float32 [384], replicated
- grad_expand_weight: float32 [384, 1536], replicated
- grad_expand_bias: float32 [1536], replicated
- grad_shrink_weight: float32 [1536, 384], replicated
- grad_shrink_bias: float32 [384], replicated
- grad_router_weight: float32 [384, 207], replicated
- grad_router_bias: float32 [207], replicated
- grad_correction: float32 [69], replicated
The draws below stay inside these ranges and needn't reach their ends.
All inputs are finite; a program needn't handle non-finite values.
Results may differ from the reference program's by a relative error of at most 0.0068.
Values sent between devices are 32-bit elements; how exact they have to be, the bound alone decides.
No kernel may reach another device: no remote copies, remote signals or barrier semaphores. Data moves between devices by JAX's collectives and lax.ppermute only.
A program may use at most 256 MiB of HBM per device.

```python
import jax
import jax.numpy as jnp
from jax import lax

D = 384
HEADS = 6
HEAD_DIM = 64
FF = 1536
EXPERTS = 3
CHANNELS = 69
LEADS = 40
FRAME = 2048
QBLOCK = 512
FRAMES = 32
TOKENS = 65536


def touch_ends(result, own_key, least, high):
    dims = result.shape
    spot = [jax.random.randint(jax.random.fold_in(own_key, axis), (), 0, dims[axis]) for axis in range(len(dims))]
    result = result.at[tuple(spot)].set(least)
    longest = dims.index(max(dims))
    spot[longest] = (spot[longest] + 1) % dims[longest]
    return result.at[tuple(spot)].set(high)


def level_of(stream_key, shape, pieces, low, top_value):
    def one(axis_at, parts):
        draws = jax.random.uniform(jax.random.fold_in(jax.random.fold_in(stream_key, 6), axis_at), (parts,), jnp.float32, low / len(pieces), top_value / len(pieces))
        return jnp.repeat(jnp.exp(draws), shape[axis_at] // parts).reshape((-1,) + (1,) * (len(shape) - axis_at - 1))

    factor_of = one(*pieces[0])
    for cut in pieces[1:]:
        factor_of = factor_of * one(*cut)
    return factor_of


def bell_draw(rng, dims, scale, reach, pieces=(), kind=jnp.bfloat16):
    drawn = jax.random.normal(rng, dims, jnp.float32) * scale
    if len(pieces) > 0:
        drawn = level_of(rng, dims, pieces, -0.22, 0.18) * drawn
    return jnp.clip(drawn, min=-reach, max=reach).astype(kind)


def setup_inputs(seed: int = 0) -> dict:
    key_of = jax.random.split(jax.random.key(seed), 23)
    return {
        "block_input": bell_draw(key_of[0], (TOKENS, D), 1.0, 6.0, ((0, 32),), jnp.float32),
        "expert_out": bell_draw(key_of[1], (TOKENS, EXPERTS * CHANNELS), 1.0, 6.0, ((0, 32),), jnp.float32),
        "upstream": bell_draw(key_of[2], (TOKENS, CHANNELS), 1.0, 6.0, ((0, 32),), jnp.float32),
        "lead_index": touch_ends(jax.random.randint(key_of[3], (FRAMES,), 0, LEADS), jax.random.fold_in(key_of[3], 1), 0, LEADS - 1).astype(jnp.int32),
        "lead_frames": touch_ends(jax.random.randint(key_of[4], (LEADS,), 1000, 8000), jax.random.fold_in(key_of[4], 1), 1000, 7999).astype(jnp.int32),
        "lead_embed": bell_draw(key_of[5], (LEADS, D), 0.5, 3.0, (), jnp.float32),
        "first_gain": jnp.clip(1.0 + 0.1 * jax.random.normal(key_of[6], (D,), jnp.float32), 0.5, 1.5),
        "first_shift": bell_draw(key_of[7], (D,), 0.1, 0.625, (), jnp.float32),
        "attend_weight": bell_draw(key_of[8], (D, 3 * D), D ** -0.5, 0.3125),
        "query_bias": bell_draw(key_of[9], (D,), 0.1, 0.625, (), jnp.float32),
        "value_bias": bell_draw(key_of[10], (D,), 0.02, 0.125, (), jnp.float32),
        "merge_weight": bell_draw(key_of[11], (D, D), (max(1, D * 3 // FRAME)) ** -0.5, 6.0),
        "merge_bias": bell_draw(key_of[12], (D,), 0.1, 0.625, (), jnp.float32),
        "second_gain": jnp.clip(1.0 + 0.1 * jax.random.normal(key_of[13], (D,), jnp.float32), 0.5, 1.5),
        "second_shift": bell_draw(key_of[14], (D,), 0.1, 0.625, (), jnp.float32),
        "expand_weight": bell_draw(key_of[15], (D, FF), D ** -0.5, 0.3125),
        "expand_bias": bell_draw(key_of[16], (FF,), 0.1, 0.625, (), jnp.float32),
        "shrink_weight": bell_draw(key_of[17], (FF, D), FF ** -0.5, 0.15625),
        "shrink_bias": bell_draw(key_of[18], (D,), 0.1, 0.625, (), jnp.float32),
        "router_weight": bell_draw(key_of[19], (D, EXPERTS * CHANNELS), (4 * D) ** -0.5, 0.15625),
        "router_bias": bell_draw(key_of[20], (EXPERTS * CHANNELS,), 0.07, 0.4375, (), jnp.float32),
        "correction": bell_draw(key_of[21], (CHANNELS,), 0.3, 1.75, (), jnp.float32),
    }


@jax.custom_vjp
def low(v):
    return lax.optimization_barrier(v.astype(jnp.bfloat16)).astype(jnp.float32)

@jax.custom_vjp
def low_back(v):
    return v

def low_keep(v):
    return (low(v), None)

def low_pass(kept, grad):
    return (grad,)

def back_keep(v):
    return (v, None)

def back_low(kept, grad):
    return (low(grad),)
low.defvjp(low_keep, low_pass)
low_back.defvjp(back_keep, back_low)
EPSILON = 1e-05
PENALTY = 1.0
GELU_COEF = 0.7978845608028654

def matmul(left, right):
    return jnp.dot(left, right, precision=lax.Precision.HIGHEST, preferred_element_type=jnp.float32)

def norm_rows(values, scaling, offset):
    centre = lax.optimization_barrier(jnp.mean(values, axis=-1, keepdims=True))
    centred = values - centre
    spread = lax.optimization_barrier(jnp.mean(centred * centred, axis=-1, keepdims=True))
    return centred * lax.rsqrt(spread + EPSILON) * scaling + offset

def gelu_tanh(values):
    return 0.5 * values * (1.0 + jnp.tanh(GELU_COEF * (values + 0.044715 * values * values * values)))

def expert_head(logits, correction, expert_frame):
    row_count = logits.shape[0]
    channels = correction.shape[0]
    grouped = logits.reshape(row_count, -1, channels)
    largest = lax.optimization_barrier(jnp.max(grouped, axis=1, keepdims=True))
    shifted = grouped - largest
    log_gates = shifted - jnp.log(lax.optimization_barrier(jnp.sum(jnp.exp(shifted), axis=1, keepdims=True)))
    gate_probs = jnp.exp(log_gates)
    blended = lax.optimization_barrier(jnp.sum(gate_probs * expert_frame.reshape(row_count, -1, channels), axis=1)) + correction
    entropy = -jnp.sum(gate_probs * log_gates)
    return (blended, entropy)

def attend(projected):
    queries = projected[:, :D].reshape(FRAME, HEADS, HEAD_DIM)
    key_rows = projected[:, D:2 * D].reshape(FRAME, HEADS, HEAD_DIM)
    values = projected[:, 2 * D:].reshape(FRAME, HEADS, HEAD_DIM)
    scaling = HEAD_DIM ** (-0.5)

    def block_out(offset):
        query_block = lax.dynamic_slice_in_dim(queries, offset, QBLOCK, 0)
        scores = low_back(jnp.einsum('qhd,khd->hqk', query_block, key_rows, precision=lax.Precision.HIGHEST) * scaling)
        largest = lax.optimization_barrier(jnp.max(scores, axis=-1, keepdims=True))
        raised = jnp.exp(scores - largest)
        softmax_out = low(raised / lax.optimization_barrier(jnp.sum(raised, axis=-1, keepdims=True)))
        mixed_rows = jnp.einsum('hqk,khd->qhd', softmax_out, values, precision=lax.Precision.HIGHEST)
        return mixed_rows.reshape(QBLOCK, D)
    offsets = jnp.arange(FRAME // QBLOCK, dtype=jnp.int32) * QBLOCK
    return lax.map(jax.checkpoint(block_out), offsets).reshape(FRAME, D)

def frame_forward(params, frame_in, expert_frame, upstream_frame, lead_id, weight):
    lead_embed, first_gain, first_shift, attend_weight, query_bias, value_bias, merge_weight, merge_bias, second_gain, second_shift, expand_weight, expand_bias, shrink_weight, shrink_bias, router_weight, router_bias, correction = params
    stream = frame_in + lax.dynamic_index_in_dim(lead_embed, lead_id, 0, keepdims=False)[None, :]
    first_norm = low(norm_rows(stream, first_gain, first_shift))
    bias_rows = jnp.concatenate([query_bias, jnp.zeros_like(query_bias), value_bias])
    projected = low(low_back(matmul(first_norm, attend_weight) + bias_rows))
    mixed_heads = low(low_back(attend(projected)))
    stream_mid = stream + low_back(matmul(mixed_heads, merge_weight)) + merge_bias
    second_norm = low(norm_rows(stream_mid, second_gain, second_shift))
    hidden = low(gelu_tanh(low_back(matmul(second_norm, expand_weight)) + expand_bias))
    output = stream_mid + low_back(matmul(hidden, shrink_weight)) + shrink_bias
    logits = low_back(matmul(low(output), router_weight)) + router_bias
    blended, entropy = expert_head(logits, correction, expert_frame)
    frame_loss = weight * (jnp.sum(blended * upstream_frame) + PENALTY * entropy)
    return (blended, frame_loss)

def reference(block_input, expert_out, upstream, lead_index, lead_frames, lead_embed, first_gain, first_shift, attend_weight, query_bias, value_bias, merge_weight, merge_bias, second_gain, second_shift, expand_weight, expand_bias, shrink_weight, shrink_bias, router_weight, router_bias, correction):
    params = (lead_embed, first_gain, first_shift, attend_weight.astype(jnp.float32), query_bias, value_bias, merge_weight.astype(jnp.float32), merge_bias, second_gain, second_shift, expand_weight.astype(jnp.float32), expand_bias, shrink_weight.astype(jnp.float32), shrink_bias, router_weight.astype(jnp.float32), router_bias, correction)
    lead_hot = (lead_index[:, None] == jnp.arange(LEADS, dtype=jnp.int32)[None, :]).astype(jnp.float32)
    counts = lax.optimization_barrier(jnp.sum(lead_hot, axis=0))
    table = lead_frames.astype(jnp.float32)
    chosen = lax.optimization_barrier(jnp.sum(lead_hot * table[None, :], axis=1))
    present = lax.optimization_barrier(jnp.sum(lead_hot * counts[None, :], axis=1))
    frame_weight = chosen * FRAMES / (present * jnp.sum(table))

    def total_loss(params, inputs):

        def frame_step(running, slices):
            frame_in, expert_frame, upstream_frame, lead_id, weight = slices
            blended, frame_loss = frame_forward(params, frame_in, expert_frame, upstream_frame, lead_id, weight)
            return (running + frame_loss, blended)
        running, blended = lax.scan(jax.checkpoint(frame_step), jnp.zeros((), jnp.float32), (inputs.reshape(FRAMES, FRAME, D), expert_out.reshape(FRAMES, FRAME, EXPERTS * CHANNELS), upstream.reshape(FRAMES, FRAME, CHANNELS), lead_index, frame_weight))
        return (running, blended.reshape(TOKENS, CHANNELS))
    loss_value, pullback, blended = jax.vjp(total_loss, params, block_input, has_aux=True)
    grads, grad_input = pullback(jnp.ones_like(loss_value))
    return (blended, grad_input, grads[0], grads[1], grads[2], grads[3], grads[4], grads[5], grads[6], grads[7], grads[8], grads[9], grads[10], grads[11], grads[12], grads[13], grads[14], grads[15], grads[16])
```

```python
import functools

import jax
import jax.numpy as jnp
from jax import lax
from jax.experimental import pallas as pl
from jax.experimental.pallas import tpu as pltpu
from jax.sharding import PartitionSpec as P

HEADS = 6
EPSILON = 1e-05
PENALTY = 1.0
GELU_COEF = 0.7978845608028654
GELU_CUBE = 0.044715
LOG2E = 1.4426950408889634
LANES = 128
STEP = 512
LIMIT = 56 * 2**20

low = jnp.bfloat16
full = jnp.float32


def mul(left, right, dims=((1,), (0,))):
    return lax.dot_general(left, right, (dims, ((), ())), preferred_element_type=full)


NT = ((1,), (1,))
TN = ((0,), (0,))


def params(count):
    return pltpu.CompilerParams(
        dimension_semantics=("arbitrary",) * count, vmem_limit_bytes=LIMIT
    )


def whole(shape):
    return pl.BlockSpec(shape, lambda *step: (0,) * len(shape))


SCALAR = pl.BlockSpec(memory_space=pltpu.SMEM)


def normalize(values):
    centre = jnp.mean(values, axis=-1, keepdims=True)
    centred = values - centre
    spread = jnp.mean(centred * centred, axis=-1, keepdims=True)
    scale = lax.rsqrt(spread + EPSILON)
    return centred * scale, scale


def norm_back(grad, unit, scale, gain):
    e = grad * gain
    first = jnp.mean(e, axis=-1, keepdims=True)
    second = jnp.mean(e * unit, axis=-1, keepdims=True)
    return scale * (e - first - unit * second)


def column_sum(values):
    return jnp.sum(values, axis=0, keepdims=True)


def project_kernel(lead, x, embed, gain, shift, weight, bias, first, projected):
    stream = x[...] + embed[pl.ds(lead[0], 1), :]
    unit, _ = normalize(stream)
    rounded = (unit * gain[...] + shift[...]).astype(low)
    first[...] = rounded
    projected[...] = (mul(rounded, weight[...]) + bias[...]).astype(low)


def project(lead, x, embed, gain, shift, weight, bias):
    rows, features = x.shape
    wide = weight.shape[1]
    return pl.pallas_call(
        project_kernel,
        grid=(rows // STEP,),
        in_specs=[
            SCALAR,
            pl.BlockSpec((STEP, features), lambda i: (i, 0)),
            whole(embed.shape),
            whole(gain.shape),
            whole(shift.shape),
            whole(weight.shape),
            whole(bias.shape),
        ],
        out_specs=[
            pl.BlockSpec((STEP, features), lambda i: (i, 0)),
            pl.BlockSpec((STEP, wide), lambda i: (i, 0)),
        ],
        out_shape=[
            jax.ShapeDtypeStruct((rows, features), low),
            jax.ShapeDtypeStruct((rows, wide), low),
        ],
        compiler_params=params(1),
        name="project",
    )(lead, x, embed, gain, shift, weight, bias)


def attend_kernel(size, q, k, v, probs, mixed, inverse, turned):
    keys = k.shape[0]
    count = q.shape[0]
    scaling = size ** (-0.5) * LOG2E

    @pl.when(pl.program_id(1) == 0)
    def _():
        across = v[...].T
        tail = lax.broadcasted_iota(jnp.int32, (16, keys), 0)
        ones = jnp.where(tail == 0, 1.0, 0.0).astype(low)
        for head in range(2):
            turned[head, 0:size, :] = across[head * size : (head + 1) * size, :]
            turned[head, size : size + 16, :] = ones

    lane = lax.broadcasted_iota(jnp.int32, (1, LANES), 1)

    def scores(head, start):
        mask = jnp.where(lane // size == head, 1.0, 0.0).astype(low)
        return mul(k[start : start + STEP, :], q[...] * mask, NT) * scaling

    def finish(head, total):
        spread = total[size : size + 1, :]
        inv = 1.0 / spread
        inverse[0, head : head + 1, :] = inv
        mixed[head * size : (head + 1) * size, :] = (total[0:size, :] * inv).astype(low)
        return spread

    extremes = []
    for head in range(2):
        total = jnp.zeros((size + 16, count), full)
        for start in range(0, keys, STEP):
            p = jnp.exp2(scores(head, start)).astype(low)
            probs[0, head, start : start + STEP, :] = p
            total = total + mul(turned[head, :, start : start + STEP], p)
        spread = finish(head, total)
        extremes.append(spread)

    both = jnp.concatenate(extremes, axis=0)
    inside = jnp.where((both > 1e-18) & (both < 1e18), 1.0, 0.0)

    @pl.when(jnp.min(inside) < 0.5)
    def _():
        for head in range(2):
            top = jnp.full((1, count), -jnp.inf, full)
            for start in range(0, keys, STEP):
                top = jnp.maximum(
                    top, jnp.max(scores(head, start), axis=0, keepdims=True)
                )
            total = jnp.zeros((size + 16, count), full)
            for start in range(0, keys, STEP):
                p = jnp.exp2(scores(head, start) - top).astype(low)
                probs[0, head, start : start + STEP, :] = p
                total = total + mul(turned[head, :, start : start + STEP], p)
            finish(head, total)


def attend(projected):
    rows, wide = projected.shape
    features = wide // 3
    pairs = features // LANES
    size = features // HEADS
    return pl.pallas_call(
        functools.partial(attend_kernel, size),
        grid=(pairs, rows // STEP),
        in_specs=[
            pl.BlockSpec((STEP, LANES), lambda p, i: (i, p)),
            pl.BlockSpec((rows, LANES), lambda p, i: (0, pairs + p)),
            pl.BlockSpec((rows, LANES), lambda p, i: (0, 2 * pairs + p)),
        ],
        out_specs=[
            pl.BlockSpec((1, 2, rows, STEP), lambda p, i: (p, 0, 0, i)),
            pl.BlockSpec((LANES, STEP), lambda p, i: (p, i)),
            pl.BlockSpec((1, 8, STEP), lambda p, i: (p, 0, i)),
        ],
        out_shape=[
            jax.ShapeDtypeStruct((pairs, 2, rows, rows), low),
            jax.ShapeDtypeStruct((features, rows), low),
            jax.ShapeDtypeStruct((pairs, 8, rows), full),
        ],
        scratch_shapes=[pltpu.VMEM((2, size + 16, rows), low)],
        compiler_params=params(2),
        name="attend",
    )(projected, projected, projected)


def middle_kernel(
    spans,
    lead,
    weight,
    x,
    mixed,
    experts,
    upstream,
    embed,
    merge_w,
    merge_b,
    gain,
    shift,
    expand_w,
    expand_b,
    shrink_w,
    shrink_b,
    router_w,
    router_b,
    correction,
    blended,
    d_mid,
    d_mixed,
    grads,
):
    features = x.shape[1]
    hidden_size = expand_w.shape[1]
    channels = correction.shape[1]
    chunk = features

    @pl.when(pl.program_id(0) == 0)
    def _():
        grads[...] = jnp.zeros_like(grads)

    def add(name, values, part=0):
        base = spans[name][0]
        height = values.shape[0]
        for block in range(values.shape[1] // LANES):
            start = base + (part + block) * height
            grads[start : start + height, :] += values[
                :, block * LANES : (block + 1) * LANES
            ]

    stream = x[...] + embed[pl.ds(lead[0], 1), :]
    mid = stream + mul(mixed[...], merge_w[...], TN) + merge_b[...]
    unit, scale = normalize(mid)
    second = (unit * gain[...] + shift[...]).astype(low)
    output = mid + shrink_b[...]
    hidden, slope = [], []
    for start in range(0, hidden_size, chunk):
        part = slice(start, start + chunk)
        u = mul(second, expand_w[:, part]) + expand_b[:, part]
        square = u * u
        t = jnp.tanh(GELU_COEF * u * (1.0 + GELU_CUBE * square))
        half = 0.5 + 0.5 * t
        act = (u * half).astype(low)
        hidden.append(act)
        slope.append(
            half
            + 0.5
            * GELU_COEF
            * u
            * (1.0 - t * t)
            * (1.0 + 3.0 * GELU_CUBE * square)
        )
        output = output + mul(act, shrink_w[part, :])
    output_low = output.astype(low)
    logits = mul(output_low, router_w[...]) + router_b[...]
    lane = lax.broadcasted_iota(jnp.int32, (1, LANES), 1)
    valid = lane < channels
    parts = [logits[:, e * LANES : (e + 1) * LANES] for e in range(3)]
    largest = jnp.maximum(jnp.maximum(parts[0], parts[1]), parts[2])
    parts = [part - largest for part in parts]
    raised = [jnp.exp(part) for part in parts]
    total = raised[0] + raised[1] + raised[2]
    shared = jnp.log(total)
    logs = [part - shared for part in parts]
    inverse = 1.0 / total
    gates = [value * inverse for value in raised]

    def widen(values):
        return jnp.concatenate(
            [values, jnp.zeros((values.shape[0], LANES - channels), full)], axis=1
        )

    frames = [
        widen(experts[:, e * channels : (e + 1) * channels]) for e in range(3)
    ]
    up = widen(upstream[...])
    mix = gates[0] * frames[0] + gates[1] * frames[1] + gates[2] * frames[2]
    entropy = -(gates[0] * logs[0] + gates[1] * logs[1] + gates[2] * logs[2])
    blended[...] = mix[:, :channels] + correction[...]
    frame_weight = weight[0]
    d_parts = [
        jnp.where(
            valid,
            frame_weight
            * gates[e]
            * (up * (frames[e] - mix) - PENALTY * (logs[e] + entropy)),
            0.0,
        )
        for e in range(3)
    ]
    add("correction", frame_weight * column_sum(up))
    d_logits = jnp.concatenate(d_parts, axis=1)
    add("router_bias", column_sum(d_logits))
    d_logits_low = d_logits.astype(low)
    add("router", mul(output_low, d_logits_low, TN))
    d_output = mul(d_logits_low, router_w[...], NT)
    add("shrink_bias", column_sum(d_output))
    d_output_low = d_output.astype(low)
    d_second = jnp.zeros_like(d_output)
    for index, start in enumerate(range(0, hidden_size, chunk)):
        part = slice(start, start + chunk)
        d_pre = mul(d_output_low, shrink_w[part, :], NT) * slope[index]
        add("expand_bias", column_sum(d_pre), start // LANES)
        d_pre_low = d_pre.astype(low)
        d_second = d_second + mul(d_pre_low, expand_w[:, part], NT)
        add("expand", mul(second, d_pre_low, TN), start // LANES)
        base = spans["shrink"][0]
        product = mul(hidden[index], d_output_low, TN)
        for block in range(features // LANES):
            at = base + block * hidden_size + start
            grads[at : at + chunk, :] += product[:, block * LANES : (block + 1) * LANES]
    add("second_gain", column_sum(d_second * unit))
    add("second_shift", column_sum(d_second))
    grad_mid = d_output + norm_back(d_second, unit, scale, gain[...])
    d_mid[...] = grad_mid
    add("merge_bias", column_sum(grad_mid))
    d_mid_low = grad_mid.astype(low)
    add("merge", mul(mixed[...], d_mid_low))
    d_mixed[...] = mul(merge_w[...], d_mid_low, NT).astype(low)


def middle(spans, height, lead, weight, x, mixed, experts, upstream, tables):
    rows, features = x.shape
    channels = upstream.shape[1]
    step = 256
    return pl.pallas_call(
        functools.partial(middle_kernel, spans),
        grid=(rows // step,),
        in_specs=[
            SCALAR,
            SCALAR,
            pl.BlockSpec((step, features), lambda i: (i, 0)),
            pl.BlockSpec((features, step), lambda i: (0, i)),
            pl.BlockSpec((step, experts.shape[1]), lambda i: (i, 0)),
            pl.BlockSpec((step, channels), lambda i: (i, 0)),
        ]
        + [whole(table.shape) for table in tables],
        out_specs=[
            pl.BlockSpec((step, channels), lambda i: (i, 0)),
            pl.BlockSpec((step, features), lambda i: (i, 0)),
            pl.BlockSpec((features, step), lambda i: (0, i)),
            whole((height, LANES)),
        ],
        out_shape=[
            jax.ShapeDtypeStruct((rows, channels), full),
            jax.ShapeDtypeStruct((rows, features), full),
            jax.ShapeDtypeStruct((features, rows), low),
            jax.ShapeDtypeStruct((height, LANES), full),
        ],
        compiler_params=params(1),
        name="middle",
    )(lead, weight, x, mixed, experts, upstream, *tables)


def attend_back_kernel(
    size,
    q,
    k,
    v,
    d_mixed,
    mixed,
    inverse,
    first,
    probs,
    d_part,
    grads,
    d_across,
    d_down,
    d_query,
):
    step = pl.program_id(0)
    last = pl.num_programs(0) - 1
    rows = q.shape[0]
    block = k.shape[0]
    scaling = size ** (-0.5)
    lane = lax.broadcasted_iota(jnp.int32, (1, LANES), 1)

    @pl.when(step == 0)
    def _():
        stack = []
        for head in range(2):
            span = slice(head * size, (head + 1) * size)
            inv = inverse[0, head : head + 1, :]
            scaled = (d_mixed[span, :].astype(full) * inv).astype(low)
            stack.append(scaled)
            centre = -column_sum(scaled.astype(full) * mixed[span, :].astype(full))
            high = centre.astype(low)
            rest = centre - high.astype(full)
            mid = rest.astype(low)
            last_bits = (rest - mid.astype(full)).astype(low)
            row = lax.broadcasted_iota(jnp.int32, (size, rows), 0)
            extra = jnp.where(
                row == 0,
                high.astype(full),
                jnp.where(
                    row == 1,
                    mid.astype(full),
                    jnp.where(row == 2, last_bits.astype(full), 0.0),
                ),
            ).astype(low)
            d_across[head, span, :] = scaled
            d_across[head, (1 - head) * size : (2 - head) * size, :] = extra
        d_down[...] = jnp.concatenate(stack, axis=0).T
        d_query[...] = jnp.zeros_like(d_query)

    k_across = k[...].T
    d_keys, d_values = [], []
    for head in range(2):
        base = (1 - head) * size
        data = jnp.where(lane // size == head, 1.0, 0.0).astype(low)
        ones = jnp.where((lane >= base) & (lane < base + 3), 1.0, 0.0).astype(low)
        values = v[...] * data + ones
        d_k = jnp.zeros((block, LANES), full)
        d_v = jnp.zeros((block, LANES), full)
        for start in range(0, rows, STEP):
            span = slice(start, start + STEP)
            p = probs[0, head, :, span]
            d_p = mul(values, d_across[head, :, span])
            d_s = (p.astype(full) * d_p).astype(low)
            d_query[head * size : (head + 1) * size, span] += mul(
                k_across[head * size : (head + 1) * size, :], d_s
            )
            d_v = d_v + mul(p, d_down[span, :])
            d_k = d_k + mul(d_s, q[span, :])
        d_keys.append(d_k)
        d_values.append(d_v)
    at = pl.ds(pl.multiple_of(step * block, block), block)
    d_part[1, at, :] = (jnp.where(lane < size, *d_keys) * scaling).astype(low)
    d_part[2, at, :] = jnp.where(lane < size, *d_values).astype(low)

    @pl.when(step == last)
    def _():
        d_part[0] = (d_query[...].T * scaling).astype(low)
        features = first.shape[1]
        for kind in range(3):
            grads[kind * features : (kind + 1) * features, :] = mul(
                first[...], d_part[kind], TN
            )


def attend_back(pair, projected, d_mixed, mixed, inverse, first, probs):
    rows, wide = projected.shape
    features = wide // 3
    pairs = features // LANES
    size = features // HEADS
    return pl.pallas_call(
        functools.partial(attend_back_kernel, size),
        grid=(rows // STEP,),
        in_specs=[
            pl.BlockSpec((rows, LANES), lambda i: (0, pair)),
            pl.BlockSpec((STEP, LANES), lambda i: (i, pairs + pair)),
            pl.BlockSpec((STEP, LANES), lambda i: (i, 2 * pairs + pair)),
            pl.BlockSpec((LANES, rows), lambda i: (pair, 0)),
            pl.BlockSpec((LANES, rows), lambda i: (pair, 0)),
            pl.BlockSpec((1, 8, rows), lambda i: (pair, 0, 0)),
            whole(first.shape),
            pl.BlockSpec((1, 2, STEP, rows), lambda i: (pair, 0, i, 0)),
        ],
        out_specs=[
            whole((3, rows, LANES)),
            whole((3 * features, LANES)),
        ],
        out_shape=[
            jax.ShapeDtypeStruct((3, rows, LANES), low),
            jax.ShapeDtypeStruct((3 * features, LANES), full),
        ],
        scratch_shapes=[
            pltpu.VMEM((2, LANES, rows), low),
            pltpu.VMEM((rows, LANES), low),
            pltpu.VMEM((LANES, rows), full),
        ],
        compiler_params=params(1),
        name="attend_back",
    )(projected, projected, projected, d_mixed, mixed, inverse, first, probs)


def finish_kernel(pairs, lead, x, embed, gain, weight, d_mid, *rest):
    d_parts = rest[:pairs]
    grad_input, sums = rest[pairs:]

    @pl.when(pl.program_id(0) == 0)
    def _():
        sums[...] = jnp.zeros_like(sums)

    stream = x[...] + embed[pl.ds(lead[0], 1), :]
    unit, scale = normalize(stream)
    d_first = jnp.zeros_like(stream)
    for pair in range(pairs):
        for kind in range(3):
            at = (kind * pairs + pair) * LANES
            d_first = d_first + mul(
                d_parts[pair][kind], weight[:, at : at + LANES], NT
            )
    d_stream = d_mid[...] + norm_back(d_first, unit, scale, gain[...])
    grad_input[...] = d_stream
    lanes = [column_sum(d_parts[pair][0].astype(full)) for pair in range(pairs)]
    values = [column_sum(d_parts[pair][2].astype(full)) for pair in range(pairs)]
    sums[0:1, :] += column_sum(d_first * unit)
    sums[1:2, :] += column_sum(d_first)
    sums[2:3, :] += jnp.concatenate(lanes, axis=1)
    sums[3:4, :] += jnp.concatenate(values, axis=1)
    sums[4:5, :] += column_sum(d_stream)


def finish(lead, x, embed, gain, weight, d_mid, d_parts):
    rows, features = x.shape
    pairs = len(d_parts)
    return pl.pallas_call(
        functools.partial(finish_kernel, pairs),
        grid=(rows // STEP,),
        in_specs=[
            SCALAR,
            pl.BlockSpec((STEP, features), lambda i: (i, 0)),
            whole(embed.shape),
            whole(gain.shape),
            whole(weight.shape),
            pl.BlockSpec((STEP, features), lambda i: (i, 0)),
        ]
        + [pl.BlockSpec((3, STEP, LANES), lambda i: (0, i, 0))] * pairs,
        out_specs=[
            pl.BlockSpec((STEP, features), lambda i: (i, 0)),
            whole((8, features)),
        ],
        out_shape=[
            jax.ShapeDtypeStruct((rows, features), full),
            jax.ShapeDtypeStruct((8, features), full),
        ],
        compiler_params=params(1),
        name="finish",
    )(lead, x, embed, gain, weight, d_mid, *d_parts)


def bits_of(sizes):
    order = []
    for axis in ("dp", "rep"):
        bit = 1
        while bit < sizes[axis]:
            order.append((axis, bit))
            bit *= 2
    return order


def swap(values, sizes, axis, bit):
    return lax.ppermute(values, axis, [(i, i ^ bit) for i in range(sizes[axis])])


def sum_small(values, sizes):
    for axis, bit in bits_of(sizes):
        values = values + swap(values, sizes, axis, bit)
    return values


def sum_all(values, sizes):
    taken = []
    for axis, bit in bits_of(sizes):
        half = values.shape[0] // 2
        side = (lax.axis_index(axis) // bit) % 2
        keep = lax.dynamic_slice_in_dim(values, side * half, half, 0)
        send = lax.dynamic_slice_in_dim(values, (1 - side) * half, half, 0)
        values = keep + swap(send, sizes, axis, bit)
        taken.append((axis, bit, side))
    for axis, bit, side in reversed(taken):
        other = swap(values, sizes, axis, bit)
        values = jnp.where(
            side == 0,
            jnp.concatenate([values, other]),
            jnp.concatenate([other, values]),
        )
    return values


def up_to(value, step):
    return -(-value // step) * step


def body(sizes, *args):
    (
        block_input,
        expert_out,
        upstream,
        lead_index,
        lead_frames,
        lead_embed,
        first_gain,
        first_shift,
        attend_weight,
        query_bias,
        value_bias,
        merge_weight,
        merge_bias,
        second_gain,
        second_shift,
        expand_weight,
        expand_bias,
        shrink_weight,
        shrink_bias,
        router_weight,
        router_bias,
        correction,
    ) = args
    rows, features = block_input.shape
    channels = correction.shape[0]
    leads = lead_embed.shape[0]
    hidden = expand_bias.shape[0]
    devices = sizes["dp"] * sizes["rep"]
    pairs = features // LANES
    grain = 8 * devices

    lead_hot = (lead_index[0] == jnp.arange(leads, dtype=jnp.int32)).astype(full)
    counts = sum_small(lead_hot, sizes)
    table = lead_frames.astype(full)
    weight = (
        jnp.sum(lead_hot * table)
        * devices
        / (jnp.sum(lead_hot * counts) * jnp.sum(table))
    ).reshape(1)

    def row(vector):
        return vector.reshape(1, -1)

    bias = row(jnp.concatenate([query_bias, jnp.zeros_like(query_bias), value_bias]))
    first, projected = project(
        lead_index,
        block_input,
        lead_embed,
        row(first_gain),
        row(first_shift),
        attend_weight,
        bias,
    )
    probs, mixed, inverse = attend(projected)

    widths = (
        ("expand", features * hidden),
        ("shrink", features * hidden),
        ("merge", features * features),
        ("router", features * 3 * LANES),
        ("expand_bias", hidden),
        ("shrink_bias", features),
        ("merge_bias", features),
        ("second_gain", features),
        ("second_shift", features),
        ("router_bias", 3 * LANES),
        ("correction", LANES),
    )
    spans, height = {}, 0
    for name, width in widths:
        spans[name] = (height, height + width // LANES)
        height += width // LANES
    height = up_to(height, grain)
    wide_router = jnp.pad(
        router_weight.reshape(features, 3, channels),
        ((0, 0), (0, 0), (0, LANES - channels)),
    ).reshape(features, 3 * LANES)
    wide_bias = jnp.pad(
        router_bias.reshape(3, channels), ((0, 0), (0, LANES - channels))
    ).reshape(1, 3 * LANES)
    tables = (
        lead_embed,
        merge_weight,
        row(merge_bias),
        row(second_gain),
        row(second_shift),
        expand_weight,
        row(expand_bias),
        shrink_weight,
        row(shrink_bias),
        wide_router,
        wide_bias,
        row(correction),
    )
    blended, d_mid, d_mixed, grads = middle(
        spans,
        height,
        lead_index,
        weight,
        block_input,
        mixed,
        expert_out,
        upstream,
        tables,
    )
    d_parts, d_weights = [], []
    for pair in range(pairs):
        d_part, d_weight = attend_back(
            pair, projected, d_mixed, mixed, inverse, first, probs
        )
        d_parts.append(d_part)
        d_weights.append(d_weight)
    grad_input, sums = finish(
        lead_index,
        block_input,
        lead_embed,
        row(first_gain),
        attend_weight,
        d_mid,
        d_parts,
    )
    grads = sum_all(grads, sizes)
    embed_rows = lead_hot[:, None] * sums[4][None, :]
    tail = jnp.concatenate(
        d_weights + [sums[:4].reshape(-1, LANES), embed_rows.reshape(-1, LANES)]
    )
    tail_rows = tail.shape[0]
    tail = jnp.pad(tail, ((0, up_to(tail_rows, grain) - tail_rows), (0, 0)))
    tail = sum_all(tail, sizes)

    def matrix(values, height):
        return values.reshape(-1, height, LANES).transpose(1, 0, 2).reshape(height, -1)

    def take(name):
        start, stop = spans[name]
        return grads[start:stop]

    def clip(values):
        return values.reshape(-1, 3, LANES)[:, :, :channels].reshape(-1, 3 * channels)

    size = pairs * 3 * features
    attend_grad = (
        tail[:size]
        .reshape(pairs, 3, features, LANES)
        .transpose(2, 1, 0, 3)
        .reshape(features, 3 * features)
    )
    vectors = tail[size : size + 4 * pairs].reshape(4, features)
    embed_grad = tail[size + 4 * pairs : tail_rows].reshape(leads, features)
    return (
        blended,
        grad_input,
        embed_grad,
        vectors[0],
        vectors[1],
        attend_grad,
        vectors[2],
        vectors[3],
        matrix(take("merge"), features),
        take("merge_bias").reshape(-1),
        take("second_gain").reshape(-1),
        take("second_shift").reshape(-1),
        matrix(take("expand"), features),
        take("expand_bias").reshape(-1),
        matrix(take("shrink"), hidden),
        take("shrink_bias").reshape(-1),
        clip(matrix(take("router"), features)),
        clip(take("router_bias").reshape(1, -1)).reshape(-1),
        take("correction").reshape(-1)[:channels],
    )


def solution(mesh):
    split = P(("dp", "rep"), None)
    sizes = dict(mesh.shape)
    return jax.shard_map(
        functools.partial(body, sizes),
        mesh=mesh,
        in_specs=(split, split, split, P(("dp", "rep"))) + (P(),) * 18,
        out_specs=(split, split) + (P(),) * 17,
        check_vma=False,
    )
```

```python
import functools

import jax
import jax.numpy as jnp
from jax import lax
from jax.experimental import pallas as pl
from jax.experimental.pallas import tpu as pltpu
from jax.sharding import PartitionSpec as P

HEADS = 6
EPSILON = 1e-05
PENALTY = 1.0
GELU_COEF = 0.7978845608028654
GELU_CUBE = 0.044715
LOG2E = 1.4426950408889634
LANES = 128
STEP = 512
LIMIT = 56 * 2**20

low = jnp.bfloat16
full = jnp.float32


def mul(left, right, dims=((1,), (0,))):
    return lax.dot_general(left, right, (dims, ((), ())), preferred_element_type=full)


NT = ((1,), (1,))
TN = ((0,), (0,))


def params(count):
    return pltpu.CompilerParams(
        dimension_semantics=("arbitrary",) * count, vmem_limit_bytes=LIMIT
    )


def whole(shape):
    return pl.BlockSpec(shape, lambda *step: (0,) * len(shape))


SCALAR = pl.BlockSpec(memory_space=pltpu.SMEM)


def normalize(values):
    centre = jnp.mean(values, axis=-1, keepdims=True)
    centred = values - centre
    spread = jnp.mean(centred * centred, axis=-1, keepdims=True)
    scale = lax.rsqrt(spread + EPSILON)
    return centred * scale, scale


def norm_back(grad, unit, scale, gain):
    e = grad * gain
    first = jnp.mean(e, axis=-1, keepdims=True)
    second = jnp.mean(e * unit, axis=-1, keepdims=True)
    return scale * (e - first - unit * second)


def column_sum(values):
    return jnp.sum(values, axis=0, keepdims=True)


def project_kernel(lead, x, embed, gain, shift, weight, bias, first, projected):
    stream = x[...] + embed[pl.ds(lead[0], 1), :]
    unit, _ = normalize(stream)
    rounded = (unit * gain[...] + shift[...]).astype(low)
    first[...] = rounded
    projected[...] = (mul(rounded, weight[...]) + bias[...]).astype(low)


def project(lead, x, embed, gain, shift, weight, bias):
    rows, features = x.shape
    wide = weight.shape[1]
    return pl.pallas_call(
        project_kernel,
        grid=(rows // STEP,),
        in_specs=[
            SCALAR,
            pl.BlockSpec((STEP, features), lambda i: (i, 0)),
            whole(embed.shape),
            whole(gain.shape),
            whole(shift.shape),
            whole(weight.shape),
            whole(bias.shape),
        ],
        out_specs=[
            pl.BlockSpec((STEP, features), lambda i: (i, 0)),
            pl.BlockSpec((STEP, wide), lambda i: (i, 0)),
        ],
        out_shape=[
            jax.ShapeDtypeStruct((rows, features), low),
            jax.ShapeDtypeStruct((rows, wide), low),
        ],
        compiler_params=params(1),
        name="project",
    )(lead, x, embed, gain, shift, weight, bias)


def attend_kernel(size, q, k, v, probs, mixed, inverse, turned):
    keys = k.shape[0]
    count = q.shape[0]
    scaling = size ** (-0.5) * LOG2E

    @pl.when(pl.program_id(1) == 0)
    def _():
        across = v[...].T
        tail = lax.broadcasted_iota(jnp.int32, (16, keys), 0)
        ones = jnp.where(tail == 0, 1.0, 0.0).astype(low)
        for head in range(2):
            turned[head, 0:size, :] = across[head * size : (head + 1) * size, :]
            turned[head, size : size + 16, :] = ones

    lane = lax.broadcasted_iota(jnp.int32, (1, LANES), 1)

    def scores(head, start):
        mask = jnp.where(lane // size == head, 1.0, 0.0).astype(low)
        return mul(k[start : start + STEP, :], q[...] * mask, NT) * scaling

    def finish(head, total):
        spread = total[size : size + 1, :]
        inv = 1.0 / spread
        inverse[0, head : head + 1, :] = inv
        mixed[head * size : (head + 1) * size, :] = (total[0:size, :] * inv).astype(low)
        return spread

    extremes = []
    for head in range(2):
        total = jnp.zeros((size + 16, count), full)
        for start in range(0, keys, STEP):
            p = jnp.exp2(scores(head, start)).astype(low)
            probs[0, head, start : start + STEP, :] = p
            total = total + mul(turned[head, :, start : start + STEP], p)
        spread = finish(head, total)
        extremes.append(spread)

    both = jnp.concatenate(extremes, axis=0)
    inside = jnp.where((both > 1e-18) & (both < 1e18), 1.0, 0.0)

    @pl.when(jnp.min(inside) < 0.5)
    def _():
        for head in range(2):
            top = jnp.full((1, count), -jnp.inf, full)
            for start in range(0, keys, STEP):
                top = jnp.maximum(
                    top, jnp.max(scores(head, start), axis=0, keepdims=True)
                )
            total = jnp.zeros((size + 16, count), full)
            for start in range(0, keys, STEP):
                p = jnp.exp2(scores(head, start) - top).astype(low)
                probs[0, head, start : start + STEP, :] = p
                total = total + mul(turned[head, :, start : start + STEP], p)
            finish(head, total)


def attend(projected):
    rows, wide = projected.shape
    features = wide // 3
    pairs = features // LANES
    size = features // HEADS
    return pl.pallas_call(
        functools.partial(attend_kernel, size),
        grid=(pairs, rows // STEP),
        in_specs=[
            pl.BlockSpec((STEP, LANES), lambda p, i: (i, p)),
            pl.BlockSpec((rows, LANES), lambda p, i: (0, pairs + p)),
            pl.BlockSpec((rows, LANES), lambda p, i: (0, 2 * pairs + p)),
        ],
        out_specs=[
            pl.BlockSpec((1, 2, rows, STEP), lambda p, i: (p, 0, 0, i)),
            pl.BlockSpec((LANES, STEP), lambda p, i: (p, i)),
            pl.BlockSpec((1, 8, STEP), lambda p, i: (p, 0, i)),
        ],
        out_shape=[
            jax.ShapeDtypeStruct((pairs, 2, rows, rows), low),
            jax.ShapeDtypeStruct((features, rows), low),
            jax.ShapeDtypeStruct((pairs, 8, rows), full),
        ],
        scratch_shapes=[pltpu.VMEM((2, size + 16, rows), low)],
        compiler_params=params(2),
        name="attend",
    )(projected, projected, projected)


def middle_kernel(
    spans,
    size,
    lead,
    x,
    mixed,
    inverse,
    experts,
    upstream,
    embed,
    merge_w,
    merge_b,
    gain,
    shift,
    expand_w,
    expand_b,
    shrink_w,
    shrink_b,
    router_w,
    router_b,
    correction,
    blended,
    d_mid,
    d_across,
    d_down,
    grads,
):
    features = x.shape[1]
    step = x.shape[0]
    hidden_size = expand_w.shape[1]
    channels = correction.shape[1]
    chunk = features

    @pl.when(pl.program_id(0) == 0)
    def _():
        grads[...] = jnp.zeros_like(grads)

    def add(name, values, part=0):
        base = spans[name][0]
        height = values.shape[0]
        for block in range(values.shape[1] // LANES):
            start = base + (part + block) * height
            grads[start : start + height, :] += values[
                :, block * LANES : (block + 1) * LANES
            ]

    stream = x[...] + embed[pl.ds(lead[0], 1), :]
    mid = stream + mul(mixed[...], merge_w[...], TN) + merge_b[...]
    unit, scale = normalize(mid)
    second = (unit * gain[...] + shift[...]).astype(low)
    output = mid + shrink_b[...]
    hidden, slope = [], []
    for start in range(0, hidden_size, chunk):
        part = slice(start, start + chunk)
        u = mul(second, expand_w[:, part]) + expand_b[:, part]
        square = u * u
        t = jnp.tanh(GELU_COEF * u * (1.0 + GELU_CUBE * square))
        half = 0.5 + 0.5 * t
        act = (u * half).astype(low)
        hidden.append(act)
        slope.append(
            half
            + 0.5
            * GELU_COEF
            * u
            * (1.0 - t * t)
            * (1.0 + 3.0 * GELU_CUBE * square)
        )
        output = output + mul(act, shrink_w[part, :])
    output_low = output.astype(low)
    logits = mul(output_low, router_w[...]) + router_b[...]
    lane = lax.broadcasted_iota(jnp.int32, (1, LANES), 1)
    valid = lane < channels
    parts = [logits[:, e * LANES : (e + 1) * LANES] for e in range(3)]
    largest = jnp.maximum(jnp.maximum(parts[0], parts[1]), parts[2])
    parts = [part - largest for part in parts]
    raised = [jnp.exp(part) for part in parts]
    total = raised[0] + raised[1] + raised[2]
    shared = jnp.log(total)
    logs = [part - shared for part in parts]
    share = 1.0 / total
    gates = [value * share for value in raised]

    def widen(values):
        return jnp.concatenate(
            [values, jnp.zeros((values.shape[0], LANES - channels), full)], axis=1
        )

    frames = [
        widen(experts[:, e * channels : (e + 1) * channels]) for e in range(3)
    ]
    up = widen(upstream[...])
    mix = gates[0] * frames[0] + gates[1] * frames[1] + gates[2] * frames[2]
    entropy = -(gates[0] * logs[0] + gates[1] * logs[1] + gates[2] * logs[2])
    blended[...] = mix[:, :channels] + correction[...]
    d_parts = [
        jnp.where(
            valid,
            gates[e]
            * (up * (frames[e] - mix) - PENALTY * (logs[e] + entropy)),
            0.0,
        )
        for e in range(3)
    ]
    add("correction", column_sum(up))
    d_logits = jnp.concatenate(d_parts, axis=1)
    add("router_bias", column_sum(d_logits))
    d_logits_low = d_logits.astype(low)
    add("router", mul(output_low, d_logits_low, TN))
    d_output = mul(d_logits_low, router_w[...], NT)
    add("shrink_bias", column_sum(d_output))
    d_output_low = d_output.astype(low)
    d_second = jnp.zeros_like(d_output)
    for index, start in enumerate(range(0, hidden_size, chunk)):
        part = slice(start, start + chunk)
        d_pre = mul(d_output_low, shrink_w[part, :], NT) * slope[index]
        add("expand_bias", column_sum(d_pre), start // LANES)
        d_pre_low = d_pre.astype(low)
        d_second = d_second + mul(d_pre_low, expand_w[:, part], NT)
        add("expand", mul(second, d_pre_low, TN), start // LANES)
        base = spans["shrink"][0]
        product = mul(hidden[index], d_output_low, TN)
        for block in range(features // LANES):
            at = base + block * hidden_size + start
            grads[at : at + chunk, :] += product[:, block * LANES : (block + 1) * LANES]
    add("second_gain", column_sum(d_second * unit))
    add("second_shift", column_sum(d_second))
    grad_mid = d_output + norm_back(d_second, unit, scale, gain[...])
    d_mid[...] = grad_mid
    add("merge_bias", column_sum(grad_mid))
    d_mid_low = grad_mid.astype(low)
    add("merge", mul(mixed[...], d_mid_low))
    d_mixed = mul(merge_w[...], d_mid_low, NT).astype(low).astype(full)
    row = lax.broadcasted_iota(jnp.int32, (size, step), 0)
    stack = []
    for head in range(features // size):
        span = slice(head * size, (head + 1) * size)
        side = head % 2
        inv = inverse[head // 2, side : side + 1, :]
        scaled = (d_mixed[span, :] * inv).astype(low)
        stack.append(scaled)
        centre = -column_sum(scaled.astype(full) * mixed[span, :].astype(full))
        one = centre.astype(low).astype(full)
        two = (centre - one).astype(low).astype(full)
        extra = jnp.where(
            row == 0,
            one,
            jnp.where(row == 1, two, jnp.where(row == 2, centre - one - two, 0.0)),
        ).astype(low)
        d_across[head, side * size : (side + 1) * size, :] = scaled
        d_across[head, (1 - side) * size : (2 - side) * size, :] = extra
    d_down[...] = jnp.concatenate(stack, axis=0).T


def middle(spans, height, lead, x, mixed, inverse, experts, upstream, tables):
    rows, features = x.shape
    size = features // HEADS
    channels = upstream.shape[1]
    step = 256
    return pl.pallas_call(
        functools.partial(middle_kernel, spans, size),
        grid=(rows // step,),
        in_specs=[
            SCALAR,
            pl.BlockSpec((step, features), lambda i: (i, 0)),
            pl.BlockSpec((features, step), lambda i: (0, i)),
            pl.BlockSpec((inverse.shape[0], 8, step), lambda i: (0, 0, i)),
            pl.BlockSpec((step, experts.shape[1]), lambda i: (i, 0)),
            pl.BlockSpec((step, channels), lambda i: (i, 0)),
        ]
        + [whole(table.shape) for table in tables],
        out_specs=[
            pl.BlockSpec((step, channels), lambda i: (i, 0)),
            pl.BlockSpec((step, features), lambda i: (i, 0)),
            pl.BlockSpec((HEADS, LANES, step), lambda i: (0, 0, i)),
            pl.BlockSpec((step, features), lambda i: (i, 0)),
            whole((height, LANES)),
        ],
        out_shape=[
            jax.ShapeDtypeStruct((rows, channels), full),
            jax.ShapeDtypeStruct((rows, features), full),
            jax.ShapeDtypeStruct((HEADS, LANES, rows), low),
            jax.ShapeDtypeStruct((rows, features), low),
            jax.ShapeDtypeStruct((height, LANES), full),
        ],
        compiler_params=params(1),
        name="middle",
    )(lead, x, mixed, inverse, experts, upstream, *tables)


def attend_back_kernel(size, first_part, last_part, *refs):
    if first_part:
        q, k, v, d_across, d_down, probs, d_query, d_pair = refs[:8]
    else:
        q, k, v, d_across, d_down, probs, carry, _, d_query, d_pair = refs[:10]
    total = refs[-1] if last_part else d_query
    step = pl.program_id(0)
    rows = q.shape[0]
    block = k.shape[0]
    scaling = size ** (-0.5)
    lane = lax.broadcasted_iota(jnp.int32, (1, LANES), 1)

    @pl.when(step == 0)
    def _():
        total[...] = jnp.zeros_like(total) if first_part else carry[...]

    k_across = k[...].T
    d_keys, d_values = [], []
    for head in range(2):
        base = (1 - head) * size
        data = jnp.where(lane // size == head, 1.0, 0.0).astype(low)
        ones = jnp.where((lane >= base) & (lane < base + 3), 1.0, 0.0).astype(low)
        values = v[...] * data + ones
        d_k = jnp.zeros((block, LANES), full)
        d_v = jnp.zeros((block, LANES), full)
        for start in range(0, rows, STEP):
            span = slice(start, start + STEP)
            p = probs[0, head, :, span]
            d_p = mul(values, d_across[head, :, span])
            d_s = (p.astype(full) * d_p).astype(low)
            total[head * size : (head + 1) * size, span] += mul(
                k_across[head * size : (head + 1) * size, :], d_s
            )
            d_v = d_v + mul(p, d_down[span, :])
            d_k = d_k + mul(d_s, q[span, :])
        d_keys.append(d_k)
        d_values.append(d_v)
    d_pair[0] = (jnp.where(lane < size, *d_keys) * scaling).astype(low)
    d_pair[1] = jnp.where(lane < size, *d_values).astype(low)

    if last_part:

        @pl.when(step == pl.num_programs(0) - 1)
        def _():
            d_query[...] = (total[...].T * scaling).astype(low)


def attend_back(pair, part, parts, projected, d_across, d_down, probs, carried):
    rows, wide = projected.shape
    features = wide // 3
    pairs = features // LANES
    size = features // HEADS
    steps = rows // STEP // parts
    base = part * steps
    first_part, last_part = part == 0, part == parts - 1
    across = (rows, LANES) if last_part else (LANES, rows)
    return pl.pallas_call(
        functools.partial(attend_back_kernel, size, first_part, last_part),
        grid=(steps,),
        in_specs=[
            pl.BlockSpec((rows, LANES), lambda i: (0, pair)),
            pl.BlockSpec((STEP, LANES), lambda i: (base + i, pairs + pair)),
            pl.BlockSpec((STEP, LANES), lambda i: (base + i, 2 * pairs + pair)),
            pl.BlockSpec((2, LANES, rows), lambda i: (pair, 0, 0)),
            pl.BlockSpec((rows, LANES), lambda i: (0, pair)),
            pl.BlockSpec((1, 2, STEP, rows), lambda i: (pair, 0, base + i, 0)),
        ]
        + ([] if first_part else [whole((LANES, rows)), pl.BlockSpec(memory_space=pl.ANY)]),
        out_specs=[
            whole(across),
            pl.BlockSpec((2, STEP, LANES), lambda i: (0, base + i, 0)),
        ],
        out_shape=[
            jax.ShapeDtypeStruct(across, low if last_part else full),
            jax.ShapeDtypeStruct((2, rows, LANES), low),
        ],
        scratch_shapes=[pltpu.VMEM((LANES, rows), full)] if last_part else [],
        input_output_aliases={} if first_part else {7: 1},
        compiler_params=params(1),
        cost_estimate=pl.CostEstimate(
            flops=10 * rows * rows * 256 // parts, bytes_accessed=rows * rows * 4 // parts, transcendentals=0
        ),
        name="attend_back",
    )(projected, projected, projected, d_across, d_down, probs, *carried)


def weigh_kernel(pairs, weight, first, *refs):
    d_query, d_pair = refs[:pairs], refs[pairs : 2 * pairs]
    grads, sums = refs[2 * pairs :]
    features = first.shape[1]
    grads[...] = jnp.zeros_like(grads)
    sums[...] = jnp.zeros_like(sums)
    for pair in range(pairs):
        lanes = slice(pair * LANES, (pair + 1) * LANES)
        for kind in range(3):
            values = d_query[pair][...] if kind == 0 else d_pair[pair][kind - 1]
            base = (kind * pairs + pair) * features
            grads[base : base + features, :] = mul(first[...], values, TN) * weight[0]
            if kind != 1:
                sums[kind // 2 : kind // 2 + 1, lanes] = weight[0] * column_sum(
                    values.astype(full)
                )


def weigh(height, weight, first, d_query, d_pair):
    features = first.shape[1]
    vmem = pl.BlockSpec(memory_space=pltpu.VMEM)
    pairs = len(d_query)
    return pl.pallas_call(
        functools.partial(weigh_kernel, pairs),
        in_specs=[SCALAR, vmem] + [vmem] * (2 * pairs),
        out_specs=[vmem] * 2,
        out_shape=[
            jax.ShapeDtypeStruct((height, LANES), full),
            jax.ShapeDtypeStruct((8, features), full),
        ],
        compiler_params=pltpu.CompilerParams(vmem_limit_bytes=LIMIT),
        name="weigh",
    )(weight, first, *d_query, *d_pair)


def finish_kernel(pairs, last_part, lead, weight, x, embed, gain, wide, d_mid, *rest):
    d_query, d_pair, rest = rest[:pairs], rest[pairs : 2 * pairs], rest[2 * pairs :]
    if last_part:
        earlier, biases, _, grad_input, vectors, sums = rest
    else:
        grad_input, sums = rest
    step = pl.program_id(0)

    @pl.when(step == 0)
    def _():
        sums[...] = earlier[...] if last_part else jnp.zeros_like(sums)

    stream = x[...] + embed[pl.ds(lead[0], 1), :]
    unit, scale = normalize(stream)
    d_first = jnp.zeros_like(stream)
    for pair in range(pairs):
        for kind in range(3):
            at = (kind * pairs + pair) * LANES
            values = d_query[pair][...] if kind == 0 else d_pair[pair][kind - 1]
            d_first = d_first + mul(values, wide[:, at : at + LANES], NT)
    d_stream = (d_mid[...] + norm_back(d_first, unit, scale, gain[...])) * weight[0]
    grad_input[...] = d_stream
    sums[0:1, :] += column_sum(d_first * unit) * weight[0]
    sums[1:2, :] += column_sum(d_first) * weight[0]
    sums[2:3, :] += column_sum(d_stream)

    if last_part:

        @pl.when(step == pl.num_programs(0) - 1)
        def _():
            vectors[...] = jnp.zeros_like(vectors)
            for block in range(pairs):
                lanes = slice(block * LANES, (block + 1) * LANES)
                for index, ref in enumerate((sums, sums, biases, biases)):
                    at = index * pairs + block
                    vectors[at : at + 1, :] = ref[index % 2 : index % 2 + 1, lanes]
                vectors[pl.ds((4 + lead[0]) * pairs + block, 1), :] = sums[2:3, lanes]


def finish(part, parts, lead, weight, x, embed, gain, wide, d_mid, d_query, d_pair, carried):
    rows, features = x.shape
    pairs = len(d_query)
    steps = rows // STEP // parts
    base = part * steps
    last_part = part == parts - 1
    height = up_to((4 + embed.shape[0]) * pairs, 8)
    row_spec = pl.BlockSpec((STEP, features), lambda i: (base + i, 0))
    small = pl.BlockSpec((8, features), lambda i: (0, 0))
    return pl.pallas_call(
        functools.partial(finish_kernel, pairs, last_part),
        grid=(steps,),
        in_specs=[
            SCALAR,
            SCALAR,
            row_spec,
            whole(embed.shape),
            whole(gain.shape),
            whole(wide.shape),
            row_spec,
        ]
        + [pl.BlockSpec((STEP, LANES), lambda i: (base + i, 0))] * pairs
        + [pl.BlockSpec((2, STEP, LANES), lambda i: (0, base + i, 0))] * pairs
        + ([small, small, pl.BlockSpec(memory_space=pl.ANY)] if last_part else []),
        out_specs=[row_spec, whole((height, LANES)) if last_part else small],
        out_shape=[
            jax.ShapeDtypeStruct((rows, features), full),
            jax.ShapeDtypeStruct((height, LANES) if last_part else (8, features), full),
        ],
        scratch_shapes=[pltpu.VMEM((8, features), full)] if last_part else [],
        input_output_aliases={9 + 2 * pairs: 0} if last_part else {},
        compiler_params=params(1),
        cost_estimate=pl.CostEstimate(
            flops=2 * rows * features * features * 3 // parts, bytes_accessed=rows * features * 18 // parts, transcendentals=0
        ),
        name="finish",
    )(lead, weight, x, embed, gain, wide, d_mid, *d_query, *d_pair, *carried)


def up_to(value, step):
    return -(-value // step) * step


def tie(value, *others):
    return lax.optimization_barrier((value,) + others)[0]


def routes(sizes):
    inner = sizes["rep"]
    outer = sizes["dp"]
    if outer % 2:
        return 0, ((), ())
    far = [inner << n for n in range(1, outer.bit_length() - 1)]
    near = [1 << n for n in range(inner.bit_length() - 1)]
    even, odd = [], []
    for n in range(max(len(far), len(near))):
        even += far[n : n + 1] + near[n : n + 1]
    odd = even[1:-1] + even[:1] + even[-1:]
    if len(even) > 2 and len(even) % 2 == 0:
        odd = even[1:3] + even[:1] + even[3:]
    return inner, (tuple(even), tuple(odd))


class Ring:
    def __init__(self, sizes):
        self.count = sizes["dp"] * sizes["rep"]
        self.core_bit, self.orders = routes(sizes)
        self.hops = len(self.orders[0]) + 1 if self.core_bit else 0
        self.index = lax.axis_index(("dp", "rep"))

    def bits(self, hop):
        if hop == 0:
            return self.core_bit, self.core_bit
        return self.orders[0][hop - 1], self.orders[1][hop - 1]

    def swap(self, values, hop):
        pair = self.bits(hop)
        moves = [
            (i, i ^ pair[(i // self.core_bit) % 2]) for i in range(self.count)
        ]
        return lax.ppermute(values, ("dp", "rep"), moves)

    def side(self, hop):
        even, odd = self.bits(hop)
        bit = even
        if even != odd:
            bit = jnp.where(self.index & self.core_bit == 0, even, odd)
        return jnp.where(self.index & bit == 0, 0, 1)

    def scatter(self, values, factor=None):
        for hop in range(self.hops):
            half = values.shape[0] // 2
            side = self.side(hop)
            send = lax.dynamic_slice_in_dim(values, (1 - side) * half, half, 0)
            keep = lax.dynamic_slice_in_dim(values, side * half, half, 0)
            if factor is not None:
                send, keep, factor = send * factor, keep * factor, None
            got = self.swap(send, hop)
            beside = yield send
            values = keep + (got if beside is None else tie(got, beside))
        return values

    def gather(self, values, extra=None):
        for hop in reversed(range(self.hops)):
            height = values.shape[0]
            send = values if extra is None else jnp.concatenate([values, extra])
            got = self.swap(send, hop)
            beside = yield send
            if beside is not None:
                got = tie(got, beside)
            if extra is not None:
                extra = extra + got[height:]
                got = got[:height]
            side = self.side(hop)
            values = jnp.where(
                side == 0,
                jnp.concatenate([values, got]),
                jnp.concatenate([got, values]),
            )
        return values if extra is None else (values, extra)


class Flow:
    def __init__(self, steps):
        self.steps = steps
        self.done = False
        self.sent = None
        self.result = None
        self.push(None)

    def push(self, beside):
        if self.done:
            return
        try:
            self.sent = self.steps.send(beside)
        except StopIteration as stop:
            self.done, self.sent, self.result = True, None, stop.value

    def drain(self):
        while not self.done:
            self.push(None)
        return self.result


def total_of(ring, values, factor):
    part = yield from ring.scatter(values, factor)
    return (yield from ring.gather(part))


def body(sizes, *args):
    (
        block_input,
        expert_out,
        upstream,
        lead_index,
        lead_frames,
        lead_embed,
        first_gain,
        first_shift,
        attend_weight,
        query_bias,
        value_bias,
        merge_weight,
        merge_bias,
        second_gain,
        second_shift,
        expand_weight,
        expand_bias,
        shrink_weight,
        shrink_bias,
        router_weight,
        router_bias,
        correction,
    ) = args
    rows, features = block_input.shape
    channels = correction.shape[0]
    leads = lead_embed.shape[0]
    hidden = expand_bias.shape[0]
    devices = sizes["dp"] * sizes["rep"]
    pairs = features // LANES
    grain = 8 * devices
    ring = Ring(sizes)

    tall = max(8, 2048 // devices)
    mine = lead_index[0].astype(full)
    leads_seen = lax.optimization_barrier(
        lax.all_gather(
            lax.optimization_barrier(jnp.full((tall, LANES), mine)), ("dp", "rep")
        )
    )
    count = jnp.sum((leads_seen[:, 0, 0] == mine).astype(full))
    table = lead_frames.astype(full)
    chosen = jnp.sum(jnp.where(jnp.arange(leads) == lead_index[0], table, 0.0))
    weight = (chosen * devices / (count * jnp.sum(table))).reshape(1)

    def row(vector):
        return vector.reshape(1, -1)

    bias = row(jnp.concatenate([query_bias, jnp.zeros_like(query_bias), value_bias]))
    first, projected = project(
        lead_index,
        block_input,
        lead_embed,
        row(first_gain),
        row(first_shift),
        attend_weight,
        bias,
    )
    probs, mixed, inverse = attend(projected)

    widths = (
        ("expand", features * hidden),
        ("shrink", features * hidden),
        ("merge", features * features),
        ("router", features * 3 * LANES),
        ("expand_bias", hidden),
        ("shrink_bias", features),
        ("merge_bias", features),
        ("second_gain", features),
        ("second_shift", features),
        ("router_bias", 3 * LANES),
        ("correction", LANES),
    )
    spans, height = {}, 0
    for name, width in widths:
        spans[name] = (height, height + width // LANES)
        height += width // LANES
    height = up_to(height, grain)
    wide_router = jnp.pad(
        router_weight.reshape(features, 3, channels),
        ((0, 0), (0, 0), (0, LANES - channels)),
    ).reshape(features, 3 * LANES)
    wide_bias = jnp.pad(
        router_bias.reshape(3, channels), ((0, 0), (0, LANES - channels))
    ).reshape(1, 3 * LANES)
    tables = (
        lead_embed,
        merge_weight,
        row(merge_bias),
        row(second_gain),
        row(second_shift),
        expand_weight,
        row(expand_bias),
        shrink_weight,
        row(shrink_bias),
        wide_router,
        wide_bias,
        row(correction),
    )
    blended, d_mid, d_across, d_down, grads = middle(
        spans,
        height,
        lead_index,
        block_input,
        mixed,
        inverse,
        expert_out,
        upstream,
        tables,
    )
    flow = Flow(total_of(ring, grads, weight[0]))
    parts = 2
    d_query, d_pair = [], []
    for pair in range(pairs):
        carried = ()
        for part in range(parts):
            now = d_down if flow.sent is None else tie(d_down, flow.sent)
            carried = attend_back(
                pair, part, parts, projected, d_across, now, probs, carried
            )
            flow.push(carried[0])
        d_query.append(carried[0])
        d_pair.append(carried[1])
    now = weight if flow.sent is None else tie(weight, flow.sent)
    size = 3 * pairs * features
    tail, biases = weigh(up_to(size, grain), now, first, d_query, d_pair)
    flow.push(tail)
    late = Flow(ring.scatter(tail))
    carried = ()
    parts = 2
    for part in range(parts):
        sent = [f.sent for f in (flow, late) if f.sent is not None]
        now = tie(weight, *sent)
        grad_input, sums = finish(
            part,
            parts,
            lead_index,
            now,
            block_input,
            lead_embed,
            row(first_gain),
            attend_weight,
            d_mid,
            d_query,
            d_pair,
            carried,
        )
        carried = (sums, biases, grad_input)
        flow.push(sums)
        late.push(sums)
    grads = flow.drain()
    piece = late.drain()
    tail, vectors = Flow(ring.gather(piece, sums)).drain()

    def matrix(values, height):
        return values.reshape(-1, height, LANES).transpose(1, 0, 2).reshape(height, -1)

    def take(name):
        start, stop = spans[name]
        return grads[start:stop]

    def clip(values):
        return values.reshape(-1, 3, LANES)[:, :, :channels].reshape(-1, 3 * channels)

    small = vectors[: 4 * pairs].reshape(4, features)
    embed_grad = vectors[4 * pairs : (4 + leads) * pairs].reshape(leads, features)
    return (
        blended,
        grad_input,
        embed_grad,
        small[0],
        small[1],
        matrix(tail[:size], features),
        small[2],
        small[3],
        matrix(take("merge"), features),
        take("merge_bias").reshape(-1),
        take("second_gain").reshape(-1),
        take("second_shift").reshape(-1),
        matrix(take("expand"), features),
        take("expand_bias").reshape(-1),
        matrix(take("shrink"), hidden),
        take("shrink_bias").reshape(-1),
        clip(matrix(take("router"), features)),
        clip(take("router_bias").reshape(1, -1)).reshape(-1),
        take("correction").reshape(-1)[:channels],
    )


def solution(mesh):
    split = P(("dp", "rep"), None)
    sizes = dict(mesh.shape)
    return jax.shard_map(
        functools.partial(body, sizes),
        mesh=mesh,
        in_specs=(split, split, split, P(("dp", "rep"))) + (P(),) * 18,
        out_specs=(split, split) + (P(),) * 17,
        check_vma=False,
    )
```

```python
import functools

import jax
import jax.numpy as jnp
from jax import lax
from jax.experimental import pallas as pl
from jax.experimental.pallas import tpu as pltpu
from jax.sharding import PartitionSpec as P

HEADS = 6
EPSILON = 1e-05
PENALTY = 1.0
GELU_COEF = 0.7978845608028654
GELU_CUBE = 0.044715
LOG2E = 1.4426950408889634
LANES = 128
ROWS = 512
KEYS = 512
LIMIT = 56 * 2**20

low = jnp.bfloat16
full = jnp.float32


def mul(left, right, dims=((1,), (0,))):
    return lax.dot_general(left, right, (dims, ((), ())), preferred_element_type=full)


NT = ((1,), (1,))
TN = ((0,), (0,))


def params(count):
    return pltpu.CompilerParams(
        dimension_semantics=("arbitrary",) * count, vmem_limit_bytes=LIMIT
    )


def whole(shape):
    return pl.BlockSpec(shape, lambda *step: (0,) * len(shape))


SCALAR = pl.BlockSpec(memory_space=pltpu.SMEM)


def normalize(values):
    centre = jnp.mean(values, axis=-1, keepdims=True)
    centred = values - centre
    spread = jnp.mean(centred * centred, axis=-1, keepdims=True)
    scale = lax.rsqrt(spread + EPSILON)
    return centred * scale, scale


def norm_back(grad, unit, scale, gain):
    e = grad * gain
    first = jnp.mean(e, axis=-1, keepdims=True)
    second = jnp.mean(e * unit, axis=-1, keepdims=True)
    return scale * (e - first - unit * second)


def column_sum(values):
    return jnp.sum(values, axis=0, keepdims=True)


def project_kernel(
    lead, x, embed, gain, shift, weight, query_b, value_b, first, projected
):
    stream = x[...] + embed[pl.ds(lead[0], 1), :]
    unit, _ = normalize(stream)
    rounded = (unit * gain[...][None, :] + shift[...][None, :]).astype(low)
    first[...] = rounded.T
    features = x.shape[1]
    query_row = query_b[...][None, :]
    bias = jnp.concatenate(
        [query_row, jnp.zeros_like(query_row), value_b[...][None, :]], axis=1
    )
    projected[...] = (mul(rounded, weight[...]) + bias).astype(low)


def project(lead, x, embed, gain, shift, weight, query_b, value_b):
    rows, features = x.shape
    wide = weight.shape[1]
    tables = (embed, gain, shift, weight, query_b, value_b)
    return pl.pallas_call(
        project_kernel,
        grid=(rows // ROWS,),
        in_specs=[SCALAR, pl.BlockSpec((ROWS, features), lambda i: (i, 0))]
        + [whole(table.shape) for table in tables],
        out_specs=[
            pl.BlockSpec((features, ROWS), lambda i: (0, i)),
            pl.BlockSpec((ROWS, wide), lambda i: (i, 0)),
        ],
        out_shape=[
            jax.ShapeDtypeStruct((features, rows), low),
            jax.ShapeDtypeStruct((rows, wide), low),
        ],
        compiler_params=params(1),
        name="project",
    )(lead, x, *tables)


def attend_kernel(size, q, k, v, probs, mixed, inverse, turned):
    keys = k.shape[0]
    count = q.shape[0]
    scaling = size ** (-0.5) * LOG2E

    @pl.when(pl.program_id(1) == 0)
    def _():
        across = v[...].T
        tail = lax.broadcasted_iota(jnp.int32, (16, keys), 0)
        ones = jnp.where(tail == 0, 1.0, 0.0).astype(low)
        for head in range(2):
            turned[head, 0:size, :] = across[head * size : (head + 1) * size, :]
            turned[head, size : size + 16, :] = ones

    lane = lax.broadcasted_iota(jnp.int32, (1, LANES), 1)

    def scores(head, start):
        mask = jnp.where(lane // size == head, 1.0, 0.0).astype(low)
        return mul(k[start : start + keys, :], q[...] * mask, NT) * scaling

    def finish(head, total):
        spread = total[size : size + 1, :]
        inv = 1.0 / spread
        inverse[0, head : head + 1, :] = inv
        mixed[head * size : (head + 1) * size, :] = (total[0:size, :] * inv).astype(low)
        return spread

    extremes = []
    for head in range(2):
        total = jnp.zeros((size + 16, count), full)
        for start in (0,):
            p = jnp.exp2(scores(head, start)).astype(low)
            probs[0, head, start : start + keys, :] = p
            total = total + mul(turned[head, :, start : start + keys], p)
        spread = finish(head, total)
        extremes.append(spread)

    both = jnp.concatenate(extremes, axis=0)
    inside = jnp.where((both > 1e-18) & (both < 1e18), 1.0, 0.0)

    @pl.when(jnp.min(inside) < 0.5)
    def _():
        for head in range(2):
            top = jnp.full((1, count), -jnp.inf, full)
            for start in (0,):
                top = jnp.maximum(
                    top, jnp.max(scores(head, start), axis=0, keepdims=True)
                )
            total = jnp.zeros((size + 16, count), full)
            for start in (0,):
                p = jnp.exp2(scores(head, start) - top).astype(low)
                probs[0, head, start : start + keys, :] = p
                total = total + mul(turned[head, :, start : start + keys], p)
            finish(head, total)


def attend(projected):
    rows, wide = projected.shape
    features = wide // 3
    pairs = features // LANES
    size = features // HEADS
    return pl.pallas_call(
        functools.partial(attend_kernel, size),
        grid=(pairs, rows // ROWS),
        in_specs=[
            pl.BlockSpec((ROWS, LANES), lambda p, i: (i, p)),
            pl.BlockSpec((rows, LANES), lambda p, i: (0, pairs + p)),
            pl.BlockSpec((rows, LANES), lambda p, i: (0, 2 * pairs + p)),
        ],
        out_specs=[
            pl.BlockSpec((1, 2, rows, ROWS), lambda p, i: (p, 0, 0, i)),
            pl.BlockSpec((LANES, ROWS), lambda p, i: (p, i)),
            pl.BlockSpec((1, 8, ROWS), lambda p, i: (p, 0, i)),
        ],
        out_shape=[
            jax.ShapeDtypeStruct((pairs, 2, rows, rows), low),
            jax.ShapeDtypeStruct((features, rows), low),
            jax.ShapeDtypeStruct((pairs, 8, rows), full),
        ],
        scratch_shapes=[pltpu.VMEM((2, size + 16, rows), low)],
        compiler_params=params(2),
        name="attend",
    )(projected, projected, projected)


def middle_kernel(
    spans,
    size,
    group,
    side,
    lead,
    x,
    mixed,
    inverse,
    experts,
    upstream,
    embed,
    merge_w,
    merge_b,
    gain,
    shift,
    expand_w,
    expand_b,
    shrink_w,
    shrink_b,
    router_w,
    columns,
    blended,
    d_mid,
    d_across,
    d_down,
    keep,
    send,
    grads,
    lanes,
    sems,
):
    features = x.shape[1]
    step = x.shape[0]
    hidden_size = expand_w.shape[1]
    channels = upstream.shape[0]
    chunk = hidden_size // 2

    @pl.when(pl.program_id(0) == 0)
    def _():
        grads[...] = jnp.zeros_like(grads)
        lanes[...] = jnp.zeros_like(lanes)

    def add(name, values, part=0):
        half, base = spans[name]
        height = values.shape[0]
        for block in range(values.shape[1] // LANES):
            start = base + (part + block) * height
            grads[half, start : start + height, :] += values[
                :, block * LANES : (block + 1) * LANES
            ]

    stream = x[...] + embed[pl.ds(lead[0], 1), :]
    mid = stream + mul(mixed[...], merge_w[...], TN) + merge_b[...][None, :]
    unit, scale = normalize(mid)
    gain_row = gain[...][None, :]
    second = (unit * gain_row + shift[...][None, :]).astype(low)
    output = mid + shrink_b[...][None, :]
    bias = expand_b[...][None, :]
    hidden, slope = [], []
    for start in range(0, hidden_size, chunk):
        part = slice(start, start + chunk)
        u = mul(second, expand_w[:, part]) + bias[:, part]
        square = u * u
        t = jnp.tanh(u * (GELU_COEF + GELU_COEF * GELU_CUBE * square))
        half = 0.5 + 0.5 * t
        act = u * half
        slope.append(
            half
            + act
            * (1.0 - half)
            * (2.0 * GELU_COEF + 6.0 * GELU_COEF * GELU_CUBE * square)
        )
        act = act.astype(low)
        hidden.append(act)
        output = output + mul(act, shrink_w[part, :])
    output_low = output.astype(low)
    logits = mul(router_w[...], output_low, NT) + columns[:, 0:1]
    valid = lax.broadcasted_iota(jnp.int32, (group, 1), 0) < channels
    parts = [logits[e * group : (e + 1) * group, :] for e in range(3)]
    largest = jnp.maximum(jnp.maximum(parts[0], parts[1]), parts[2])
    parts = [part - largest for part in parts]
    raised = [jnp.exp(part) for part in parts]
    total = raised[0] + raised[1] + raised[2]
    shared = jnp.log(total)
    logs = [part - shared for part in parts]
    share = 1.0 / total
    gates = [value * share for value in raised]

    def widen(values):
        return jnp.concatenate(
            [values, jnp.zeros((group - channels, step), full)], axis=0
        )

    frames = [
        widen(experts[e * channels : (e + 1) * channels, :]) for e in range(3)
    ]
    up = widen(upstream[...])
    mix = gates[0] * frames[0] + gates[1] * frames[1] + gates[2] * frames[2]
    entropy = -(gates[0] * logs[0] + gates[1] * logs[1] + gates[2] * logs[2])
    blended[...] = mix[:channels, :] + columns[:channels, 1:2]
    d_parts = [
        jnp.where(
            valid,
            gates[e] * (up * (frames[e] - mix) - PENALTY * (logs[e] + entropy)),
            0.0,
        )
        for e in range(3)
    ]
    for index, values in enumerate(d_parts + [up]):
        for start in range(0, step, LANES):
            lanes[index * group : (index + 1) * group, :] += values[
                :, start : start + LANES
            ]
    d_logits_low = jnp.concatenate(d_parts, axis=0).astype(low)
    add("router", mul(d_logits_low, output_low))
    d_output = mul(d_logits_low, router_w[...], TN)
    add("shrink_bias", column_sum(d_output))
    d_output_low = d_output.astype(low)
    d_turned = d_output_low.T
    second_turned = second.T
    d_second = jnp.zeros_like(d_output)
    for index, start in enumerate(range(0, hidden_size, chunk)):
        part = slice(start, start + chunk)
        d_pre = mul(d_output_low, shrink_w[part, :], NT) * slope[index]
        add("expand_bias", column_sum(d_pre), start // LANES)
        d_pre_low = d_pre.astype(low)
        d_second = d_second + mul(d_pre_low, expand_w[:, part], NT)
        add("expand", mul(second_turned, d_pre_low), start // LANES)
        add("shrink", mul(d_turned, hidden[index]), start // LANES)
    add("second_gain", column_sum(d_second * unit))
    add("second_shift", column_sum(d_second))
    grad_mid = d_output + norm_back(d_second, unit, scale, gain_row)
    d_mid[...] = grad_mid
    add("merge_bias", column_sum(grad_mid))
    d_mid_low = grad_mid.astype(low)
    add("merge", mul(mixed[...], d_mid_low))
    d_mixed = mul(merge_w[...], d_mid_low, NT).astype(low).astype(full)
    row = lax.broadcasted_iota(jnp.int32, (size, step), 0)
    stack = []
    for head in range(features // size):
        span = slice(head * size, (head + 1) * size)
        odd = head % 2
        inv = inverse[head // 2, odd : odd + 1, :]
        scaled = (d_mixed[span, :] * inv).astype(low)
        stack.append(scaled)
        centre = -column_sum(scaled.astype(full) * mixed[span, :].astype(full))
        one = centre.astype(low).astype(full)
        two = (centre - one).astype(low).astype(full)
        extra = jnp.where(
            row == 0,
            one,
            jnp.where(row == 1, two, jnp.where(row == 2, centre - one - two, 0.0)),
        ).astype(low)
        d_across[head, odd * size : (odd + 1) * size, :] = scaled
        d_across[head, (1 - odd) * size : (2 - odd) * size, :] = extra
    d_down[...] = jnp.concatenate(stack, axis=0).T

    @pl.when(pl.program_id(0) == pl.num_programs(0) - 1)
    def _():
        sums = column_sum(lanes[...].T)
        width = sums.shape[1]
        wide = up_to(width, LANES)
        sums = jnp.concatenate([sums, jnp.zeros((1, wide - width), full)], axis=1)
        add("head", sums)
        copies = [
            pltpu.make_async_copy(grads.at[side[0]], keep, sems.at[0]),
            pltpu.make_async_copy(grads.at[1 - side[0]], send, sems.at[1]),
        ]
        for copy in copies:
            copy.start()
        for copy in copies:
            copy.wait()


def middle(spans, height, group, side, lead, x, mixed, inverse, experts, upstream, tables):
    rows, features = x.shape
    size = features // HEADS
    channels = upstream.shape[0]
    step = ROWS
    anywhere = pl.BlockSpec(memory_space=pl.ANY)
    return pl.pallas_call(
        functools.partial(middle_kernel, spans, size, group),
        grid=(rows // step,),
        in_specs=[
            SCALAR,
            SCALAR,
            pl.BlockSpec((step, features), lambda i: (i, 0)),
            pl.BlockSpec((features, step), lambda i: (0, i)),
            pl.BlockSpec((inverse.shape[0], 8, step), lambda i: (0, 0, i)),
            pl.BlockSpec((experts.shape[0], step), lambda i: (0, i)),
            pl.BlockSpec((channels, step), lambda i: (0, i)),
        ]
        + [whole(table.shape) for table in tables],
        out_specs=[
            pl.BlockSpec((channels, step), lambda i: (0, i)),
            pl.BlockSpec((step, features), lambda i: (i, 0)),
            pl.BlockSpec((HEADS, LANES, step), lambda i: (0, 0, i)),
            pl.BlockSpec((step, features), lambda i: (i, 0)),
            anywhere,
            anywhere,
        ],
        out_shape=[
            jax.ShapeDtypeStruct((channels, rows), full),
            jax.ShapeDtypeStruct((rows, features), full),
            jax.ShapeDtypeStruct((HEADS, LANES, rows), low),
            jax.ShapeDtypeStruct((rows, features), low),
            jax.ShapeDtypeStruct((height, LANES), full),
            jax.ShapeDtypeStruct((height, LANES), full),
        ],
        scratch_shapes=[
            pltpu.VMEM((2, height, LANES), full),
            pltpu.VMEM((4 * group, LANES), full),
            pltpu.SemaphoreType.DMA((2,)),
        ],
        compiler_params=params(1),
        name="middle",
    )(side, lead, x, mixed, inverse, experts, upstream, *tables)


def attend_back_kernel(size, first_part, last_part, *refs):
    if first_part:
        q, k, v, d_across, d_down, probs, d_query, d_pair = refs[:8]
    else:
        q, k, v, d_across, d_down, probs, carry, _, d_query, d_pair = refs[:10]
    total = refs[-1] if last_part else d_query
    step = pl.program_id(0)
    rows = q.shape[0]
    block = k.shape[0]
    scaling = size ** (-0.5)
    lane = lax.broadcasted_iota(jnp.int32, (1, LANES), 1)

    @pl.when(step == 0)
    def _():
        total[...] = jnp.zeros_like(total) if first_part else carry[...]

    k_across = k[...].T
    d_keys, d_values = [], []
    for head in range(2):
        base = (1 - head) * size
        data = jnp.where(lane // size == head, 1.0, 0.0).astype(low)
        ones = jnp.where((lane >= base) & (lane < base + 3), 1.0, 0.0).astype(low)
        values = v[...] * data + ones
        d_k = jnp.zeros((block, LANES), full)
        d_v = jnp.zeros((block, LANES), full)
        for start in (0,):
            span = slice(start, start + rows)
            p = probs[0, head, :, span]
            d_p = mul(values, d_across[head, :, span])
            d_s = (p.astype(full) * d_p).astype(low)
            total[head * size : (head + 1) * size, span] += mul(
                k_across[head * size : (head + 1) * size, :], d_s
            )
            d_v = d_v + mul(p, d_down[span, :])
            d_k = d_k + mul(d_s, q[span, :])
        d_keys.append(d_k)
        d_values.append(d_v)
    d_pair[0] = (jnp.where(lane < size, *d_keys) * scaling).astype(low)
    d_pair[1] = jnp.where(lane < size, *d_values).astype(low)

    if last_part:

        @pl.when(step == pl.num_programs(0) - 1)
        def _():
            d_query[...] = (total[...].T * scaling).astype(low)


def attend_back(pair, base, steps, projected, d_across, d_down, probs, carried):
    rows, wide = projected.shape
    features = wide // 3
    pairs = features // LANES
    size = features // HEADS
    total = rows // KEYS
    first_part, last_part = base == 0, base + steps == total
    across = (rows, LANES) if last_part else (LANES, rows)
    return pl.pallas_call(
        functools.partial(attend_back_kernel, size, first_part, last_part),
        grid=(steps,),
        in_specs=[
            pl.BlockSpec((rows, LANES), lambda i: (0, pair)),
            pl.BlockSpec((KEYS, LANES), lambda i: (base + i, pairs + pair)),
            pl.BlockSpec((KEYS, LANES), lambda i: (base + i, 2 * pairs + pair)),
            pl.BlockSpec((2, LANES, rows), lambda i: (pair, 0, 0)),
            pl.BlockSpec((rows, LANES), lambda i: (0, pair)),
            pl.BlockSpec((1, 2, KEYS, rows), lambda i: (pair, 0, base + i, 0)),
        ]
        + ([] if first_part else [whole((LANES, rows)), pl.BlockSpec(memory_space=pl.ANY)]),
        out_specs=[
            whole(across),
            pl.BlockSpec((2, KEYS, LANES), lambda i: (0, base + i, 0)),
        ],
        out_shape=[
            jax.ShapeDtypeStruct(across, low if last_part else full),
            jax.ShapeDtypeStruct((2, rows, LANES), low),
        ],
        scratch_shapes=[pltpu.VMEM((LANES, rows), full)] if last_part else [],
        input_output_aliases={} if first_part else {7: 1},
        compiler_params=params(1),
        cost_estimate=pl.CostEstimate(
            flops=10 * rows * rows * 256 * steps // total,
            bytes_accessed=rows * rows * 4 * steps // total,
            transcendentals=0,
        ),
        name="attend_back",
    )(projected, projected, projected, d_across, d_down, probs, *carried)


def weigh_kernel(pairs, places, side, weight, first, *refs):
    d_query, d_pair = refs[:pairs], refs[pairs : 2 * pairs]
    keep, send, sums, grads, sems = refs[2 * pairs :]
    features = first.shape[0]
    grads[...] = jnp.zeros_like(grads)
    sums[...] = jnp.zeros_like(sums)
    parts = []
    for kind in range(3):
        for pair in range(pairs):
            values = d_query[pair][...] if kind == 0 else d_pair[pair][kind - 1]
            parts.append(values)
            if kind != 1:
                sums[
                    kind // 2 : kind // 2 + 1, pair * LANES : (pair + 1) * LANES
                ] = weight[0] * column_sum(values.astype(full))
    for start in range(0, len(parts), 2):
        some = parts[start : start + 2]
        product = mul(first[...], jnp.concatenate(some, axis=1)) * weight[0]
        for index in range(len(some)):
            half, base = places[start + index]
            grads[half, base : base + features, :] = product[
                :, index * LANES : (index + 1) * LANES
            ]
    copies = [
        pltpu.make_async_copy(grads.at[side[0]], keep, sems.at[0]),
        pltpu.make_async_copy(grads.at[1 - side[0]], send, sems.at[1]),
    ]
    for copy in copies:
        copy.start()
    for copy in copies:
        copy.wait()


def weigh(places, height, side, weight, first, d_query, d_pair):
    features = first.shape[0]
    vmem = pl.BlockSpec(memory_space=pltpu.VMEM)
    anywhere = pl.BlockSpec(memory_space=pl.ANY)
    pairs = len(d_query)
    return pl.pallas_call(
        functools.partial(weigh_kernel, pairs, places),
        in_specs=[SCALAR, SCALAR, vmem] + [vmem] * (2 * pairs),
        out_specs=[anywhere, anywhere, vmem],
        out_shape=[
            jax.ShapeDtypeStruct((height, LANES), full),
            jax.ShapeDtypeStruct((height, LANES), full),
            jax.ShapeDtypeStruct((8, features), full),
        ],
        scratch_shapes=[
            pltpu.VMEM((2, height, LANES), full),
            pltpu.SemaphoreType.DMA((2,)),
        ],
        compiler_params=pltpu.CompilerParams(vmem_limit_bytes=LIMIT),
        cost_estimate=pl.CostEstimate(
            flops=18 * d_query[0].shape[0] * features * features,
            bytes_accessed=d_query[0].shape[0] * features * 8,
            transcendentals=0,
        ),
        name="weigh",
    )(side, weight, first, *d_query, *d_pair)


def finish_kernel(pairs, last_part, lead, weight, x, embed, gain, wide, d_mid, *rest):
    d_query, d_pair, rest = rest[:pairs], rest[pairs : 2 * pairs], rest[2 * pairs :]
    if last_part:
        earlier, biases, _, grad_input, vectors, sums = rest
    else:
        grad_input, sums = rest
    step = pl.program_id(0)

    @pl.when(step == 0)
    def _():
        sums[...] = earlier[...] if last_part else jnp.zeros_like(sums)

    stream = x[...] + embed[pl.ds(lead[0], 1), :]
    unit, scale = normalize(stream)
    parts = []
    for kind in range(3):
        for pair in range(pairs):
            parts.append(d_query[pair][...] if kind == 0 else d_pair[pair][kind - 1])
    d_first = mul(jnp.concatenate(parts, axis=1), wide[...], NT)
    d_stream = (
        d_mid[...] + norm_back(d_first, unit, scale, gain[...][None, :])
    ) * weight[0]
    grad_input[...] = d_stream
    sums[0:1, :] += column_sum(d_first * unit) * weight[0]
    sums[1:2, :] += column_sum(d_first) * weight[0]
    sums[2:3, :] += column_sum(d_stream)

    if last_part:

        @pl.when(step == pl.num_programs(0) - 1)
        def _():
            vectors[...] = jnp.zeros_like(vectors)
            for block in range(pairs):
                lanes = slice(block * LANES, (block + 1) * LANES)
                for index, ref in enumerate((sums, sums, biases, biases)):
                    at = index * pairs + block
                    vectors[at : at + 1, :] = ref[index % 2 : index % 2 + 1, lanes]
                vectors[pl.ds((4 + lead[0]) * pairs + block, 1), :] = sums[2:3, lanes]


def finish(base, steps, lead, weight, x, embed, gain, wide, d_mid, d_query, d_pair, carried):
    rows, features = x.shape
    pairs = len(d_query)
    total = rows // ROWS
    last_part = base + steps == total
    height = up_to((4 + embed.shape[0]) * pairs, 8)
    row_spec = pl.BlockSpec((ROWS, features), lambda i: (base + i, 0))
    small = pl.BlockSpec((8, features), lambda i: (0, 0))
    return pl.pallas_call(
        functools.partial(finish_kernel, pairs, last_part),
        grid=(steps,),
        in_specs=[
            SCALAR,
            SCALAR,
            row_spec,
            whole(embed.shape),
            whole(gain.shape),
            whole(wide.shape),
            row_spec,
        ]
        + [pl.BlockSpec((ROWS, LANES), lambda i: (base + i, 0))] * pairs
        + [pl.BlockSpec((2, ROWS, LANES), lambda i: (0, base + i, 0))] * pairs
        + ([small, small, pl.BlockSpec(memory_space=pl.ANY)] if last_part else []),
        out_specs=[row_spec, whole((height, LANES)) if last_part else small],
        out_shape=[
            jax.ShapeDtypeStruct((rows, features), full),
            jax.ShapeDtypeStruct((height, LANES) if last_part else (8, features), full),
        ],
        scratch_shapes=[pltpu.VMEM((8, features), full)] if last_part else [],
        input_output_aliases={9 + 2 * pairs: 0} if last_part else {},
        compiler_params=params(1),
        cost_estimate=pl.CostEstimate(
            flops=6 * rows * features * features * steps // total,
            bytes_accessed=rows * features * 18 * steps // total,
            transcendentals=0,
        ),
        name="finish",
    )(lead, weight, x, embed, gain, wide, d_mid, *d_query, *d_pair, *carried)


def unpack_kernel(spans, group, channels, places, *refs):
    pieces = refs[:4]
    expand, shrink, merge, router, vectors, grads, sems = refs[4:]
    quarter = pieces[0].shape[0]
    height = 2 * quarter
    arrivals = [
        pltpu.make_async_copy(
            pieces[n], grads.at[pl.ds(places[n] * quarter, quarter)], sems.at[n]
        )
        for n in range(4)
    ]
    for copy in arrivals:
        copy.start()
    for copy in arrivals:
        copy.wait()

    def block(name, rows, index):
        half, base = spans[name]
        start = half * height + base + index * rows
        return grads.at[pl.ds(start, rows)]

    features, hidden = expand.shape
    leaving = []
    for target, name in ((expand, "expand"), (merge, "merge")):
        for index in range(target.shape[1] // LANES):
            leaving.append(
                pltpu.make_async_copy(
                    block(name, features, index),
                    target.at[:, pl.ds(index * LANES, LANES)],
                    sems.at[4 + len(leaving)],
                )
            )
    for copy in leaving:
        copy.start()
    for index in range(hidden // LANES):
        shrink[index * LANES : (index + 1) * LANES, :] = block("shrink", features, index)[
            ...
        ].T
    rows = 3 * group
    for index in range(features // LANES):
        values = block("router", rows, index)
        for e in range(3):
            router[
                e * channels : (e + 1) * channels, index * LANES : (index + 1) * LANES
            ] = values[e * group : e * group + channels, :]
    vectors[...] = block("expand_bias", vectors.shape[0], 0)[...]
    for copy in leaving:
        copy.wait()


def unpack(spans, group, channels, features, hidden, tall, places, pieces):
    vmem = pl.BlockSpec(memory_space=pltpu.VMEM)
    anywhere = pl.BlockSpec(memory_space=pl.ANY)
    quarter = pieces[0].shape[0]
    return pl.pallas_call(
        functools.partial(unpack_kernel, spans, group, channels),
        in_specs=[SCALAR] + [anywhere] * 4,
        out_specs=[anywhere, vmem, anywhere, vmem, vmem],
        out_shape=[
            jax.ShapeDtypeStruct((features, hidden), full),
            jax.ShapeDtypeStruct((hidden, features), full),
            jax.ShapeDtypeStruct((features, features), full),
            jax.ShapeDtypeStruct((3 * channels, features), full),
            jax.ShapeDtypeStruct((tall, LANES), full),
        ],
        scratch_shapes=[
            pltpu.VMEM((4 * quarter, LANES), full),
            pltpu.SemaphoreType.DMA((4 + (hidden + features) // LANES,)),
        ],
        compiler_params=pltpu.CompilerParams(vmem_limit_bytes=LIMIT),
        cost_estimate=pl.CostEstimate(
            flops=8 * 10**9, bytes_accessed=quarter * 8192, transcendentals=0
        ),
        name="unpack",
    )(places, *pieces)


def join_kernel(shared, side, mine, got, out):
    height = mine.shape[0] - shared
    out[:shared, :] = mine[:shared, :] + got[:shared, :]
    left = pl.multiple_of(shared + side[0] * height, 8)
    right = pl.multiple_of(shared + (1 - side[0]) * height, 8)
    out[pl.ds(left, height), :] = mine[shared:, :]
    out[pl.ds(right, height), :] = got[shared:, :]


def join(shared, side, mine, got):
    vmem = pl.BlockSpec(memory_space=pltpu.VMEM)
    height = 2 * mine.shape[0] - shared
    return pl.pallas_call(
        functools.partial(join_kernel, shared),
        in_specs=[SCALAR, vmem, vmem],
        out_specs=vmem,
        out_shape=jax.ShapeDtypeStruct((height, LANES), full),
        compiler_params=pltpu.CompilerParams(vmem_limit_bytes=LIMIT),
        name="join",
    )(side, mine, got)


def settle_kernel(places, side, mine, got, attend, embed, vectors, grads, sums, sems):
    shared = sums.shape[0]
    height = mine.shape[0] - shared
    features = attend.shape[0]
    leads = embed.shape[0]
    pairs = features // LANES
    arrivals = [
        pltpu.make_async_copy(
            mine.at[pl.ds(shared, height)], grads.at[side[0]], sems.at[0]
        ),
        pltpu.make_async_copy(
            got.at[pl.ds(shared, height)], grads.at[1 - side[0]], sems.at[1]
        ),
    ]
    for copy in arrivals:
        copy.start()
    sums[...] = mine[:shared, :] + got[:shared, :]
    vectors[...] = sums[: vectors.shape[0], :]
    for block in range(pairs):
        embed[:, block * LANES : (block + 1) * LANES] = sums[
            pl.ds(4 * pairs + block, leads, stride=pairs), :
        ]
    for copy in arrivals:
        copy.wait()
    leaving = []
    for index, (half, base) in enumerate(places):
        leaving.append(
            pltpu.make_async_copy(
                grads.at[half, pl.ds(base, features)],
                attend.at[:, pl.ds(index * LANES, LANES)],
                sems.at[2 + index],
            )
        )
    for copy in leaving:
        copy.start()
    for copy in leaving:
        copy.wait()


def settle(places, shared, leads, features, side, mine, got):
    vmem = pl.BlockSpec(memory_space=pltpu.VMEM)
    height = mine.shape[0] - shared
    return pl.pallas_call(
        functools.partial(settle_kernel, places),
        in_specs=[SCALAR, vmem, vmem],
        out_specs=[pl.BlockSpec(memory_space=pl.ANY), vmem, vmem],
        out_shape=[
            jax.ShapeDtypeStruct((features, 3 * features), full),
            jax.ShapeDtypeStruct((leads, features), full),
            jax.ShapeDtypeStruct((up_to(4 * features // LANES, 8), LANES), full),
        ],
        scratch_shapes=[
            pltpu.VMEM((2, height, LANES), full),
            pltpu.VMEM((shared, LANES), full),
            pltpu.SemaphoreType.DMA((2 + len(places),)),
        ],
        compiler_params=pltpu.CompilerParams(vmem_limit_bytes=LIMIT),
        name="settle",
    )(side, mine, got)


def up_to(value, step):
    return -(-value // step) * step


def tie(value, *others):
    return lax.optimization_barrier((value,) + others)[0]


def routes(sizes):
    inner = sizes["rep"]
    outer = sizes["dp"]
    if outer % 2:
        return 0, ((), ())
    far = [inner << n for n in range(1, outer.bit_length() - 1)]
    near = [1 << n for n in range(inner.bit_length() - 1)]
    even = []
    for n in range(max(len(far), len(near))):
        even += far[n : n + 1] + near[n : n + 1]
    odd = even[1:3] + even[:1] + even[3:]
    return inner, (tuple(even), tuple(odd))


class Ring:
    def __init__(self, sizes):
        self.count = sizes["dp"] * sizes["rep"]
        self.core_bit, self.orders = routes(sizes)
        self.hops = len(self.orders[0]) + 1 if self.core_bit else 0
        self.index = lax.axis_index(("dp", "rep"))

    def bits(self, hop):
        if hop == 0:
            return self.core_bit, self.core_bit
        return self.orders[0][hop - 1], self.orders[1][hop - 1]

    def swap(self, values, hop):
        pair = self.bits(hop)
        moves = [
            (i, i ^ pair[(i // self.core_bit) % 2]) for i in range(self.count)
        ]
        return lax.ppermute(values, ("dp", "rep"), moves)

    def side(self, hop, partner=False):
        if not self.hops:
            return jnp.int32(0)
        even, odd = self.bits(hop)
        if partner:
            even, odd = odd, even
        bit = even
        if even != odd:
            bit = jnp.where(self.index & self.core_bit == 0, even, odd)
        return jnp.where(self.index & bit == 0, 0, 1)

    def scatter(self, keep, send, factors=(None, None)):
        got = self.swap(send, 0)
        beside = yield send
        got = got if beside is None else tie(got, beside)
        terms = [[keep, 0, factors[0]], [got, 0, factors[1]]]
        length = keep.shape[0]

        def region(start, size):
            total = None
            for values, offset, factor in terms:
                part = lax.dynamic_slice_in_dim(values, offset + start, size, 0)
                part = part if factor is None else part * factor
                total = part if total is None else total + part
            return total

        for hop in range(1, self.hops):
            length //= 2
            side = self.side(hop)
            send = region((1 - side) * length, length)
            got = self.swap(send, hop)
            for term in terms:
                term[1] = term[1] + side * length
            beside = yield send
            terms.append([got if beside is None else tie(got, beside), 0, None])
        return region(0, length)

    def gather(self, values):
        for hop in reversed(range(2, self.hops)):
            got = self.swap(values, hop)
            beside = yield values
            if beside is not None:
                got = tie(got, beside)
            values = jnp.where(
                self.side(hop) == 0,
                jnp.concatenate([values, got]),
                jnp.concatenate([got, values]),
            )
        got = self.swap(values, 1)
        across = self.swap(values, 0)
        beside = yield values
        if beside is not None:
            got, across = tie(got, beside), tie(across, beside)
        final = self.swap(got, 0)
        beside = yield got
        if beside is not None:
            final = tie(final, beside)
        core, near, far = self.side(0), self.side(1), self.side(1, partner=True)
        places = jnp.stack(
            [
                2 * core + near,
                2 * core + 1 - near,
                2 * (1 - core) + far,
                2 * (1 - core) + 1 - far,
            ]
        )
        return places, (values, got, across, final)


class Flow:
    def __init__(self, steps):
        self.steps = steps
        self.done = False
        self.sent = None
        self.result = None
        self.push(None)

    def push(self, beside):
        if self.done:
            return
        try:
            self.sent = self.steps.send(beside)
        except StopIteration as stop:
            self.done, self.sent, self.result = True, None, stop.value

    def drain(self):
        while not self.done:
            self.push(None)
        return self.result


def total_of(ring, keep, send, factors):
    part = yield from ring.scatter(keep, send, factors)
    return (yield from ring.gather(part))


def body(sizes, *args):
    (
        block_input,
        expert_out,
        upstream,
        lead_index,
        lead_frames,
        lead_embed,
        first_gain,
        first_shift,
        attend_weight,
        query_bias,
        value_bias,
        merge_weight,
        merge_bias,
        second_gain,
        second_shift,
        expand_weight,
        expand_bias,
        shrink_weight,
        shrink_bias,
        router_weight,
        router_bias,
        correction,
    ) = args
    rows, features = block_input.shape
    channels = correction.shape[0]
    leads = lead_embed.shape[0]
    hidden = expand_bias.shape[0]
    devices = sizes["dp"] * sizes["rep"]
    pairs = features // LANES
    grain = 4 * devices
    ring = Ring(sizes)
    core = ring.side(0).reshape(1)

    tall = max(8, 2048 // devices)
    mine = lead_index[0].astype(full)
    leads_seen = lax.optimization_barrier(
        lax.all_gather(
            lax.optimization_barrier(jnp.full((tall, LANES), mine)), ("dp", "rep")
        )
    )[:, 0, 0]
    table = lead_frames.astype(full)

    def weight_of(lead):
        count = jnp.sum((leads_seen == lead).astype(full))
        chosen = jnp.sum(
            jnp.where(jnp.arange(leads, dtype=jnp.int32).astype(full) == lead, table, 0.0)
        )
        return chosen * devices / (count * jnp.sum(table))

    scale = weight_of(mine)
    other = scale
    if ring.hops:
        position = ring.index ^ ring.core_bit
        other = weight_of(
            jnp.sum(jnp.where(jnp.arange(devices) == position, leads_seen, 0.0))
        )
    weight = scale.reshape(1)

    first, projected = project(
        lead_index,
        block_input,
        lead_embed,
        first_gain,
        first_shift,
        attend_weight,
        query_bias,
        value_bias,
    )
    probs, mixed, inverse = attend(projected)

    group = up_to(channels, 16)
    spans, heights = {}, [0, 0]
    for name, half, height in (
        ("expand", 0, features * hidden // LANES),
        ("merge", 0, features * features // LANES),
        ("shrink", 1, features * hidden // LANES),
        ("router", 1, features * 3 * group // LANES),
        ("expand_bias", 1, hidden // LANES),
        ("shrink_bias", 1, pairs),
        ("merge_bias", 1, pairs),
        ("second_gain", 1, pairs),
        ("second_shift", 1, pairs),
        ("head", 1, up_to(4 * group, LANES) // LANES),
    ):
        spans[name] = (half, heights[half])
        heights[half] += height
    vector_rows = up_to(heights[1] - spans["expand_bias"][1], 8)
    height = up_to(max(heights[0], spans["expand_bias"][1] + vector_rows), grain)
    wide_router = jnp.pad(
        router_weight.T.reshape(3, channels, features),
        ((0, 0), (0, group - channels), (0, 0)),
    ).reshape(3 * group, features)
    columns = jnp.stack(
        [
            jnp.pad(
                router_bias.reshape(3, channels), ((0, 0), (0, group - channels))
            ).reshape(-1),
            jnp.pad(correction, (0, 3 * group - channels)),
        ],
        axis=1,
    )
    tables = (
        lead_embed,
        merge_weight,
        merge_bias,
        second_gain,
        second_shift,
        expand_weight,
        expand_bias,
        shrink_weight,
        shrink_bias,
        wide_router,
        columns,
    )
    blended, d_mid, d_across, d_down, keep, send = middle(
        spans,
        height,
        group,
        core,
        lead_index,
        block_input,
        mixed,
        inverse,
        expert_out.T,
        upstream.T,
        tables,
    )
    flow = None
    if ring.hops:
        flow = Flow(total_of(ring, keep, tie(send, leads_seen), (scale, other)))
    plan = ((1, 2, 1), (1, 1, 1, 1), (1, 2, 1))
    d_query, d_pair = [], []
    for pair in range(pairs):
        carried = ()
        base = 0
        for steps in plan[pair]:
            now = d_down if flow is None or flow.done else tie(d_down, flow.sent)
            carried = attend_back(
                pair, base, steps, projected, d_across, now, probs, carried
            )
            base += steps
            if flow is not None:
                flow.push(carried[0])
        d_query.append(carried[0])
        d_pair.append(carried[1])
    places = tuple(
        (n // 5, (n % 5) * features) for n in range(3 * pairs)
    )
    tail_height = up_to(5 * features, grain)
    now = weight if flow is None else tie(weight, flow.drain()[1][3])
    tail_keep, tail_send, biases = weigh(
        places, tail_height, core, now, first, d_query, d_pair
    )
    late = None
    if ring.hops:
        late = Flow(ring.scatter(tail_keep, tail_send))
    carried = ()
    base = 0
    for steps in (2, 2):
        now = weight if late is None else tie(weight, late.sent)
        grad_input, sums = finish(
            base,
            steps,
            lead_index,
            now,
            block_input,
            lead_embed,
            first_gain,
            attend_weight,
            d_mid,
            d_query,
            d_pair,
            carried,
        )
        base += steps
        carried = (sums, biases, grad_input)
        if late is not None:
            late.push(sums)
    shared = sums.shape[0]
    if ring.hops:
        where, pieces = flow.result
        where = tie(where, late.sent)
    else:
        where = jnp.arange(4, dtype=jnp.int32)
        pieces = [
            half[start : start + height // 2] * scale
            for half in (keep, send)
            for start in (0, height // 2)
        ]
    grad_expand, grad_shrink, grad_merge, grad_router, vectors = unpack(
        spans, group, channels, features, hidden, vector_rows, where, pieces
    )
    first_vector = spans["expand_bias"][1]

    def take(name, length):
        start = spans[name][1] - first_vector
        return vectors[start : start + length // LANES].reshape(-1)

    head = take("head", up_to(4 * group, LANES))
    middle_vectors = (
        take("merge_bias", features),
        take("second_gain", features),
        take("second_shift", features),
        take("expand_bias", hidden),
        take("shrink_bias", features),
        head[: 3 * group].reshape(3, group)[:, :channels].reshape(-1),
        head[3 * group : 3 * group + channels],
    )
    if ring.hops:
        late.push(vectors)
        piece = jnp.concatenate([sums, late.drain()])
        for hop in reversed(range(1, ring.hops)):
            got = ring.swap(piece, hop)
            piece = join(shared, ring.side(hop).reshape(1), piece, got)
        got = ring.swap(piece, 0)
    else:
        piece = jnp.concatenate([sums, tail_keep])
        got = jnp.concatenate([jnp.zeros_like(sums), tail_send])
    grad_attend, grad_embed, small = settle(
        places, shared, leads, features, core, piece, got
    )
    small = small[: 4 * pairs].reshape(4, features)
    merge_b, gain_b, shift_b, expand_b, shrink_b, router_b, correct = middle_vectors
    return (
        blended.T,
        grad_input,
        grad_embed,
        small[0],
        small[1],
        grad_attend,
        small[2],
        small[3],
        grad_merge,
        merge_b,
        gain_b,
        shift_b,
        grad_expand,
        expand_b,
        grad_shrink,
        shrink_b,
        grad_router.T,
        router_b,
        correct,
    )


def solution(mesh):
    split = P(("dp", "rep"), None)
    sizes = dict(mesh.shape)
    return jax.shard_map(
        functools.partial(body, sizes),
        mesh=mesh,
        in_specs=(split, split, split, P(("dp", "rep"))) + (P(),) * 18,
        out_specs=(split, split) + (P(),) * 17,
        check_vma=False,
    )
```

```python
import functools

import jax
import jax.numpy as jnp
from jax import lax
from jax.experimental import pallas as pl
from jax.experimental.pallas import tpu as pltpu
from jax.sharding import PartitionSpec as P

HEADS = 6
EPSILON = 1e-05
PENALTY = 1.0
GELU_COEF = 0.7978845608028654
GELU_CUBE = 0.044715
LOG2E = 1.4426950408889634
LANES = 128
ROWS = 512
KEYS = 512
LIMIT = 56 * 2**20

low = jnp.bfloat16
full = jnp.float32


def mul(left, right, dims=((1,), (0,))):
    return lax.dot_general(left, right, (dims, ((), ())), preferred_element_type=full)


NT = ((1,), (1,))
TN = ((0,), (0,))


def params(count):
    return pltpu.CompilerParams(
        dimension_semantics=("arbitrary",) * count, vmem_limit_bytes=LIMIT
    )


def whole(shape):
    return pl.BlockSpec(shape, lambda *step: (0,) * len(shape))


SCALAR = pl.BlockSpec(memory_space=pltpu.SMEM)


def normalize(values):
    centre = jnp.mean(values, axis=-1, keepdims=True)
    centred = values - centre
    spread = jnp.mean(centred * centred, axis=-1, keepdims=True)
    scale = lax.rsqrt(spread + EPSILON)
    return centred * scale, scale


def norm_back(grad, unit, scale, gain):
    e = grad * gain
    first = jnp.mean(e, axis=-1, keepdims=True)
    second = jnp.mean(e * unit, axis=-1, keepdims=True)
    return scale * (e - first - unit * second)


def column_sum(values):
    return jnp.sum(values, axis=0, keepdims=True)


def project_kernel(
    lead, x, embed, gain, shift, weight, query_b, value_b, first, projected
):
    stream = x[...] + embed[pl.ds(lead[0], 1), :]
    unit, _ = normalize(stream)
    rounded = (unit * gain[...][None, :] + shift[...][None, :]).astype(low)
    first[...] = rounded.T
    features = x.shape[1]
    query_row = query_b[...][None, :]
    bias = jnp.concatenate(
        [query_row, jnp.zeros_like(query_row), value_b[...][None, :]], axis=1
    )
    projected[...] = (mul(rounded, weight[...]) + bias).astype(low)


def project(lead, x, embed, gain, shift, weight, query_b, value_b):
    rows, features = x.shape
    wide = weight.shape[1]
    tables = (embed, gain, shift, weight, query_b, value_b)
    return pl.pallas_call(
        project_kernel,
        grid=(rows // ROWS,),
        in_specs=[SCALAR, pl.BlockSpec((ROWS, features), lambda i: (i, 0))]
        + [whole(table.shape) for table in tables],
        out_specs=[
            pl.BlockSpec((features, ROWS), lambda i: (0, i)),
            pl.BlockSpec((ROWS, wide), lambda i: (i, 0)),
        ],
        out_shape=[
            jax.ShapeDtypeStruct((features, rows), low),
            jax.ShapeDtypeStruct((rows, wide), low),
        ],
        compiler_params=params(1),
        name="project",
    )(lead, x, *tables)


def attend_kernel(size, q, k, v, probs, mixed, inverse, turned):
    keys = k.shape[0]
    count = q.shape[0]
    scaling = size ** (-0.5) * LOG2E

    @pl.when(pl.program_id(1) == 0)
    def _():
        across = v[...].T
        tail = lax.broadcasted_iota(jnp.int32, (16, keys), 0)
        ones = jnp.where(tail == 0, 1.0, 0.0).astype(low)
        for head in range(2):
            turned[head, 0:size, :] = across[head * size : (head + 1) * size, :]
            turned[head, size : size + 16, :] = ones

    lane = lax.broadcasted_iota(jnp.int32, (1, LANES), 1)

    def scores(head, start):
        mask = jnp.where(lane // size == head, 1.0, 0.0).astype(low)
        return mul(k[start : start + keys, :], q[...] * mask, NT) * scaling

    def finish(head, total):
        spread = total[size : size + 1, :]
        inv = 1.0 / spread
        inverse[0, head : head + 1, :] = inv
        mixed[head * size : (head + 1) * size, :] = (total[0:size, :] * inv).astype(low)
        return spread

    extremes = []
    for head in range(2):
        total = jnp.zeros((size + 16, count), full)
        for start in (0,):
            p = jnp.exp2(scores(head, start)).astype(low)
            probs[0, head, start : start + keys, :] = p
            total = total + mul(turned[head, :, start : start + keys], p)
        spread = finish(head, total)
        extremes.append(spread)

    both = jnp.concatenate(extremes, axis=0)
    inside = jnp.where((both > 1e-18) & (both < 1e18), 1.0, 0.0)

    @pl.when(jnp.min(inside) < 0.5)
    def _():
        for head in range(2):
            top = jnp.full((1, count), -jnp.inf, full)
            for start in (0,):
                top = jnp.maximum(
                    top, jnp.max(scores(head, start), axis=0, keepdims=True)
                )
            total = jnp.zeros((size + 16, count), full)
            for start in (0,):
                p = jnp.exp2(scores(head, start) - top).astype(low)
                probs[0, head, start : start + keys, :] = p
                total = total + mul(turned[head, :, start : start + keys], p)
            finish(head, total)


def attend(projected):
    rows, wide = projected.shape
    features = wide // 3
    pairs = features // LANES
    size = features // HEADS
    return pl.pallas_call(
        functools.partial(attend_kernel, size),
        grid=(pairs, rows // ROWS),
        in_specs=[
            pl.BlockSpec((ROWS, LANES), lambda p, i: (i, p)),
            pl.BlockSpec((rows, LANES), lambda p, i: (0, pairs + p)),
            pl.BlockSpec((rows, LANES), lambda p, i: (0, 2 * pairs + p)),
        ],
        out_specs=[
            pl.BlockSpec((1, 2, rows, ROWS), lambda p, i: (p, 0, 0, i)),
            pl.BlockSpec((LANES, ROWS), lambda p, i: (p, i)),
            pl.BlockSpec((1, 8, ROWS), lambda p, i: (p, 0, i)),
        ],
        out_shape=[
            jax.ShapeDtypeStruct((pairs, 2, rows, rows), low),
            jax.ShapeDtypeStruct((features, rows), low),
            jax.ShapeDtypeStruct((pairs, 8, rows), full),
        ],
        scratch_shapes=[pltpu.VMEM((2, size + 16, rows), low)],
        compiler_params=params(2),
        name="attend",
    )(projected, projected, projected)


def middle_kernel(
    spans,
    size,
    group,
    side,
    lead,
    x,
    mixed,
    inverse,
    experts,
    upstream,
    embed,
    merge_w,
    merge_b,
    gain,
    shift,
    expand_w,
    expand_b,
    shrink_w,
    shrink_b,
    router_w,
    columns,
    blended,
    d_mid,
    d_across,
    d_down,
    keep,
    send,
    grads,
    lanes,
    sems,
):
    features = x.shape[1]
    step = x.shape[0]
    hidden_size = expand_w.shape[1]
    channels = upstream.shape[0]
    chunk = hidden_size // 2

    @pl.when(pl.program_id(0) == 0)
    def _():
        grads[...] = jnp.zeros_like(grads)
        lanes[...] = jnp.zeros_like(lanes)

    def add(name, values, part=0):
        half, base = spans[name]
        height = values.shape[0]
        for block in range(values.shape[1] // LANES):
            start = base + (part + block) * height
            grads[half, start : start + height, :] += values[
                :, block * LANES : (block + 1) * LANES
            ]

    stream = x[...] + embed[pl.ds(lead[0], 1), :]
    mid = stream + mul(mixed[...], merge_w[...], TN) + merge_b[...][None, :]
    unit, scale = normalize(mid)
    gain_row = gain[...][None, :]
    second = (unit * gain_row + shift[...][None, :]).astype(low)
    output = mid + shrink_b[...][None, :]
    bias = expand_b[...][None, :]
    hidden, slope = [], []
    for start in range(0, hidden_size, chunk):
        part = slice(start, start + chunk)
        u = mul(second, expand_w[:, part]) + bias[:, part]
        square = u * u
        t = jnp.tanh(u * (GELU_COEF + GELU_COEF * GELU_CUBE * square))
        half = 0.5 + 0.5 * t
        act = u * half
        slope.append(
            half
            + act
            * (1.0 - half)
            * (2.0 * GELU_COEF + 6.0 * GELU_COEF * GELU_CUBE * square)
        )
        act = act.astype(low)
        hidden.append(act)
        output = output + mul(act, shrink_w[part, :])
    output_low = output.astype(low)
    logits = mul(router_w[...], output_low, NT) + columns[:, 0:1]
    valid = lax.broadcasted_iota(jnp.int32, (group, 1), 0) < channels
    parts = [logits[e * group : (e + 1) * group, :] for e in range(3)]
    largest = jnp.maximum(jnp.maximum(parts[0], parts[1]), parts[2])
    parts = [part - largest for part in parts]
    raised = [jnp.exp(part) for part in parts]
    total = raised[0] + raised[1] + raised[2]
    shared = jnp.log(total)
    logs = [part - shared for part in parts]
    share = 1.0 / total
    gates = [value * share for value in raised]

    def widen(values):
        return jnp.concatenate(
            [values, jnp.zeros((group - channels, step), full)], axis=0
        )

    frames = [
        widen(experts[e * channels : (e + 1) * channels, :]) for e in range(3)
    ]
    up = widen(upstream[...])
    mix = gates[0] * frames[0] + gates[1] * frames[1] + gates[2] * frames[2]
    entropy = -(gates[0] * logs[0] + gates[1] * logs[1] + gates[2] * logs[2])
    blended[...] = mix[:channels, :] + columns[:channels, 1:2]
    d_parts = [
        jnp.where(
            valid,
            gates[e] * (up * (frames[e] - mix) - PENALTY * (logs[e] + entropy)),
            0.0,
        )
        for e in range(3)
    ]
    for index, values in enumerate(d_parts + [up]):
        for start in range(0, step, LANES):
            lanes[index * group : (index + 1) * group, :] += values[
                :, start : start + LANES
            ]
    d_logits_low = jnp.concatenate(d_parts, axis=0).astype(low)
    add("router", mul(d_logits_low, output_low))
    d_output = mul(d_logits_low, router_w[...], TN)
    add("shrink_bias", column_sum(d_output))
    d_output_low = d_output.astype(low)
    d_turned = d_output_low.T
    second_turned = second.T
    d_second = jnp.zeros_like(d_output)
    for index, start in enumerate(range(0, hidden_size, chunk)):
        part = slice(start, start + chunk)
        d_pre = mul(d_output_low, shrink_w[part, :], NT) * slope[index]
        add("expand_bias", column_sum(d_pre), start // LANES)
        d_pre_low = d_pre.astype(low)
        d_second = d_second + mul(d_pre_low, expand_w[:, part], NT)
        add("expand", mul(second_turned, d_pre_low), start // LANES)
        add("shrink", mul(d_turned, hidden[index]), start // LANES)
    add("second_gain", column_sum(d_second * unit))
    add("second_shift", column_sum(d_second))
    grad_mid = d_output + norm_back(d_second, unit, scale, gain_row)
    d_mid[...] = grad_mid
    add("merge_bias", column_sum(grad_mid))
    d_mid_low = grad_mid.astype(low)
    add("merge", mul(mixed[...], d_mid_low))
    d_mixed = mul(merge_w[...], d_mid_low, NT).astype(low).astype(full)
    row = lax.broadcasted_iota(jnp.int32, (size, step), 0)
    stack = []
    for head in range(features // size):
        span = slice(head * size, (head + 1) * size)
        odd = head % 2
        inv = inverse[head // 2, odd : odd + 1, :]
        scaled = (d_mixed[span, :] * inv).astype(low)
        stack.append(scaled)
        centre = -column_sum(scaled.astype(full) * mixed[span, :].astype(full))
        one = centre.astype(low).astype(full)
        two = (centre - one).astype(low).astype(full)
        extra = jnp.where(
            row == 0,
            one,
            jnp.where(row == 1, two, jnp.where(row == 2, centre - one - two, 0.0)),
        ).astype(low)
        d_across[head, odd * size : (odd + 1) * size, :] = scaled
        d_across[head, (1 - odd) * size : (2 - odd) * size, :] = extra
    d_down[...] = jnp.concatenate(stack, axis=0).T

    @pl.when(pl.program_id(0) == pl.num_programs(0) - 1)
    def _():
        sums = column_sum(lanes[...].T)
        width = sums.shape[1]
        wide = up_to(width, LANES)
        sums = jnp.concatenate([sums, jnp.zeros((1, wide - width), full)], axis=1)
        add("head", sums)
        copies = [
            pltpu.make_async_copy(grads.at[side[0]], keep, sems.at[0]),
            pltpu.make_async_copy(grads.at[1 - side[0]], send, sems.at[1]),
        ]
        for copy in copies:
            copy.start()
        for copy in copies:
            copy.wait()


def middle(spans, height, group, side, lead, x, mixed, inverse, experts, upstream, tables):
    rows, features = x.shape
    size = features // HEADS
    channels = upstream.shape[0]
    step = ROWS
    anywhere = pl.BlockSpec(memory_space=pl.ANY)
    return pl.pallas_call(
        functools.partial(middle_kernel, spans, size, group),
        grid=(rows // step,),
        in_specs=[
            SCALAR,
            SCALAR,
            pl.BlockSpec((step, features), lambda i: (i, 0)),
            pl.BlockSpec((features, step), lambda i: (0, i)),
            pl.BlockSpec((inverse.shape[0], 8, step), lambda i: (0, 0, i)),
            pl.BlockSpec((experts.shape[0], step), lambda i: (0, i)),
            pl.BlockSpec((channels, step), lambda i: (0, i)),
        ]
        + [whole(table.shape) for table in tables],
        out_specs=[
            pl.BlockSpec((channels, step), lambda i: (0, i)),
            pl.BlockSpec((step, features), lambda i: (i, 0)),
            pl.BlockSpec((HEADS, LANES, step), lambda i: (0, 0, i)),
            pl.BlockSpec((step, features), lambda i: (i, 0)),
            anywhere,
            anywhere,
        ],
        out_shape=[
            jax.ShapeDtypeStruct((channels, rows), full),
            jax.ShapeDtypeStruct((rows, features), full),
            jax.ShapeDtypeStruct((HEADS, LANES, rows), low),
            jax.ShapeDtypeStruct((rows, features), low),
            jax.ShapeDtypeStruct((height, LANES), full),
            jax.ShapeDtypeStruct((height, LANES), full),
        ],
        scratch_shapes=[
            pltpu.VMEM((2, height, LANES), full),
            pltpu.VMEM((4 * group, LANES), full),
            pltpu.SemaphoreType.DMA((2,)),
        ],
        compiler_params=params(1),
        name="middle",
    )(side, lead, x, mixed, inverse, experts, upstream, *tables)


def attend_back_kernel(size, pair, base, steps, last_part, token, *refs):
    if base == 0:
        projected, d_across, d_down, probs, d_query, d_pair, total, held, sems = refs
        carry = None
    else:
        projected, d_across, d_down, probs, carry, earlier, *refs = refs
        d_query, d_pair, total, held, sems = refs
        d_pair[:, : base * KEYS, :] = earlier[:, : base * KEYS, :]
    rows = projected.shape[0]
    pairs = projected.shape[1] // (3 * LANES)
    scaling = size ** (-0.5)
    lane = lax.broadcasted_iota(jnp.int32, (1, LANES), 1)

    def fetch(step, slot):
        return pltpu.make_async_copy(
            probs.at[pair, :, pl.ds((base + step) * KEYS, KEYS), :],
            held.at[slot],
            sems.at[slot],
        )

    fetch(0, 0).start()
    total[...] = jnp.zeros_like(total) if carry is None else carry[...]

    def one_step(step, unused):
        slot = lax.rem(step, 2)

        @pl.when(step + 1 < steps)
        def _():
            fetch(step + 1, 1 - slot).start()

        fetch(step, slot).wait()
        at = pl.ds(pl.multiple_of((base + step) * KEYS, KEYS), KEYS)
        k = projected[at, (pairs + pair) * LANES : (pairs + pair + 1) * LANES]
        v = projected[at, (2 * pairs + pair) * LANES : (2 * pairs + pair + 1) * LANES]
        q = projected[:, pair * LANES : (pair + 1) * LANES]
        down = d_down[:, pair * LANES : (pair + 1) * LANES]
        k_across = k.T
        d_keys, d_values = [], []
        for head in range(2):
            other = (1 - head) * size
            data = jnp.where(lane // size == head, 1.0, 0.0).astype(low)
            ones = jnp.where((lane >= other) & (lane < other + 3), 1.0, 0.0)
            values = v * data + ones.astype(low)
            p = held[slot, head]
            d_p = mul(values, d_across[2 * pair + head])
            d_s = (p.astype(full) * d_p).astype(low)
            span = slice(head * size, (head + 1) * size)
            total[span, :] += mul(k_across[span, :], d_s)
            d_values.append(mul(p, down))
            d_keys.append(mul(d_s, q))
        d_pair[0, at, :] = (jnp.where(lane < size, *d_keys) * scaling).astype(low)
        d_pair[1, at, :] = jnp.where(lane < size, *d_values).astype(low)
        return unused

    lax.fori_loop(0, steps, one_step, 0)
    if last_part:
        d_query[...] = (total[...].T * scaling).astype(low)
    else:
        d_query[...] = total[...]


def attend_back(
    pair, base, steps, token, projected, d_across, d_down, probs, carried
):
    rows, wide = projected.shape
    features = wide // 3
    size = features // HEADS
    all_steps = rows // KEYS
    last_part = base + steps == all_steps
    across = (rows, LANES) if last_part else (LANES, rows)
    vmem = pl.BlockSpec(memory_space=pltpu.VMEM)
    return pl.pallas_call(
        functools.partial(attend_back_kernel, size, pair, base, steps, last_part),
        in_specs=[SCALAR, vmem, vmem, vmem, pl.BlockSpec(memory_space=pl.ANY)]
        + [vmem] * len(carried),
        out_specs=[vmem, vmem],
        out_shape=[
            jax.ShapeDtypeStruct(across, low if last_part else full),
            jax.ShapeDtypeStruct((2, rows, LANES), low),
        ],
        scratch_shapes=[
            pltpu.VMEM((LANES, rows), full),
            pltpu.VMEM((2, 2, KEYS, rows), low),
            pltpu.SemaphoreType.DMA((2,)),
        ],
        compiler_params=pltpu.CompilerParams(vmem_limit_bytes=32 * 2**20),
        cost_estimate=pl.CostEstimate(
            flops=10 * rows * rows * 256 * steps // all_steps,
            bytes_accessed=rows * rows * 4 * steps // all_steps,
            transcendentals=0,
        ),
        name="attend_back",
    )(token, projected, d_across, d_down, probs, *carried)


def weigh_kernel(pairs, places, side, weight, first, *refs):
    d_query, d_pair = refs[:pairs], refs[pairs : 2 * pairs]
    keep, send, sums, grads, sems = refs[2 * pairs :]
    features = first.shape[0]
    grads[...] = jnp.zeros_like(grads)
    sums[...] = jnp.zeros_like(sums)
    parts = []
    for kind in range(3):
        for pair in range(pairs):
            values = d_query[pair][...] if kind == 0 else d_pair[pair][kind - 1]
            parts.append(values)
            if kind != 1:
                sums[
                    kind // 2 : kind // 2 + 1, pair * LANES : (pair + 1) * LANES
                ] = weight[0] * column_sum(values.astype(full))
    for start in range(0, len(parts), 2):
        some = parts[start : start + 2]
        product = mul(first[...], jnp.concatenate(some, axis=1)) * weight[0]
        for index in range(len(some)):
            half, base = places[start + index]
            grads[half, base : base + features, :] = product[
                :, index * LANES : (index + 1) * LANES
            ]
    copies = [
        pltpu.make_async_copy(grads.at[side[0]], keep, sems.at[0]),
        pltpu.make_async_copy(grads.at[1 - side[0]], send, sems.at[1]),
    ]
    for copy in copies:
        copy.start()
    for copy in copies:
        copy.wait()


def weigh(places, height, side, weight, first, d_query, d_pair):
    features = first.shape[0]
    vmem = pl.BlockSpec(memory_space=pltpu.VMEM)
    anywhere = pl.BlockSpec(memory_space=pl.ANY)
    pairs = len(d_query)
    return pl.pallas_call(
        functools.partial(weigh_kernel, pairs, places),
        in_specs=[SCALAR, SCALAR, vmem] + [vmem] * (2 * pairs),
        out_specs=[anywhere, anywhere, vmem],
        out_shape=[
            jax.ShapeDtypeStruct((height, LANES), full),
            jax.ShapeDtypeStruct((height, LANES), full),
            jax.ShapeDtypeStruct((8, features), full),
        ],
        scratch_shapes=[
            pltpu.VMEM((2, height, LANES), full),
            pltpu.SemaphoreType.DMA((2,)),
        ],
        compiler_params=pltpu.CompilerParams(vmem_limit_bytes=LIMIT),
        cost_estimate=pl.CostEstimate(
            flops=18 * d_query[0].shape[0] * features * features,
            bytes_accessed=d_query[0].shape[0] * features * 8,
            transcendentals=0,
        ),
        name="weigh",
    )(side, weight, first, *d_query, *d_pair)


def finish_kernel(pairs, last_part, lead, weight, x, embed, gain, wide, d_mid, *rest):
    d_query, d_pair, rest = rest[:pairs], rest[pairs : 2 * pairs], rest[2 * pairs :]
    if last_part:
        earlier, biases, _, grad_input, vectors, sums = rest
    else:
        grad_input, sums = rest
    step = pl.program_id(0)

    @pl.when(step == 0)
    def _():
        sums[...] = earlier[...] if last_part else jnp.zeros_like(sums)

    stream = x[...] + embed[pl.ds(lead[0], 1), :]
    unit, scale = normalize(stream)
    parts = []
    for kind in range(3):
        for pair in range(pairs):
            parts.append(d_query[pair][...] if kind == 0 else d_pair[pair][kind - 1])
    d_first = mul(jnp.concatenate(parts, axis=1), wide[...], NT)
    d_stream = (
        d_mid[...] + norm_back(d_first, unit, scale, gain[...][None, :])
    ) * weight[0]
    grad_input[...] = d_stream
    sums[0:1, :] += column_sum(d_first * unit) * weight[0]
    sums[1:2, :] += column_sum(d_first) * weight[0]
    sums[2:3, :] += column_sum(d_stream)

    if last_part:

        @pl.when(step == pl.num_programs(0) - 1)
        def _():
            vectors[...] = jnp.zeros_like(vectors)
            for index, (ref, at) in enumerate(
                ((sums, 0), (sums, 1), (biases, 0), (biases, 1), (sums, 2))
            ):
                for block in range(pairs):
                    row = index * pairs + block
                    vectors[row : row + 1, :] = ref[
                        at : at + 1, block * LANES : (block + 1) * LANES
                    ]


def finish(base, steps, lead, weight, x, embed, gain, wide, d_mid, d_query, d_pair, carried):
    rows, features = x.shape
    pairs = len(d_query)
    total = rows // ROWS
    last_part = base + steps == total
    height = up_to(5 * pairs, 8)
    row_spec = pl.BlockSpec((ROWS, features), lambda i: (base + i, 0))
    small = pl.BlockSpec((8, features), lambda i: (0, 0))
    return pl.pallas_call(
        functools.partial(finish_kernel, pairs, last_part),
        grid=(steps,),
        in_specs=[
            SCALAR,
            SCALAR,
            row_spec,
            whole(embed.shape),
            whole(gain.shape),
            whole(wide.shape),
            row_spec,
        ]
        + [pl.BlockSpec((ROWS, LANES), lambda i: (base + i, 0))] * pairs
        + [pl.BlockSpec((2, ROWS, LANES), lambda i: (0, base + i, 0))] * pairs
        + ([small, small, pl.BlockSpec(memory_space=pl.ANY)] if last_part else []),
        out_specs=[row_spec, whole((height, LANES)) if last_part else small],
        out_shape=[
            jax.ShapeDtypeStruct((rows, features), full),
            jax.ShapeDtypeStruct((height, LANES) if last_part else (8, features), full),
        ],
        scratch_shapes=[pltpu.VMEM((8, features), full)] if last_part else [],
        input_output_aliases={9 + 2 * pairs: 0} if last_part else {},
        compiler_params=params(1),
        cost_estimate=pl.CostEstimate(
            flops=6 * rows * features * features * steps // total,
            bytes_accessed=rows * features * 18 * steps // total,
            transcendentals=0,
        ),
        name="finish",
    )(lead, weight, x, embed, gain, wide, d_mid, *d_query, *d_pair, *carried)


def unpack_kernel(spans, group, channels, owners, *refs):
    chunks, expand, shrink, merge, router, vectors, grads, sems = refs
    chunk = chunks.shape[1]
    height = len(owners) * chunk // 2
    arrivals = [
        pltpu.make_async_copy(
            chunks.at[owner], grads.at[pl.ds(n * chunk, chunk)], sems.at[n]
        )
        for n, owner in enumerate(owners)
    ]
    for copy in arrivals:
        copy.start()
    for copy in arrivals:
        copy.wait()

    def block(name, rows, index):
        half, base = spans[name]
        start = half * height + base + index * rows
        return grads.at[pl.ds(start, rows)]

    features, hidden = expand.shape
    leaving = []
    for target, name in ((expand, "expand"), (merge, "merge")):
        for index in range(target.shape[1] // LANES):
            leaving.append(
                pltpu.make_async_copy(
                    block(name, features, index),
                    target.at[:, pl.ds(index * LANES, LANES)],
                    sems.at[len(owners) + len(leaving)],
                )
            )
    for copy in leaving:
        copy.start()
    for index in range(hidden // LANES):
        shrink[index * LANES : (index + 1) * LANES, :] = block("shrink", features, index)[
            ...
        ].T
    rows = 3 * group
    for index in range(features // LANES):
        values = block("router", rows, index)
        for e in range(3):
            router[
                e * channels : (e + 1) * channels, index * LANES : (index + 1) * LANES
            ] = values[e * group : e * group + channels, :]
    vectors[...] = block("expand_bias", vectors.shape[0], 0)[...]
    for copy in leaving:
        copy.wait()


def unpack(spans, group, channels, owners, features, hidden, tall, chunks):
    vmem = pl.BlockSpec(memory_space=pltpu.VMEM)
    anywhere = pl.BlockSpec(memory_space=pl.ANY)
    height = len(owners) * chunks.shape[1]
    return pl.pallas_call(
        functools.partial(unpack_kernel, spans, group, channels, owners),
        in_specs=[anywhere],
        out_specs=[anywhere, vmem, anywhere, vmem, vmem],
        out_shape=[
            jax.ShapeDtypeStruct((features, hidden), full),
            jax.ShapeDtypeStruct((hidden, features), full),
            jax.ShapeDtypeStruct((features, features), full),
            jax.ShapeDtypeStruct((3 * channels, features), full),
            jax.ShapeDtypeStruct((tall, LANES), full),
        ],
        scratch_shapes=[
            pltpu.VMEM((height, LANES), full),
            pltpu.SemaphoreType.DMA((len(owners) + (hidden + features) // LANES,)),
        ],
        compiler_params=pltpu.CompilerParams(vmem_limit_bytes=LIMIT),
        cost_estimate=pl.CostEstimate(
            flops=8 * 10**9, bytes_accessed=height * 1024, transcendentals=0
        ),
        name="unpack",
    )(chunks)


def join_kernel(hop, sides, mine, got, out, sems):
    height = mine.shape[0]
    copies = []
    for index, (rows, at) in enumerate(
        ((mine, sides[hop]), (got, 1 - sides[hop]))
    ):
        start = pl.multiple_of(at * height, 8)
        copies.append(
            pltpu.make_async_copy(rows, out.at[pl.ds(start, height)], sems.at[index])
        )
    for copy in copies:
        copy.start()
    for copy in copies:
        copy.wait()


def join(hop, sides, mine, got):
    anywhere = pl.BlockSpec(memory_space=pl.ANY)
    return pl.pallas_call(
        functools.partial(join_kernel, hop),
        in_specs=[SCALAR, anywhere, anywhere],
        out_specs=anywhere,
        out_shape=jax.ShapeDtypeStruct((2 * mine.shape[0], LANES), full),
        scratch_shapes=[pltpu.SemaphoreType.DMA((2,))],
        compiler_params=pltpu.CompilerParams(vmem_limit_bytes=2**20),
        name="join",
    )(sides, mine, got)


def settle_kernel(
    places,
    owners,
    chunk,
    extra,
    side,
    leads,
    mine,
    got,
    attend,
    embed,
    vectors,
    held,
    table,
    sems,
):
    features = attend.shape[0]
    pairs = features // LANES
    arrivals = [
        pltpu.make_async_copy(mine, held.at[side[0]], sems.at[0]),
        pltpu.make_async_copy(got, held.at[1 - side[0]], sems.at[1]),
    ]
    for copy in arrivals:
        copy.start()
    table[...] = jnp.zeros_like(table)
    for copy in arrivals:
        copy.wait()
    stride = chunk + extra
    count = mine.shape[0] // stride
    leaving = []
    for index, (half, base) in enumerate(places):
        done = 0
        while done < features:
            at = base + done
            inside = at % chunk
            size = min(features - done, chunk - inside)
            leaving.append(
                pltpu.make_async_copy(
                    held.at[half, pl.ds(at // chunk * stride + inside, size)],
                    attend.at[pl.ds(done, size), pl.ds(index * LANES, LANES)],
                    sems.at[2 + len(leaving)],
                )
            )
            done += size
    for copy in leaving:
        copy.start()
    total = jnp.zeros((extra, LANES), full)
    row = lax.broadcasted_iota(jnp.int32, (table.shape[1], LANES), 0).astype(full)
    for half in range(2):
        for n in range(count):
            rows = held[half, n * stride + chunk : (n + 1) * stride, :]
            total = total + rows
            owner = owners[half * count + n]
            here = row == leads[owner : owner + 1, :]
            for block in range(pairs):
                at = 4 * pairs + block
                table[block] += jnp.where(here, rows[at : at + 1, :], 0.0)
    vectors[...] = total
    for block in range(pairs):
        embed[:, block * LANES : (block + 1) * LANES] = table[block]
    for copy in leaving:
        copy.wait()


def settle(places, owners, chunk, extra, leads, features, side, seen, mine, got):
    vmem = pl.BlockSpec(memory_space=pltpu.VMEM)
    anywhere = pl.BlockSpec(memory_space=pl.ANY)
    moves = 0
    for _, base in places:
        moves += (base + features - 1) // chunk - base // chunk + 1
    return pl.pallas_call(
        functools.partial(settle_kernel, places, owners, chunk, extra),
        in_specs=[SCALAR, vmem, anywhere, anywhere],
        out_specs=[anywhere, vmem, vmem],
        out_shape=[
            jax.ShapeDtypeStruct((features, 3 * features), full),
            jax.ShapeDtypeStruct((leads, features), full),
            jax.ShapeDtypeStruct((extra, LANES), full),
        ],
        scratch_shapes=[
            pltpu.VMEM((2, mine.shape[0], LANES), full),
            pltpu.VMEM((features // LANES, leads, LANES), full),
            pltpu.SemaphoreType.DMA((2 + moves,)),
        ],
        compiler_params=pltpu.CompilerParams(vmem_limit_bytes=32 * 2**20),
        name="settle",
    )(side, seen, mine, got)


def fold_kernel(count, sides, factors, *refs):
    total = refs[0][...] * factors[0]
    for index in range(1, count):
        total = total + refs[index][...] * factors[min(index, 2)]
    refs[count][...] = total


def fold(hop, hops, sides, factors, unit, terms):
    def spec(made):
        def index(i, sides, factors):
            at = i
            for step in range(made + 1, hop):
                at = at + sides[step] * 2 ** (hops - 1 - step)
            if hop < hops:
                at = at + (1 - sides[hop]) * 2 ** (hops - 1 - hop)
            return at, 0

        return pl.BlockSpec((unit, LANES), index)

    length = 2 ** (hops - 1 - hop) if hop < hops else 1
    return pl.pallas_call(
        functools.partial(fold_kernel, len(terms)),
        grid_spec=pltpu.PrefetchScalarGridSpec(
            num_scalar_prefetch=2,
            grid=(length,),
            in_specs=[spec(max(index - 1, 0)) for index in range(len(terms))],
            out_specs=pl.BlockSpec((unit, LANES), lambda i, *tables: (i, 0)),
        ),
        out_shape=jax.ShapeDtypeStruct((length * unit, LANES), full),
        compiler_params=pltpu.CompilerParams(
            dimension_semantics=("arbitrary",), vmem_limit_bytes=8 * 2**20
        ),
        name="fold",
    )(sides, factors, *terms)


def weights_kernel(index, frames, seen, weights, leads, held, sem):
    copy = pltpu.make_async_copy(seen.at[:, pl.ds(0, 8), :], held, sem)
    copy.start()
    total = lax.fori_loop(
        0, frames.shape[0], lambda n, sofar: sofar + frames[n], jnp.int32(0)
    ).astype(full)
    copy.wait()
    count = held.shape[0]
    rows = held[:, 0, :]
    leads[...] = rows
    device = lax.broadcasted_iota(jnp.int32, rows.shape, 0)
    for side in range(2):
        lead = jnp.max(jnp.where(device == index[side], rows, 0.0))
        same = jnp.sum(jnp.where(rows == lead, 1.0, 0.0)) / LANES
        chosen = frames[lead.astype(jnp.int32)].astype(full)
        weights[side] = chosen * count / (same * total)
    weights[2] = jnp.float32(1.0)


def weights_of(index, frames, seen):
    count = seen.shape[0]
    smem = pl.BlockSpec(memory_space=pltpu.SMEM)
    return pl.pallas_call(
        weights_kernel,
        in_specs=[smem, smem, pl.BlockSpec(memory_space=pl.ANY)],
        out_specs=[smem, pl.BlockSpec(memory_space=pltpu.VMEM)],
        out_shape=[
            jax.ShapeDtypeStruct((3,), full),
            jax.ShapeDtypeStruct((count, LANES), full),
        ],
        scratch_shapes=[
            pltpu.VMEM((count, 8, LANES), full),
            pltpu.SemaphoreType.DMA,
        ],
        compiler_params=pltpu.CompilerParams(vmem_limit_bytes=8 * 2**20),
        name="weights",
    )(index, frames, seen)


def up_to(value, step):
    return -(-value // step) * step


def tie(value, *others):
    return lax.optimization_barrier((value,) + others)[0]


def routes(sizes):
    inner = sizes["rep"]
    outer = sizes["dp"]
    if outer % 2:
        return 0, ((), ())
    far = [inner << n for n in range(1, outer.bit_length() - 1)]
    near = [1 << n for n in range(inner.bit_length() - 1)]
    even = []
    for n in range(max(len(far), len(near))):
        even += far[n : n + 1] + near[n : n + 1]
    odd = even[1:3] + even[:1] + even[3:]
    return inner, (tuple(even), tuple(odd))


class Ring:
    def __init__(self, sizes):
        self.count = sizes["dp"] * sizes["rep"]
        self.core_bit, self.orders = routes(sizes)
        self.hops = len(self.orders[0]) + 1 if self.core_bit else 0
        self.index = lax.axis_index(("dp", "rep"))

    def bits(self, hop):
        if hop == 0:
            return self.core_bit, self.core_bit
        return self.orders[0][hop - 1], self.orders[1][hop - 1]

    def swap(self, values, hop):
        pair = self.bits(hop)
        moves = [
            (i, i ^ pair[(i // self.core_bit) % 2]) for i in range(self.count)
        ]
        return lax.ppermute(values, ("dp", "rep"), moves)

    def sides(self):
        if not self.hops:
            return jnp.zeros((1,), jnp.int32)
        even, odd = (
            jnp.array((self.core_bit,) + order, jnp.int32) for order in self.orders
        )
        bits = jnp.where(self.index & self.core_bit == 0, even, odd)
        return jnp.where(self.index & bits == 0, 0, 1).astype(jnp.int32)

    def scatter(self, sides, factors, keep, send):
        unit = keep.shape[0] >> (self.hops - 1)
        terms = [keep]
        for hop in range(self.hops):
            if hop:
                send = fold(hop, self.hops, sides, factors, unit, terms)
            got = self.swap(send, hop)
            beside = yield send
            terms.append(got if beside is None else tie(got, beside))
        return fold(self.hops, self.hops, sides, factors, unit, terms)

    def owners(self):
        found = [0] * self.count
        for device in range(self.count):
            core = (device // self.core_bit) % 2
            chunk = 0
            for hop in range(self.hops):
                chunk = 2 * chunk + (1 if device & self.bits(hop)[core] else 0)
            found[chunk] = device
        return tuple(found)


class Flow:
    def __init__(self, steps):
        self.steps = steps
        self.done = False
        self.sent = None
        self.result = None
        self.push(None)

    def push(self, beside):
        if self.done:
            return
        try:
            self.sent = self.steps.send(beside)
        except StopIteration as stop:
            self.done, self.sent, self.result = True, None, stop.value

    def drain(self):
        while not self.done:
            self.push(None)
        return self.result


def body(sizes, *args):
    (
        block_input,
        expert_out,
        upstream,
        lead_index,
        lead_frames,
        lead_embed,
        first_gain,
        first_shift,
        attend_weight,
        query_bias,
        value_bias,
        merge_weight,
        merge_bias,
        second_gain,
        second_shift,
        expand_weight,
        expand_bias,
        shrink_weight,
        shrink_bias,
        router_weight,
        router_bias,
        correction,
    ) = args
    rows, features = block_input.shape
    channels = correction.shape[0]
    leads = lead_embed.shape[0]
    hidden = expand_bias.shape[0]
    devices = sizes["dp"] * sizes["rep"]
    pairs = features // LANES
    grain = 4 * devices
    ring = Ring(sizes)
    sides = ring.sides()

    tall = max(8, 2048 // devices)
    mine = lead_index[0].astype(full)
    seen = lax.optimization_barrier(
        lax.all_gather(
            lax.optimization_barrier(jnp.full((tall, LANES), mine)), ("dp", "rep")
        )
    )
    weight, leads_seen = weights_of(
        jnp.stack([ring.index, ring.index ^ ring.core_bit]).astype(jnp.int32),
        lead_frames,
        seen,
    )

    first, projected = project(
        lead_index,
        block_input,
        lead_embed,
        first_gain,
        first_shift,
        attend_weight,
        query_bias,
        value_bias,
    )
    probs, mixed, inverse = attend(projected)

    group = up_to(channels, 16)
    spans, heights = {}, [0, 0]
    for name, half, height in (
        ("expand", 0, features * hidden // LANES),
        ("merge", 0, features * features // LANES),
        ("shrink", 1, features * hidden // LANES),
        ("router", 1, features * 3 * group // LANES),
        ("expand_bias", 1, hidden // LANES),
        ("shrink_bias", 1, pairs),
        ("merge_bias", 1, pairs),
        ("second_gain", 1, pairs),
        ("second_shift", 1, pairs),
        ("head", 1, up_to(4 * group, LANES) // LANES),
    ):
        spans[name] = (half, heights[half])
        heights[half] += height
    vector_rows = up_to(heights[1] - spans["expand_bias"][1], 8)
    height = up_to(max(heights[0], spans["expand_bias"][1] + vector_rows), grain)
    wide_router = jnp.pad(
        router_weight.T.reshape(3, channels, features),
        ((0, 0), (0, group - channels), (0, 0)),
    ).reshape(3 * group, features)
    columns = jnp.stack(
        [
            jnp.pad(
                router_bias.reshape(3, channels), ((0, 0), (0, group - channels))
            ).reshape(-1),
            jnp.pad(correction, (0, 3 * group - channels)),
        ],
        axis=1,
    )
    tables = (
        lead_embed,
        merge_weight,
        merge_bias,
        second_gain,
        second_shift,
        expand_weight,
        expand_bias,
        shrink_weight,
        shrink_bias,
        wide_router,
        columns,
    )
    blended, d_mid, d_across, d_down, keep, send = middle(
        spans,
        height,
        group,
        sides,
        lead_index,
        block_input,
        mixed,
        inverse,
        expert_out.T,
        upstream.T,
        tables,
    )
    flow = None
    if ring.hops:
        flow = Flow(ring.scatter(sides, weight, keep, tie(send, seen)))
    plan = ((1, 3), (2, 1, 1), (4,))
    d_query, d_pair = [], []
    for pair in range(pairs):
        carried = ()
        base = 0
        for steps in plan[pair]:
            token = sides if flow is None or flow.done else tie(sides, flow.sent)
            carried = attend_back(
                pair, base, steps, token, projected, d_across, d_down, probs, carried
            )
            base += steps
            if flow is not None:
                flow.push(carried[0])
        d_query.append(carried[0])
        d_pair.append(carried[1])
    places = tuple(
        (n // 5, (n % 5) * features) for n in range(3 * pairs)
    )
    tail_height = up_to(5 * features, grain)
    now = weight if flow is None else tie(weight, flow.drain())
    tail_keep, tail_send, biases = weigh(
        places, tail_height, sides, now, first, d_query, d_pair
    )
    late = None
    if ring.hops:
        ones = jnp.ones((3,), full)
        late = Flow(ring.scatter(sides, ones, tail_keep, tail_send))
    carried = ()
    base = 0
    for steps in (2, 2):
        now = weight if late is None else tie(weight, late.sent)
        grad_input, sums = finish(
            base,
            steps,
            lead_index,
            now,
            block_input,
            lead_embed,
            first_gain,
            attend_weight,
            d_mid,
            d_query,
            d_pair,
            carried,
        )
        base += steps
        carried = (sums, biases, grad_input)
        if late is not None:
            late.push(sums)
    extra = sums.shape[0]
    if ring.hops:
        owners = ring.owners()
        chunks = lax.all_gather(flow.result, ("dp", "rep"))
        piece = jnp.concatenate([late.drain(), sums])
        for hop in reversed(range(1, ring.hops)):
            got = ring.swap(piece, hop)
            if hop == 1:
                chunks = tie(chunks, piece)
            piece = join(hop, sides, piece, got)
        got = ring.swap(piece, 0)
        chunk = 2 * tail_height // devices
    else:
        owners = (0, 1)
        chunks = jnp.stack([keep, send]) * weight[0]
        chunk = tail_height
        piece = jnp.concatenate([tail_keep, sums])
        got = jnp.concatenate([tail_send, jnp.zeros_like(sums)])
        leads_seen = jnp.concatenate([leads_seen, leads_seen + leads])
    grad_expand, grad_shrink, grad_merge, grad_router, vectors = unpack(
        spans, group, channels, owners, features, hidden, vector_rows, chunks
    )
    first_vector = spans["expand_bias"][1]

    def take(name, length):
        start = spans[name][1] - first_vector
        return vectors[start : start + length // LANES].reshape(-1)

    head = take("head", up_to(4 * group, LANES))
    middle_vectors = (
        take("merge_bias", features),
        take("second_gain", features),
        take("second_shift", features),
        take("expand_bias", hidden),
        take("shrink_bias", features),
        head[: 3 * group].reshape(3, group)[:, :channels].reshape(-1),
        head[3 * group : 3 * group + channels],
    )
    if ring.hops:
        got = tie(got, vectors)
    grad_attend, grad_embed, small = settle(
        places,
        owners,
        chunk,
        extra,
        leads,
        features,
        sides,
        leads_seen,
        piece,
        got,
    )
    small = small[: 4 * pairs].reshape(4, features)
    merge_b, gain_b, shift_b, expand_b, shrink_b, router_b, correct = middle_vectors
    return (
        blended.T,
        grad_input,
        grad_embed,
        small[0],
        small[1],
        grad_attend,
        small[2],
        small[3],
        grad_merge,
        merge_b,
        gain_b,
        shift_b,
        grad_expand,
        expand_b,
        grad_shrink,
        shrink_b,
        grad_router.T,
        router_b,
        correct,
    )


def solution(mesh):
    split = P(("dp", "rep"), None)
    sizes = dict(mesh.shape)
    return jax.shard_map(
        functools.partial(body, sizes),
        mesh=mesh,
        in_specs=(split, split, split, P(("dp", "rep"))) + (P(),) * 18,
        out_specs=(split, split) + (P(),) * 17,
        check_vma=False,
    )
```

```python
import functools

import jax
import jax.numpy as jnp
from jax import lax
from jax.experimental import pallas as pl
from jax.experimental.pallas import tpu as pltpu
from jax.sharding import PartitionSpec as P

HEADS = 6
EPSILON = 1e-05
PENALTY = 1.0
GELU_COEF = 0.7978845608028654
GELU_CUBE = 0.044715
LOG2E = 1.4426950408889634
LANES = 128
ROWS = 512
KEYS = 512
LIMIT = 56 * 2**20

low = jnp.bfloat16
full = jnp.float32


def mul(left, right, dims=((1,), (0,))):
    return lax.dot_general(left, right, (dims, ((), ())), preferred_element_type=full)


NT = ((1,), (1,))
TN = ((0,), (0,))


def params(count):
    return pltpu.CompilerParams(
        dimension_semantics=("arbitrary",) * count, vmem_limit_bytes=LIMIT
    )


def whole(shape):
    return pl.BlockSpec(shape, lambda *step: (0,) * len(shape))


SCALAR = pl.BlockSpec(memory_space=pltpu.SMEM)


def normalize(values):
    centre = jnp.mean(values, axis=-1, keepdims=True)
    centred = values - centre
    spread = jnp.mean(centred * centred, axis=-1, keepdims=True)
    scale = lax.rsqrt(spread + EPSILON)
    return centred * scale, scale


def norm_back(grad, unit, scale, gain):
    e = grad * gain
    first = jnp.mean(e, axis=-1, keepdims=True)
    second = jnp.mean(e * unit, axis=-1, keepdims=True)
    return scale * (e - first - unit * second)


def column_sum(values):
    return jnp.sum(values, axis=0, keepdims=True)


def project_kernel(
    lead, x, embed, gain, shift, weight, query_b, value_b, first, projected, *own
):
    stream = x[...] + embed[pl.ds(lead[0], 1), :]
    unit, _ = normalize(stream)
    rounded = (unit * gain[...][None, :] + shift[...][None, :]).astype(low)
    first[...] = rounded.T
    features = x.shape[1]
    query_row = query_b[...][None, :]
    bias = jnp.concatenate(
        [query_row, jnp.zeros_like(query_row), value_b[...][None, :]], axis=1
    )
    product = (mul(rounded, weight[...]) + bias).astype(low)
    pairs = projected.shape[0]
    for pair in range(pairs):
        for kind in range(3):
            block = kind * pairs + pair
            values = product[:, block * LANES : (block + 1) * LANES]
            projected[pair, kind] = values
            own[pair][kind] = values


def project(lead, x, embed, gain, shift, weight, query_b, value_b):
    rows, features = x.shape
    tables = (embed, gain, shift, weight, query_b, value_b)
    return pl.pallas_call(
        project_kernel,
        grid=(rows // ROWS,),
        in_specs=[SCALAR, pl.BlockSpec((ROWS, features), lambda i: (i, 0))]
        + [whole(table.shape) for table in tables],
        out_specs=[
            pl.BlockSpec((features, ROWS), lambda i: (0, i)),
            pl.BlockSpec((features // LANES, 3, ROWS, LANES), lambda i: (0, 0, i, 0)),
        ]
        + [pl.BlockSpec((3, ROWS, LANES), lambda i: (0, i, 0))] * (features // LANES),
        out_shape=[
            jax.ShapeDtypeStruct((features, rows), low),
            jax.ShapeDtypeStruct((features // LANES, 3, rows, LANES), low),
        ]
        + [jax.ShapeDtypeStruct((3, rows, LANES), low)] * (features // LANES),
        compiler_params=params(1),
        name="project",
    )(lead, x, *tables)


def attend_kernel(size, q, k, v, probs, mixed, inverse, turned):
    keys = k.shape[2]
    count = q.shape[2]
    scaling = size ** (-0.5) * LOG2E

    @pl.when(pl.program_id(1) == 0)
    def _():
        across = v[0, 0].T
        tail = lax.broadcasted_iota(jnp.int32, (16, keys), 0)
        ones = jnp.where(tail == 0, 1.0, 0.0).astype(low)
        for head in range(2):
            turned[head, 0:size, :] = across[head * size : (head + 1) * size, :]
            turned[head, size : size + 16, :] = ones

    lane = lax.broadcasted_iota(jnp.int32, (1, LANES), 1)

    def scores(head, start):
        mask = jnp.where(lane // size == head, 1.0, 0.0).astype(low)
        return mul(k[0, 0, start : start + keys, :], q[0, 0] * mask, NT) * scaling

    def finish(head, total):
        spread = total[size : size + 1, :]
        inv = 1.0 / spread
        inverse[0, head : head + 1, :] = inv
        mixed[head * size : (head + 1) * size, :] = (total[0:size, :] * inv).astype(low)
        return spread

    extremes = []
    for head in range(2):
        total = jnp.zeros((size + 16, count), full)
        for start in (0,):
            p = jnp.exp2(scores(head, start)).astype(low)
            probs[0, head, start : start + keys, :] = p
            total = total + mul(turned[head, :, start : start + keys], p)
        spread = finish(head, total)
        extremes.append(spread)

    both = jnp.concatenate(extremes, axis=0)
    inside = jnp.where((both > 1e-18) & (both < 1e18), 1.0, 0.0)

    @pl.when(jnp.min(inside) < 0.5)
    def _():
        for head in range(2):
            top = jnp.full((1, count), -jnp.inf, full)
            for start in (0,):
                top = jnp.maximum(
                    top, jnp.max(scores(head, start), axis=0, keepdims=True)
                )
            total = jnp.zeros((size + 16, count), full)
            for start in (0,):
                p = jnp.exp2(scores(head, start) - top).astype(low)
                probs[0, head, start : start + keys, :] = p
                total = total + mul(turned[head, :, start : start + keys], p)
            finish(head, total)


def attend(projected):
    pairs, _, rows, _ = projected.shape
    features = pairs * LANES
    size = features // HEADS
    return pl.pallas_call(
        functools.partial(attend_kernel, size),
        grid=(pairs, rows // ROWS),
        in_specs=[
            pl.BlockSpec((1, 1, ROWS, LANES), lambda p, i: (p, 0, i, 0)),
            pl.BlockSpec((1, 1, rows, LANES), lambda p, i: (p, 1, 0, 0)),
            pl.BlockSpec((1, 1, rows, LANES), lambda p, i: (p, 2, 0, 0)),
        ],
        out_specs=[
            pl.BlockSpec((1, 2, rows, ROWS), lambda p, i: (p, 0, 0, i)),
            pl.BlockSpec((LANES, ROWS), lambda p, i: (p, i)),
            pl.BlockSpec((1, 8, ROWS), lambda p, i: (p, 0, i)),
        ],
        out_shape=[
            jax.ShapeDtypeStruct((pairs, 2, rows, rows), low),
            jax.ShapeDtypeStruct((features, rows), low),
            jax.ShapeDtypeStruct((pairs, 8, rows), full),
        ],
        scratch_shapes=[pltpu.VMEM((2, size + 16, rows), low)],
        compiler_params=params(2),
        name="attend",
    )(projected, projected, projected)


def middle_kernel(
    spans,
    size,
    group,
    side,
    lead,
    x,
    mixed,
    inverse,
    experts,
    upstream,
    embed,
    merge_w,
    merge_b,
    gain,
    shift,
    expand_w,
    expand_b,
    shrink_w,
    shrink_b,
    router_w,
    columns,
    blended,
    d_mid,
    *rest,
):
    pairs = x.shape[1] // LANES
    d_across, d_down = rest[:pairs], rest[pairs : 2 * pairs]
    keep, send, grads, lanes, sems = rest[2 * pairs :]
    features = x.shape[1]
    step = x.shape[0]
    hidden_size = expand_w.shape[1]
    channels = upstream.shape[0]
    chunk = hidden_size // 2

    @pl.when(pl.program_id(0) == 0)
    def _():
        grads[...] = jnp.zeros_like(grads)
        lanes[...] = jnp.zeros_like(lanes)

    def add(name, values, part=0):
        half, base = spans[name]
        height = values.shape[0]
        for block in range(values.shape[1] // LANES):
            start = base + (part + block) * height
            grads[half, start : start + height, :] += values[
                :, block * LANES : (block + 1) * LANES
            ]

    stream = x[...] + embed[pl.ds(lead[0], 1), :]
    mid = stream + mul(mixed[...], merge_w[...], TN) + merge_b[...][None, :]
    unit, scale = normalize(mid)
    gain_row = gain[...][None, :]
    second = (unit * gain_row + shift[...][None, :]).astype(low)
    output = mid + shrink_b[...][None, :]
    bias = expand_b[...][None, :]
    hidden, slope = [], []
    for start in range(0, hidden_size, chunk):
        part = slice(start, start + chunk)
        u = mul(second, expand_w[:, part]) + bias[:, part]
        square = u * u
        t = jnp.tanh(u * (GELU_COEF + GELU_COEF * GELU_CUBE * square))
        half = 0.5 + 0.5 * t
        act = u * half
        slope.append(
            half
            + act
            * (1.0 - half)
            * (2.0 * GELU_COEF + 6.0 * GELU_COEF * GELU_CUBE * square)
        )
        act = act.astype(low)
        hidden.append(act)
        output = output + mul(act, shrink_w[part, :])
    output_low = output.astype(low)
    logits = mul(router_w[...], output_low, NT) + columns[:, 0:1]
    valid = lax.broadcasted_iota(jnp.int32, (group, 1), 0) < channels
    parts = [logits[e * group : (e + 1) * group, :] for e in range(3)]
    largest = jnp.maximum(jnp.maximum(parts[0], parts[1]), parts[2])
    parts = [part - largest for part in parts]
    raised = [jnp.exp(part) for part in parts]
    total = raised[0] + raised[1] + raised[2]
    shared = jnp.log(total)
    logs = [part - shared for part in parts]
    share = 1.0 / total
    gates = [value * share for value in raised]

    def widen(values):
        return jnp.concatenate(
            [values, jnp.zeros((group - channels, step), full)], axis=0
        )

    frames = [
        widen(experts[e * channels : (e + 1) * channels, :]) for e in range(3)
    ]
    up = widen(upstream[...])
    mix = gates[0] * frames[0] + gates[1] * frames[1] + gates[2] * frames[2]
    entropy = -(gates[0] * logs[0] + gates[1] * logs[1] + gates[2] * logs[2])
    blended[...] = mix[:channels, :] + columns[:channels, 1:2]
    d_parts = [
        jnp.where(
            valid,
            gates[e] * (up * (frames[e] - mix) - PENALTY * (logs[e] + entropy)),
            0.0,
        )
        for e in range(3)
    ]
    for index, values in enumerate(d_parts + [up]):
        for start in range(0, step, LANES):
            lanes[index * group : (index + 1) * group, :] += values[
                :, start : start + LANES
            ]
    d_logits_low = jnp.concatenate(d_parts, axis=0).astype(low)
    add("router", mul(d_logits_low, output_low))
    d_output = mul(d_logits_low, router_w[...], TN)
    add("shrink_bias", column_sum(d_output))
    d_output_low = d_output.astype(low)
    d_turned = d_output_low.T
    second_turned = second.T
    d_second = jnp.zeros_like(d_output)
    for index, start in enumerate(range(0, hidden_size, chunk)):
        part = slice(start, start + chunk)
        d_pre = mul(d_output_low, shrink_w[part, :], NT) * slope[index]
        add("expand_bias", column_sum(d_pre), start // LANES)
        d_pre_low = d_pre.astype(low)
        d_second = d_second + mul(d_pre_low, expand_w[:, part], NT)
        add("expand", mul(second_turned, d_pre_low), start // LANES)
        add("shrink", mul(d_turned, hidden[index]), start // LANES)
    add("second_gain", column_sum(d_second * unit))
    add("second_shift", column_sum(d_second))
    grad_mid = d_output + norm_back(d_second, unit, scale, gain_row)
    d_mid[...] = grad_mid
    add("merge_bias", column_sum(grad_mid))
    d_mid_low = grad_mid.astype(low)
    add("merge", mul(mixed[...], d_mid_low))
    d_mixed = mul(merge_w[...], d_mid_low, NT).astype(low).astype(full)
    row = lax.broadcasted_iota(jnp.int32, (size, step), 0)
    stack = []
    for head in range(features // size):
        span = slice(head * size, (head + 1) * size)
        odd = head % 2
        inv = inverse[head // 2, odd : odd + 1, :]
        scaled = (d_mixed[span, :] * inv).astype(low)
        stack.append(scaled)
        centre = -column_sum(scaled.astype(full) * mixed[span, :].astype(full))
        one = centre.astype(low).astype(full)
        two = (centre - one).astype(low).astype(full)
        extra = jnp.where(
            row == 0,
            one,
            jnp.where(row == 1, two, jnp.where(row == 2, centre - one - two, 0.0)),
        ).astype(low)
        across = d_across[head // 2]
        across[odd, odd * size : (odd + 1) * size, :] = scaled
        across[odd, (1 - odd) * size : (2 - odd) * size, :] = extra
    for pair in range(pairs):
        d_down[pair][...] = jnp.concatenate(stack[2 * pair : 2 * pair + 2], axis=0).T

    @pl.when(pl.program_id(0) == pl.num_programs(0) - 1)
    def _():
        sums = column_sum(lanes[...].T)
        width = sums.shape[1]
        wide = up_to(width, LANES)
        sums = jnp.concatenate([sums, jnp.zeros((1, wide - width), full)], axis=1)
        add("head", sums)
        copies = [
            pltpu.make_async_copy(grads.at[side[0]], keep, sems.at[0]),
            pltpu.make_async_copy(grads.at[1 - side[0]], send, sems.at[1]),
        ]
        for copy in copies:
            copy.start()
        for copy in copies:
            copy.wait()


def middle(spans, height, group, side, lead, x, mixed, inverse, experts, upstream, tables):
    rows, features = x.shape
    size = features // HEADS
    channels = upstream.shape[0]
    step = ROWS
    pairs = features // LANES
    anywhere = pl.BlockSpec(memory_space=pl.ANY)
    return pl.pallas_call(
        functools.partial(middle_kernel, spans, size, group),
        grid=(rows // step,),
        in_specs=[
            SCALAR,
            SCALAR,
            pl.BlockSpec((step, features), lambda i: (i, 0)),
            pl.BlockSpec((features, step), lambda i: (0, i)),
            pl.BlockSpec((inverse.shape[0], 8, step), lambda i: (0, 0, i)),
            pl.BlockSpec((experts.shape[0], step), lambda i: (0, i)),
            pl.BlockSpec((channels, step), lambda i: (0, i)),
        ]
        + [whole(table.shape) for table in tables],
        out_specs=[
            pl.BlockSpec((channels, step), lambda i: (0, i)),
            pl.BlockSpec((step, features), lambda i: (i, 0)),
        ]
        + [pl.BlockSpec((2, LANES, step), lambda i: (0, 0, i))] * pairs
        + [pl.BlockSpec((step, LANES), lambda i: (i, 0))] * pairs
        + [anywhere, anywhere],
        out_shape=[
            jax.ShapeDtypeStruct((channels, rows), full),
            jax.ShapeDtypeStruct((rows, features), full),
        ]
        + [jax.ShapeDtypeStruct((2, LANES, rows), low)] * pairs
        + [jax.ShapeDtypeStruct((rows, LANES), low)] * pairs
        + [jax.ShapeDtypeStruct((height, LANES), full)] * 2,
        scratch_shapes=[
            pltpu.VMEM((2, height, LANES), full),
            pltpu.VMEM((4 * group, LANES), full),
            pltpu.SemaphoreType.DMA((2,)),
        ],
        compiler_params=params(1),
        name="middle",
    )(side, lead, x, mixed, inverse, experts, upstream, *tables)


def attend_back_kernel(size, pair, base, steps, last_part, token, *refs):
    if base == 0:
        projected, d_across, d_down, probs, d_query, d_pair, total, held, sems = refs
        carry = None
    else:
        projected, d_across, d_down, probs, carry, earlier, *refs = refs
        d_query, d_pair, total, held, sems = refs
        d_pair[:, : base * KEYS, :] = earlier[:, : base * KEYS, :]
    rows = d_down.shape[0]
    scaling = size ** (-0.5)
    lane = lax.broadcasted_iota(jnp.int32, (1, LANES), 1)

    def fetch(step, slot):
        return pltpu.make_async_copy(
            probs.at[pair, :, pl.ds((base + step) * KEYS, KEYS), :],
            held.at[slot],
            sems.at[slot],
        )

    fetch(0, 0).start()
    total[...] = jnp.zeros_like(total) if carry is None else carry[...]

    def one_step(step, unused):
        slot = lax.rem(step, 2)

        @pl.when(step + 1 < steps)
        def _():
            fetch(step + 1, 1 - slot).start()

        fetch(step, slot).wait()
        at = pl.ds(pl.multiple_of((base + step) * KEYS, KEYS), KEYS)
        v = projected[2, at, :]
        k_across = projected[1, at, :].T
        d_keys, d_values = [], []
        for head in range(2):
            other = (1 - head) * size
            data = jnp.where(lane // size == head, 1.0, 0.0).astype(low)
            ones = jnp.where((lane >= other) & (lane < other + 3), 1.0, 0.0)
            values = v * data + ones.astype(low)
            p = held[slot, head]
            d_p = mul(values, d_across[head])
            d_s = (p.astype(full) * d_p).astype(low)
            span = slice(head * size, (head + 1) * size)
            total[span, :] += mul(k_across[span, :], d_s)
            d_values.append(mul(p, d_down[...]))
            d_keys.append(mul(d_s, projected[0]))
        d_pair[0, at, :] = (jnp.where(lane < size, *d_keys) * scaling).astype(low)
        d_pair[1, at, :] = jnp.where(lane < size, *d_values).astype(low)
        return unused

    lax.fori_loop(0, steps, one_step, 0)
    if last_part:
        d_query[...] = (total[...].T * scaling).astype(low)
    else:
        d_query[...] = total[...]


def attend_back(
    pair, base, steps, token, projected, d_across, d_down, probs, carried
):
    rows = d_down.shape[0]
    size = LANES // 2
    all_steps = rows // KEYS
    last_part = base + steps == all_steps
    across = (rows, LANES) if last_part else (LANES, rows)
    vmem = pl.BlockSpec(memory_space=pltpu.VMEM)
    return pl.pallas_call(
        functools.partial(attend_back_kernel, size, pair, base, steps, last_part),
        in_specs=[SCALAR, vmem, vmem, vmem, pl.BlockSpec(memory_space=pl.ANY)]
        + [vmem] * len(carried),
        out_specs=[vmem, vmem],
        out_shape=[
            jax.ShapeDtypeStruct(across, low if last_part else full),
            jax.ShapeDtypeStruct((2, rows, LANES), low),
        ],
        scratch_shapes=[
            pltpu.VMEM((LANES, rows), full),
            pltpu.VMEM((2, 2, KEYS, rows), low),
            pltpu.SemaphoreType.DMA((2,)),
        ],
        compiler_params=pltpu.CompilerParams(vmem_limit_bytes=32 * 2**20),
        cost_estimate=pl.CostEstimate(
            flops=10 * rows * rows * 256 * steps // all_steps,
            bytes_accessed=rows * rows * 4 * steps // all_steps,
            transcendentals=0,
        ),
        name="attend_back",
    )(token, projected, d_across, d_down, probs, *carried)


def weigh_kernel(pairs, places, side, weight, first, *refs):
    d_query, d_pair = refs[:pairs], refs[pairs : 2 * pairs]
    keep, send, sums, grads, sems = refs[2 * pairs :]
    features = first.shape[0]
    grads[...] = jnp.zeros_like(grads)
    sums[...] = jnp.zeros_like(sums)
    parts = []
    for kind in range(3):
        for pair in range(pairs):
            values = d_query[pair][...] if kind == 0 else d_pair[pair][kind - 1]
            parts.append(values)
            if kind != 1:
                sums[
                    kind // 2 : kind // 2 + 1, pair * LANES : (pair + 1) * LANES
                ] = weight[0] * column_sum(values.astype(full))
    for start in range(0, len(parts), 2):
        some = parts[start : start + 2]
        product = mul(first[...], jnp.concatenate(some, axis=1)) * weight[0]
        for index in range(len(some)):
            half, base = places[start + index]
            grads[half, base : base + features, :] = product[
                :, index * LANES : (index + 1) * LANES
            ]
    copies = [
        pltpu.make_async_copy(grads.at[side[0]], keep, sems.at[0]),
        pltpu.make_async_copy(grads.at[1 - side[0]], send, sems.at[1]),
    ]
    for copy in copies:
        copy.start()
    for copy in copies:
        copy.wait()


def weigh(places, height, side, weight, first, d_query, d_pair):
    features = first.shape[0]
    vmem = pl.BlockSpec(memory_space=pltpu.VMEM)
    anywhere = pl.BlockSpec(memory_space=pl.ANY)
    pairs = len(d_query)
    return pl.pallas_call(
        functools.partial(weigh_kernel, pairs, places),
        in_specs=[SCALAR, SCALAR, vmem] + [vmem] * (2 * pairs),
        out_specs=[anywhere, anywhere, vmem],
        out_shape=[
            jax.ShapeDtypeStruct((height, LANES), full),
            jax.ShapeDtypeStruct((height, LANES), full),
            jax.ShapeDtypeStruct((8, features), full),
        ],
        scratch_shapes=[
            pltpu.VMEM((2, height, LANES), full),
            pltpu.SemaphoreType.DMA((2,)),
        ],
        compiler_params=pltpu.CompilerParams(vmem_limit_bytes=20 * 2**20),
        cost_estimate=pl.CostEstimate(
            flops=18 * d_query[0].shape[0] * features * features,
            bytes_accessed=d_query[0].shape[0] * features * 8,
            transcendentals=0,
        ),
        name="weigh",
    )(side, weight, first, *d_query, *d_pair)


def finish_kernel(pairs, last_part, lead, weight, x, embed, gain, wide, d_mid, *rest):
    d_query, d_pair, rest = rest[:pairs], rest[pairs : 2 * pairs], rest[2 * pairs :]
    if last_part:
        earlier, biases, _, grad_input, vectors, sums = rest
    else:
        grad_input, sums = rest
    step = pl.program_id(0)

    @pl.when(step == 0)
    def _():
        sums[...] = earlier[...] if last_part else jnp.zeros_like(sums)

    stream = x[...] + embed[pl.ds(lead[0], 1), :]
    unit, scale = normalize(stream)
    parts = []
    for kind in range(3):
        for pair in range(pairs):
            parts.append(d_query[pair][...] if kind == 0 else d_pair[pair][kind - 1])
    d_first = mul(jnp.concatenate(parts, axis=1), wide[...], NT)
    d_stream = (
        d_mid[...] + norm_back(d_first, unit, scale, gain[...][None, :])
    ) * weight[0]
    grad_input[...] = d_stream
    sums[0:1, :] += column_sum(d_first * unit) * weight[0]
    sums[1:2, :] += column_sum(d_first) * weight[0]
    sums[2:3, :] += column_sum(d_stream)

    if last_part:

        @pl.when(step == pl.num_programs(0) - 1)
        def _():
            vectors[...] = jnp.zeros_like(vectors)
            for index, (ref, at) in enumerate(
                ((sums, 0), (sums, 1), (biases, 0), (biases, 1), (sums, 2))
            ):
                for block in range(pairs):
                    row = index * pairs + block
                    vectors[row : row + 1, :] = ref[
                        at : at + 1, block * LANES : (block + 1) * LANES
                    ]


def finish(base, steps, lead, weight, x, embed, gain, wide, d_mid, d_query, d_pair, carried):
    rows, features = x.shape
    pairs = len(d_query)
    total = rows // ROWS
    last_part = base + steps == total
    height = up_to(5 * pairs, 8)
    row_spec = pl.BlockSpec((ROWS, features), lambda i: (base + i, 0))
    small = pl.BlockSpec((8, features), lambda i: (0, 0))
    return pl.pallas_call(
        functools.partial(finish_kernel, pairs, last_part),
        grid=(steps,),
        in_specs=[
            SCALAR,
            SCALAR,
            row_spec,
            whole(embed.shape),
            whole(gain.shape),
            whole(wide.shape),
            row_spec,
        ]
        + [pl.BlockSpec((ROWS, LANES), lambda i: (base + i, 0))] * pairs
        + [pl.BlockSpec((2, ROWS, LANES), lambda i: (0, base + i, 0))] * pairs
        + ([small, small, pl.BlockSpec(memory_space=pl.ANY)] if last_part else []),
        out_specs=[row_spec, whole((height, LANES)) if last_part else small],
        out_shape=[
            jax.ShapeDtypeStruct((rows, features), full),
            jax.ShapeDtypeStruct((height, LANES) if last_part else (8, features), full),
        ],
        scratch_shapes=[pltpu.VMEM((8, features), full)] if last_part else [],
        input_output_aliases={9 + 2 * pairs: 0} if last_part else {},
        compiler_params=params(1),
        cost_estimate=pl.CostEstimate(
            flops=6 * rows * features * features * steps // total,
            bytes_accessed=rows * features * 18 * steps // total,
            transcendentals=0,
        ),
        name="finish",
    )(lead, weight, x, embed, gain, wide, d_mid, *d_query, *d_pair, *carried)


def unpack_kernel(spans, group, channels, owners, *refs):
    chunks, expand, shrink, merge, router, vectors, grads, sems = refs
    chunk = chunks.shape[1]
    height = len(owners) * chunk // 2
    arrivals = [
        pltpu.make_async_copy(
            chunks.at[owner], grads.at[pl.ds(n * chunk, chunk)], sems.at[n]
        )
        for n, owner in enumerate(owners)
    ]
    for copy in arrivals:
        copy.start()
    for copy in arrivals:
        copy.wait()

    def block(name, rows, index):
        half, base = spans[name]
        start = half * height + base + index * rows
        return grads.at[pl.ds(start, rows)]

    features, hidden = expand.shape
    leaving = []
    for target, name in ((expand, "expand"), (merge, "merge")):
        for index in range(target.shape[1] // LANES):
            leaving.append(
                pltpu.make_async_copy(
                    block(name, features, index),
                    target.at[:, pl.ds(index * LANES, LANES)],
                    sems.at[len(owners) + len(leaving)],
                )
            )
    for copy in leaving:
        copy.start()
    for index in range(hidden // LANES):
        shrink[index * LANES : (index + 1) * LANES, :] = block("shrink", features, index)[
            ...
        ].T
    rows = 3 * group
    for index in range(features // LANES):
        values = block("router", rows, index)
        for e in range(3):
            router[
                e * channels : (e + 1) * channels, index * LANES : (index + 1) * LANES
            ] = values[e * group : e * group + channels, :]
    vectors[...] = block("expand_bias", vectors.shape[0], 0)[...]
    for copy in leaving:
        copy.wait()


def unpack(spans, group, channels, owners, features, hidden, tall, chunks):
    vmem = pl.BlockSpec(memory_space=pltpu.VMEM)
    anywhere = pl.BlockSpec(memory_space=pl.ANY)
    height = len(owners) * chunks.shape[1]
    return pl.pallas_call(
        functools.partial(unpack_kernel, spans, group, channels, owners),
        in_specs=[anywhere],
        out_specs=[anywhere, vmem, anywhere, vmem, vmem],
        out_shape=[
            jax.ShapeDtypeStruct((features, hidden), full),
            jax.ShapeDtypeStruct((hidden, features), full),
            jax.ShapeDtypeStruct((features, features), full),
            jax.ShapeDtypeStruct((3 * channels, features), full),
            jax.ShapeDtypeStruct((tall, LANES), full),
        ],
        scratch_shapes=[
            pltpu.VMEM((height, LANES), full),
            pltpu.SemaphoreType.DMA((len(owners) + (hidden + features) // LANES,)),
        ],
        compiler_params=pltpu.CompilerParams(vmem_limit_bytes=LIMIT),
        cost_estimate=pl.CostEstimate(
            flops=8 * 10**9, bytes_accessed=height * 1024, transcendentals=0
        ),
        name="unpack",
    )(chunks)


def join_kernel(group, spots, *refs):
    pieces, (out, sems) = refs[:-2], refs[-2:]
    height = pieces[0].shape[0]
    copies = []
    for mask, rows in enumerate(pieces):
        start = pl.multiple_of((spots[group] ^ mask) * height, 8)
        copies.append(
            pltpu.make_async_copy(rows, out.at[pl.ds(start, height)], sems.at[mask])
        )
    for copy in copies:
        copy.start()
    for copy in copies:
        copy.wait()


def join(group, spots, pieces):
    anywhere = pl.BlockSpec(memory_space=pl.ANY)
    return pl.pallas_call(
        functools.partial(join_kernel, group),
        in_specs=[SCALAR] + [anywhere] * len(pieces),
        out_specs=anywhere,
        out_shape=jax.ShapeDtypeStruct(
            (len(pieces) * pieces[0].shape[0], LANES), full
        ),
        scratch_shapes=[pltpu.SemaphoreType.DMA((len(pieces),))],
        compiler_params=pltpu.CompilerParams(vmem_limit_bytes=2**20),
        name="join",
    )(spots, *pieces)


def split_kernel(count, spots, *refs):
    outs = refs[-(len(refs) // (count + 1)) :]
    for mask, out in enumerate(outs):
        total = refs[mask * count][...]
        for index in range(1, count):
            total = total + refs[mask * count + index][...]
        out[...] = total


def split(group, fan, spots, terms):
    height = terms[0].shape[0] // fan

    def spec(mask):
        if fan == 1:
            return pl.BlockSpec((height, LANES), lambda i, spots: (0, 0))
        return pl.BlockSpec((height, LANES), lambda i, spots: (spots[group] ^ mask, 0))

    return pl.pallas_call(
        functools.partial(split_kernel, len(terms)),
        grid_spec=pltpu.PrefetchScalarGridSpec(
            num_scalar_prefetch=1,
            grid=(1,),
            in_specs=[spec(mask) for mask in range(fan) for _ in terms],
            out_specs=[pl.BlockSpec((height, LANES), lambda i, spots: (0, 0))] * fan,
        ),
        out_shape=[jax.ShapeDtypeStruct((height, LANES), full)] * fan,
        compiler_params=pltpu.CompilerParams(
            dimension_semantics=("arbitrary",), vmem_limit_bytes=16 * 2**20
        ),
        name="split",
    )(spots, *(list(terms) * fan))


def settle_kernel(
    places,
    owners,
    chunk,
    extra,
    side,
    leads,
    mine,
    got,
    attend,
    embed,
    vectors,
    held,
    table,
    sems,
):
    features = attend.shape[0]
    pairs = features // LANES
    arrivals = [
        pltpu.make_async_copy(mine, held.at[side[0]], sems.at[0]),
        pltpu.make_async_copy(got, held.at[1 - side[0]], sems.at[1]),
    ]
    for copy in arrivals:
        copy.start()
    table[...] = jnp.zeros_like(table)
    for copy in arrivals:
        copy.wait()
    stride = chunk + extra
    count = mine.shape[0] // stride
    leaving = []
    for index, (half, base) in enumerate(places):
        done = 0
        while done < features:
            at = base + done
            inside = at % chunk
            size = min(features - done, chunk - inside)
            leaving.append(
                pltpu.make_async_copy(
                    held.at[half, pl.ds(at // chunk * stride + inside, size)],
                    attend.at[pl.ds(done, size), pl.ds(index * LANES, LANES)],
                    sems.at[2 + len(leaving)],
                )
            )
            done += size
    for copy in leaving:
        copy.start()
    total = jnp.zeros((extra, LANES), full)
    row = lax.broadcasted_iota(jnp.int32, (table.shape[1], LANES), 0).astype(full)
    for half in range(2):
        for n in range(count):
            rows = held[half, n * stride + chunk : (n + 1) * stride, :]
            total = total + rows
            owner = owners[half * count + n]
            here = row == leads[owner : owner + 1, :]
            for block in range(pairs):
                at = 4 * pairs + block
                table[block] += jnp.where(here, rows[at : at + 1, :], 0.0)
    vectors[...] = total
    for block in range(pairs):
        embed[:, block * LANES : (block + 1) * LANES] = table[block]
    for copy in leaving:
        copy.wait()


def settle(places, owners, chunk, extra, leads, features, side, seen, mine, got):
    vmem = pl.BlockSpec(memory_space=pltpu.VMEM)
    anywhere = pl.BlockSpec(memory_space=pl.ANY)
    moves = 0
    for _, base in places:
        moves += (base + features - 1) // chunk - base // chunk + 1
    return pl.pallas_call(
        functools.partial(settle_kernel, places, owners, chunk, extra),
        in_specs=[SCALAR, vmem, anywhere, anywhere],
        out_specs=[anywhere, vmem, vmem],
        out_shape=[
            jax.ShapeDtypeStruct((features, 3 * features), full),
            jax.ShapeDtypeStruct((leads, features), full),
            jax.ShapeDtypeStruct((extra, LANES), full),
        ],
        scratch_shapes=[
            pltpu.VMEM((2, mine.shape[0], LANES), full),
            pltpu.VMEM((features // LANES, leads, LANES), full),
            pltpu.SemaphoreType.DMA((2 + moves,)),
        ],
        compiler_params=pltpu.CompilerParams(vmem_limit_bytes=32 * 2**20),
        name="settle",
    )(side, seen, mine, got)


def fold_kernel(count, sides, factors, *refs):
    total = refs[0][...] * factors[0]
    for index in range(1, count):
        total = total + refs[index][...] * factors[min(index, 2)]
    refs[count][...] = total


def fold(hop, hops, sides, factors, unit, terms):
    def spec(made):
        def index(i, sides, factors):
            at = i
            for step in range(made + 1, hop):
                at = at + sides[step] * 2 ** (hops - 1 - step)
            if hop < hops:
                at = at + (1 - sides[hop]) * 2 ** (hops - 1 - hop)
            return at, 0

        return pl.BlockSpec((unit, LANES), index)

    length = 2 ** (hops - 1 - hop) if hop < hops else 1
    return pl.pallas_call(
        functools.partial(fold_kernel, len(terms)),
        grid_spec=pltpu.PrefetchScalarGridSpec(
            num_scalar_prefetch=2,
            grid=(length,),
            in_specs=[spec(max(index - 1, 0)) for index in range(len(terms))],
            out_specs=pl.BlockSpec((unit, LANES), lambda i, *tables: (i, 0)),
        ),
        out_shape=jax.ShapeDtypeStruct((length * unit, LANES), full),
        compiler_params=pltpu.CompilerParams(
            dimension_semantics=("arbitrary",), vmem_limit_bytes=8 * 2**20
        ),
        name="fold",
    )(sides, factors, *terms)


def weights_kernel(index, frames, seen, weights, leads, held, sem):
    copy = pltpu.make_async_copy(seen.at[:, pl.ds(0, 8), :], held, sem)
    copy.start()
    total = lax.fori_loop(
        0, frames.shape[0], lambda n, sofar: sofar + frames[n], jnp.int32(0)
    ).astype(full)
    copy.wait()
    count = held.shape[0]
    rows = held[:, 0, :]
    leads[...] = rows
    device = lax.broadcasted_iota(jnp.int32, rows.shape, 0)
    for side in range(2):
        lead = jnp.max(jnp.where(device == index[side], rows, 0.0))
        same = jnp.sum(jnp.where(rows == lead, 1.0, 0.0)) / LANES
        chosen = frames[lead.astype(jnp.int32)].astype(full)
        weights[side] = chosen * count / (same * total)
    weights[2] = jnp.float32(1.0)


def weights_of(index, frames, seen):
    count = seen.shape[0]
    smem = pl.BlockSpec(memory_space=pltpu.SMEM)
    return pl.pallas_call(
        weights_kernel,
        in_specs=[smem, smem, pl.BlockSpec(memory_space=pl.ANY)],
        out_specs=[smem, pl.BlockSpec(memory_space=pltpu.VMEM)],
        out_shape=[
            jax.ShapeDtypeStruct((3,), full),
            jax.ShapeDtypeStruct((count, LANES), full),
        ],
        scratch_shapes=[
            pltpu.VMEM((count, 8, LANES), full),
            pltpu.SemaphoreType.DMA,
        ],
        compiler_params=pltpu.CompilerParams(vmem_limit_bytes=8 * 2**20),
        name="weights",
    )(index, frames, seen)


def up_to(value, step):
    return -(-value // step) * step


def tie(value, *others):
    return lax.optimization_barrier((value,) + others)[0]


def routes(sizes):
    inner = sizes["rep"]
    outer = sizes["dp"]
    if outer % 2:
        return 0, ((), ())
    far = [inner << n for n in range(1, outer.bit_length() - 1)]
    near = [1 << n for n in range(inner.bit_length() - 1)]
    even = []
    for n in range(max(len(far), len(near))):
        even += far[n : n + 1] + near[n : n + 1]
    odd = even[1:3] + even[:1] + even[3:]
    return inner, (tuple(even), tuple(odd))


class Ring:
    def __init__(self, sizes):
        self.count = sizes["dp"] * sizes["rep"]
        self.core_bit, self.orders = routes(sizes)
        self.hops = len(self.orders[0]) + 1 if self.core_bit else 0
        self.index = lax.axis_index(("dp", "rep"))

    def bits(self, hop):
        if hop == 0:
            return self.core_bit, self.core_bit
        return self.orders[0][hop - 1], self.orders[1][hop - 1]

    def swap(self, values, hop):
        pair = self.bits(hop)
        moves = [
            (i, i ^ pair[(i // self.core_bit) % 2]) for i in range(self.count)
        ]
        return lax.ppermute(values, ("dp", "rep"), moves)

    def sides(self):
        if not self.hops:
            return jnp.zeros((1,), jnp.int32)
        even, odd = (
            jnp.array((self.core_bit,) + order, jnp.int32) for order in self.orders
        )
        bits = jnp.where(self.index & self.core_bit == 0, even, odd)
        return jnp.where(self.index & bits == 0, 0, 1).astype(jnp.int32)

    def scatter(self, sides, factors, keep, send):
        unit = keep.shape[0] >> (self.hops - 1)
        terms = [keep]
        for hop in range(self.hops):
            if hop:
                send = fold(hop, self.hops, sides, factors, unit, terms)
            got = self.swap(send, hop)
            beside = yield send
            terms.append(got if beside is None else tie(got, beside))
        return fold(self.hops, self.hops, sides, factors, unit, terms)

    def owners(self):
        found = [0] * self.count
        for device in range(self.count):
            core = (device // self.core_bit) % 2
            chunk = 0
            for hop in range(self.hops):
                chunk = 2 * chunk + (1 if device & self.bits(hop)[core] else 0)
            found[chunk] = device
        return tuple(found)


class Wide:
    def __init__(self, ring):
        self.ring = ring
        order = ring.orders[0]
        even = [order[n : n + 2] for n in range(0, len(order), 2)]
        odd = list(even)
        if len(even) > 1 and len(even[1]) == 2:
            odd[0], odd[1] = even[1], even[0]
        self.groups = list(zip(even, odd))

    def place(self, device, group):
        core = 1 if device & self.ring.core_bit else 0
        spot = 0
        for bit in self.groups[group][core]:
            spot = 2 * spot + (1 if device & bit else 0)
        return spot

    def spots(self):
        ring = self.ring
        rows = []
        for device in range(ring.count):
            core = 1 if device & ring.core_bit else 0
            rows.append(
                [core] + [self.place(device, n) for n in range(len(self.groups))]
            )
        table = jnp.array(rows, jnp.int32)
        return lax.dynamic_index_in_dim(table, ring.index, 0, keepdims=False)

    def owners(self):
        found = [0] * self.ring.count
        for device in range(self.ring.count):
            chunk = 1 if device & self.ring.core_bit else 0
            for group, pair in enumerate(self.groups):
                chunk = chunk * 2 ** len(pair[0]) + self.place(device, group)
            found[chunk] = device
        return tuple(found)

    def swap(self, values, group, mask):
        ring = self.ring
        jumps = []
        for bits in self.groups[group]:
            jump = 0
            for n, bit in enumerate(reversed(bits)):
                jump |= bit if mask >> n & 1 else 0
            jumps.append(jump)
        moves = [
            (i, i ^ jumps[1 if i & ring.core_bit else 0]) for i in range(ring.count)
        ]
        return lax.ppermute(values, ("dp", "rep"), moves)

    def scatter(self, spots, keep, send):
        got = self.ring.swap(send, 0)
        beside = yield send
        terms = [keep, got if beside is None else tie(got, beside)]
        for group, pair in enumerate(self.groups):
            fan = 2 ** len(pair[0])
            own, *sends = split(group + 1, fan, spots, terms)
            gots = [
                self.swap(values, group, mask + 1) for mask, values in enumerate(sends)
            ]
            beside = yield own
            if beside is not None:
                gots = [tie(got, beside) for got in gots]
            terms = [own] + gots
        return split(0, 1, spots, terms)[0]


class Flow:
    def __init__(self, steps):
        self.steps = steps
        self.done = False
        self.sent = None
        self.result = None
        self.push(None)

    def push(self, beside):
        if self.done:
            return
        try:
            self.sent = self.steps.send(beside)
        except StopIteration as stop:
            self.done, self.sent, self.result = True, None, stop.value

    def drain(self):
        while not self.done:
            self.push(None)
        return self.result


def body(sizes, *args):
    (
        block_input,
        expert_out,
        upstream,
        lead_index,
        lead_frames,
        lead_embed,
        first_gain,
        first_shift,
        attend_weight,
        query_bias,
        value_bias,
        merge_weight,
        merge_bias,
        second_gain,
        second_shift,
        expand_weight,
        expand_bias,
        shrink_weight,
        shrink_bias,
        router_weight,
        router_bias,
        correction,
    ) = args
    rows, features = block_input.shape
    channels = correction.shape[0]
    leads = lead_embed.shape[0]
    hidden = expand_bias.shape[0]
    devices = sizes["dp"] * sizes["rep"]
    pairs = features // LANES
    grain = 4 * devices
    ring = Ring(sizes)
    sides = ring.sides()
    wide = Wide(ring) if ring.hops else None
    spots = wide.spots() if ring.hops else sides

    tall = max(8, 2048 // devices)
    mine = lead_index[0].astype(full)
    seen = lax.optimization_barrier(
        lax.all_gather(
            lax.optimization_barrier(jnp.full((tall, LANES), mine)), ("dp", "rep")
        )
    )
    weight, leads_seen = weights_of(
        jnp.stack([ring.index, ring.index ^ ring.core_bit]).astype(jnp.int32),
        lead_frames,
        seen,
    )

    first, projected, *own = project(
        lead_index,
        block_input,
        lead_embed,
        first_gain,
        first_shift,
        attend_weight,
        query_bias,
        value_bias,
    )
    probs, mixed, inverse = attend(projected)

    group = up_to(channels, 16)
    spans, heights = {}, [0, 0]
    for name, half, height in (
        ("expand", 0, features * hidden // LANES),
        ("merge", 0, features * features // LANES),
        ("shrink", 1, features * hidden // LANES),
        ("router", 1, features * 3 * group // LANES),
        ("expand_bias", 1, hidden // LANES),
        ("shrink_bias", 1, pairs),
        ("merge_bias", 1, pairs),
        ("second_gain", 1, pairs),
        ("second_shift", 1, pairs),
        ("head", 1, up_to(4 * group, LANES) // LANES),
    ):
        spans[name] = (half, heights[half])
        heights[half] += height
    vector_rows = up_to(heights[1] - spans["expand_bias"][1], 8)
    height = up_to(max(heights[0], spans["expand_bias"][1] + vector_rows), grain)
    wide_router = jnp.pad(
        router_weight.T.reshape(3, channels, features),
        ((0, 0), (0, group - channels), (0, 0)),
    ).reshape(3 * group, features)
    columns = jnp.stack(
        [
            jnp.pad(
                router_bias.reshape(3, channels), ((0, 0), (0, group - channels))
            ).reshape(-1),
            jnp.pad(correction, (0, 3 * group - channels)),
        ],
        axis=1,
    )
    tables = (
        lead_embed,
        merge_weight,
        merge_bias,
        second_gain,
        second_shift,
        expand_weight,
        expand_bias,
        shrink_weight,
        shrink_bias,
        wide_router,
        columns,
    )
    blended, d_mid, *rest = middle(
        spans,
        height,
        group,
        sides,
        lead_index,
        block_input,
        mixed,
        inverse,
        expert_out.T,
        upstream.T,
        tables,
    )
    d_across, d_down = rest[:pairs], rest[pairs : 2 * pairs]
    keep, send = rest[2 * pairs :]
    flow = None
    if ring.hops:
        flow = Flow(ring.scatter(sides, weight, keep, tie(send, seen)))
    plan = ((1, 3), (2, 1, 1), (4,))
    d_query, d_pair = [], []
    for pair in range(pairs):
        carried = ()
        base = 0
        for steps in plan[pair]:
            token = sides if flow is None or flow.done else tie(sides, flow.sent)
            carried = attend_back(
                pair,
                base,
                steps,
                token,
                own[pair],
                d_across[pair],
                d_down[pair],
                probs,
                carried,
            )
            base += steps
            if flow is not None:
                flow.push(carried[0])
        d_query.append(carried[0])
        d_pair.append(carried[1])
    places = tuple(
        (n // 5, (n % 5) * features) for n in range(3 * pairs)
    )
    tail_height = up_to(5 * features, grain)
    now = weight if flow is None else tie(weight, flow.drain())
    tail_keep, tail_send, biases = weigh(
        places, tail_height, sides, now, first, d_query, d_pair
    )
    late = None
    if ring.hops:
        late = Flow(wide.scatter(spots, tail_keep, tail_send))
    carried = ()
    base = 0
    for steps in (2, 2):
        now = weight if late is None else tie(weight, late.sent)
        grad_input, sums = finish(
            base,
            steps,
            lead_index,
            now,
            block_input,
            lead_embed,
            first_gain,
            attend_weight,
            d_mid,
            d_query,
            d_pair,
            carried,
        )
        base += steps
        carried = (sums, biases, grad_input)
        if late is not None:
            late.push(sums)
    extra = sums.shape[0]
    if ring.hops:
        owners = ring.owners()
        chunks = lax.all_gather(flow.result, ("dp", "rep"))
        piece = jnp.concatenate([late.drain(), sums])
        for stage in reversed(range(1, len(wide.groups))):
            fan = 2 ** len(wide.groups[stage][0])
            gots = [wide.swap(piece, stage, mask) for mask in range(1, fan)]
            piece = join(stage + 1, spots, [piece] + gots)
        gots = [
            wide.swap(piece, 0, mask) for mask in range(1, 2 ** len(wide.groups[0][0]))
        ]
        chunks = tie(chunks, piece)
        chunk = 2 * tail_height // devices
    else:
        owners = (0, 1)
        chunks = jnp.stack([keep, send]) * weight[0]
        chunk = tail_height
        piece = jnp.concatenate([tail_keep, sums])
        got = jnp.concatenate([tail_send, jnp.zeros_like(sums)])
        leads_seen = jnp.concatenate([leads_seen, leads_seen + leads])
    grad_expand, grad_shrink, grad_merge, grad_router, vectors = unpack(
        spans, group, channels, owners, features, hidden, vector_rows, chunks
    )
    first_vector = spans["expand_bias"][1]

    def take(name, length):
        start = spans[name][1] - first_vector
        return vectors[start : start + length // LANES].reshape(-1)

    head = take("head", up_to(4 * group, LANES))
    middle_vectors = (
        take("merge_bias", features),
        take("second_gain", features),
        take("second_shift", features),
        take("expand_bias", hidden),
        take("shrink_bias", features),
        head[: 3 * group].reshape(3, group)[:, :channels].reshape(-1),
        head[3 * group : 3 * group + channels],
    )
    if ring.hops:
        gots = [tie(got, *middle_vectors) for got in gots]
        piece = join(1, spots, [piece] + gots)
        got = ring.swap(piece, 0)
        owners = wide.owners()
    grad_attend, grad_embed, small = settle(
        places,
        owners,
        chunk,
        extra,
        leads,
        features,
        sides,
        leads_seen,
        piece,
        got,
    )
    small = small[: 4 * pairs].reshape(4, features)
    merge_b, gain_b, shift_b, expand_b, shrink_b, router_b, correct = middle_vectors
    return (
        blended.T,
        grad_input,
        grad_embed,
        small[0],
        small[1],
        grad_attend,
        small[2],
        small[3],
        grad_merge,
        merge_b,
        gain_b,
        shift_b,
        grad_expand,
        expand_b,
        grad_shrink,
        shrink_b,
        grad_router.T,
        router_b,
        correct,
    )


def solution(mesh):
    split = P(("dp", "rep"), None)
    sizes = dict(mesh.shape)
    return jax.shard_map(
        functools.partial(body, sizes),
        mesh=mesh,
        in_specs=(split, split, split, P(("dp", "rep"))) + (P(),) * 18,
        out_specs=(split, split) + (P(),) * 17,
        check_vma=False,
    )
```

```python
import functools

import jax
import jax.numpy as jnp
from jax import lax
from jax.experimental import pallas as pl
from jax.experimental.pallas import tpu as pltpu
from jax.sharding import PartitionSpec as P

HEADS = 6
EPSILON = 1e-05
PENALTY = 1.0
GELU_COEF = 0.7978845608028654
GELU_CUBE = 0.044715
LOG2E = 1.4426950408889634
LANES = 128
ROWS = 512
KEYS = 512
LIMIT = 56 * 2**20
BACK_LIMIT = 26 * 2**20
NORM_ROWS = 1024

low = jnp.bfloat16
full = jnp.float32


def mul(left, right, dims=((1,), (0,))):
    return lax.dot_general(left, right, (dims, ((), ())), preferred_element_type=full)


NT = ((1,), (1,))
TN = ((0,), (0,))


def params(count, limit=LIMIT):
    return pltpu.CompilerParams(
        dimension_semantics=("arbitrary",) * count, vmem_limit_bytes=limit
    )


def whole(shape):
    return pl.BlockSpec(shape, lambda *step: (0,) * len(shape))


SCALAR = pl.BlockSpec(memory_space=pltpu.SMEM)


def normalize(values):
    centre = jnp.mean(values, axis=-1, keepdims=True)
    centred = values - centre
    spread = jnp.mean(centred * centred, axis=-1, keepdims=True)
    scale = lax.rsqrt(spread + EPSILON)
    return centred * scale, scale


def norm_back(grad, unit, scale, gain):
    e = grad * gain
    first = jnp.mean(e, axis=-1, keepdims=True)
    second = jnp.mean(e * unit, axis=-1, keepdims=True)
    return scale * (e - first - unit * second)


def column_sum(values):
    return jnp.sum(values, axis=0, keepdims=True)


def project_kernel(
    lead, x, embed, gain, shift, weight, query_b, value_b, first, projected, *own
):
    stream = x[...] + embed[pl.ds(lead[0], 1), :]
    unit, _ = normalize(stream)
    rounded = (unit * gain[...][None, :] + shift[...][None, :]).astype(low)
    first[...] = rounded.T
    features = x.shape[1]
    query_row = query_b[...][None, :]
    bias = jnp.concatenate(
        [query_row, jnp.zeros_like(query_row), value_b[...][None, :]], axis=1
    )
    product = (mul(rounded, weight[...]) + bias).astype(low)
    pairs = projected.shape[0]
    for pair in range(pairs):
        for kind in range(3):
            block = kind * pairs + pair
            values = product[:, block * LANES : (block + 1) * LANES]
            projected[pair, kind] = values
            own[pair][kind] = values


def project(lead, x, embed, gain, shift, weight, query_b, value_b):
    rows, features = x.shape
    tables = (embed, gain, shift, weight, query_b, value_b)
    return pl.pallas_call(
        project_kernel,
        grid=(rows // NORM_ROWS,),
        in_specs=[SCALAR, pl.BlockSpec((NORM_ROWS, features), lambda i: (i, 0))]
        + [whole(table.shape) for table in tables],
        out_specs=[
            pl.BlockSpec((features, NORM_ROWS), lambda i: (0, i)),
            pl.BlockSpec((features // LANES, 3, NORM_ROWS, LANES), lambda i: (0, 0, i, 0)),
        ]
        + [pl.BlockSpec((3, NORM_ROWS, LANES), lambda i: (0, i, 0))] * (features // LANES),
        out_shape=[
            jax.ShapeDtypeStruct((features, rows), low),
            jax.ShapeDtypeStruct((features // LANES, 3, rows, LANES), low),
        ]
        + [jax.ShapeDtypeStruct((3, rows, LANES), low)] * (features // LANES),
        compiler_params=params(1),
        name="project",
    )(lead, x, *tables)


def attend_kernel(size, q, k, v, probs, mixed, inverse, turned):
    keys = k.shape[2]
    count = q.shape[2]
    scaling = size ** (-0.5) * LOG2E

    @pl.when(pl.program_id(1) == 0)
    def _():
        across = v[0, 0].T
        tail = lax.broadcasted_iota(jnp.int32, (16, keys), 0)
        ones = jnp.where(tail == 0, 1.0, 0.0).astype(low)
        for head in range(2):
            turned[head, 0:size, :] = across[head * size : (head + 1) * size, :]
            turned[head, size : size + 16, :] = ones

    lane = lax.broadcasted_iota(jnp.int32, (1, LANES), 1)

    def scores(head, start):
        mask = jnp.where(lane // size == head, 1.0, 0.0).astype(low)
        return mul(k[0, 0, start : start + keys, :], q[0, 0] * mask, NT) * scaling

    def finish(head, total):
        spread = total[size : size + 1, :]
        inv = 1.0 / spread
        inverse[0, head : head + 1, :] = inv
        mixed[head * size : (head + 1) * size, :] = (total[0:size, :] * inv).astype(low)
        return spread

    extremes = []
    for head in range(2):
        total = jnp.zeros((size + 16, count), full)
        for start in (0,):
            p = jnp.exp2(scores(head, start)).astype(low)
            probs[0, head, start : start + keys, :] = p
            total = total + mul(turned[head, :, start : start + keys], p)
        spread = finish(head, total)
        extremes.append(spread)

    both = jnp.concatenate(extremes, axis=0)
    inside = jnp.where((both > 1e-18) & (both < 1e18), 1.0, 0.0)

    @pl.when(jnp.min(inside) < 0.5)
    def _():
        for head in range(2):
            top = jnp.full((1, count), -jnp.inf, full)
            for start in (0,):
                top = jnp.maximum(
                    top, jnp.max(scores(head, start), axis=0, keepdims=True)
                )
            total = jnp.zeros((size + 16, count), full)
            for start in (0,):
                p = jnp.exp2(scores(head, start) - top).astype(low)
                probs[0, head, start : start + keys, :] = p
                total = total + mul(turned[head, :, start : start + keys], p)
            finish(head, total)


def attend(projected):
    pairs, _, rows, _ = projected.shape
    features = pairs * LANES
    size = features // HEADS
    return pl.pallas_call(
        functools.partial(attend_kernel, size),
        grid=(pairs, rows // ROWS),
        in_specs=[
            pl.BlockSpec((1, 1, ROWS, LANES), lambda p, i: (p, 0, i, 0)),
            pl.BlockSpec((1, 1, rows, LANES), lambda p, i: (p, 1, 0, 0)),
            pl.BlockSpec((1, 1, rows, LANES), lambda p, i: (p, 2, 0, 0)),
        ],
        out_specs=[
            pl.BlockSpec((1, 2, rows, ROWS), lambda p, i: (p, 0, 0, i)),
            pl.BlockSpec((LANES, ROWS), lambda p, i: (p, i)),
            pl.BlockSpec((1, 8, ROWS), lambda p, i: (p, 0, i)),
        ],
        out_shape=[
            jax.ShapeDtypeStruct((pairs, 2, rows, rows), low),
            jax.ShapeDtypeStruct((features, rows), low),
            jax.ShapeDtypeStruct((pairs, 8, rows), full),
        ],
        scratch_shapes=[pltpu.VMEM((2, size + 16, rows), low)],
        compiler_params=params(2),
        name="attend",
    )(projected, projected, projected)


def middle_kernel(
    spans,
    size,
    group,
    side,
    lead,
    x,
    mixed,
    inverse,
    experts,
    upstream,
    embed,
    merge_w,
    merge_b,
    gain,
    shift,
    expand_w,
    expand_b,
    shrink_w,
    shrink_b,
    router_in,
    router_b,
    correct,
    blended,
    d_mid,
    *rest,
):
    pairs = x.shape[1] // LANES
    d_across, d_down = rest[:pairs], rest[pairs : 2 * pairs]
    keep, send, grads, lanes, router_w, columns, sems = rest[2 * pairs :]
    features = x.shape[1]
    step = x.shape[0]
    hidden_size = expand_w.shape[1]
    channels = upstream.shape[0]
    chunk = hidden_size // 2

    @pl.when(pl.program_id(0) == 0)
    def _():
        grads[...] = jnp.zeros_like(grads)
        lanes[...] = jnp.zeros_like(lanes)
        weights = router_in[...].astype(full)
        wide = up_to(3 * channels, LANES)

        def down(row, width):
            row = jnp.concatenate(
                [row, jnp.zeros((1, width - row.shape[1]), full)], axis=1
            )
            return jnp.broadcast_to(row, (8, width)).T

        biases = down(router_b[...][None, :], wide)
        columns[...] = jnp.zeros_like(columns)
        for e in range(3):
            rows = slice(e * channels, (e + 1) * channels)
            router_w[e * group : (e + 1) * group, :] = jnp.concatenate(
                [weights[rows, :], jnp.zeros((group - channels, features), full)],
                axis=0,
            ).astype(low)
            columns[e * group : e * group + channels, 0:8] = biases[rows, :]
        columns[0:channels, 8:16] = down(correct[...][None, :], LANES)[:channels, :]

    def add(name, values, part=0):
        half, base = spans[name]
        height = values.shape[0]
        for block in range(values.shape[1] // LANES):
            start = base + (part + block) * height
            grads[half, start : start + height, :] += values[
                :, block * LANES : (block + 1) * LANES
            ]

    stream = x[...] + embed[pl.ds(lead[0], 1), :]
    mid = stream + mul(mixed[...], merge_w[...], TN) + merge_b[...][None, :]
    unit, scale = normalize(mid)
    gain_row = gain[...][None, :]
    second = (unit * gain_row + shift[...][None, :]).astype(low)
    output = mid + shrink_b[...][None, :]
    bias = expand_b[...][None, :]
    hidden, slope = [], []
    for start in range(0, hidden_size, chunk):
        part = slice(start, start + chunk)
        u = mul(second, expand_w[:, part]) + bias[:, part]
        square = u * u
        t = jnp.tanh(u * (GELU_COEF + GELU_COEF * GELU_CUBE * square))
        half = 0.5 + 0.5 * t
        act = u * half
        slope.append(
            half
            + act
            * (1.0 - half)
            * (2.0 * GELU_COEF + 6.0 * GELU_COEF * GELU_CUBE * square)
        )
        act = act.astype(low)
        hidden.append(act)
        output = output + mul(act, shrink_w[part, :])
    output_low = output.astype(low)
    logits = mul(router_w[...], output_low, NT) + columns[:, 0:1]
    valid = lax.broadcasted_iota(jnp.int32, (group, 1), 0) < channels
    parts = [logits[e * group : (e + 1) * group, :] for e in range(3)]
    largest = jnp.maximum(jnp.maximum(parts[0], parts[1]), parts[2])
    parts = [part - largest for part in parts]
    raised = [jnp.exp(part) for part in parts]
    total = raised[0] + raised[1] + raised[2]
    shared = jnp.log(total)
    logs = [part - shared for part in parts]
    share = 1.0 / total
    gates = [value * share for value in raised]

    def widen(values):
        return jnp.concatenate(
            [values, jnp.zeros((group - channels, step), full)], axis=0
        )

    frames = [
        widen(experts[e * channels : (e + 1) * channels, :]) for e in range(3)
    ]
    up = widen(upstream[...])
    mix = gates[0] * frames[0] + gates[1] * frames[1] + gates[2] * frames[2]
    entropy = -(gates[0] * logs[0] + gates[1] * logs[1] + gates[2] * logs[2])
    blended[...] = mix[:channels, :] + columns[:channels, 8:9]
    d_parts = [
        jnp.where(
            valid,
            gates[e] * (up * (frames[e] - mix) - PENALTY * (logs[e] + entropy)),
            0.0,
        )
        for e in range(3)
    ]
    for index, values in enumerate(d_parts + [up]):
        for start in range(0, step, LANES):
            lanes[index * group : (index + 1) * group, :] += values[
                :, start : start + LANES
            ]
    d_logits_low = jnp.concatenate(d_parts, axis=0).astype(low)
    add("router", mul(d_logits_low, output_low))
    d_output = mul(d_logits_low, router_w[...], TN)
    add("shrink_bias", column_sum(d_output))
    d_output_low = d_output.astype(low)
    d_turned = d_output_low.T
    second_turned = second.T
    d_second = jnp.zeros_like(d_output)
    for index, start in enumerate(range(0, hidden_size, chunk)):
        part = slice(start, start + chunk)
        d_pre = mul(d_output_low, shrink_w[part, :], NT) * slope[index]
        add("expand_bias", column_sum(d_pre), start // LANES)
        d_pre_low = d_pre.astype(low)
        d_second = d_second + mul(d_pre_low, expand_w[:, part], NT)
        add("expand", mul(second_turned, d_pre_low), start // LANES)
        add("shrink", mul(d_turned, hidden[index]), start // LANES)
    add("second_gain", column_sum(d_second * unit))
    add("second_shift", column_sum(d_second))
    grad_mid = d_output + norm_back(d_second, unit, scale, gain_row)
    d_mid[...] = grad_mid
    add("merge_bias", column_sum(grad_mid))
    d_mid_low = grad_mid.astype(low)
    add("merge", mul(mixed[...], d_mid_low))
    d_mixed = mul(merge_w[...], d_mid_low, NT).astype(low).astype(full)
    row = lax.broadcasted_iota(jnp.int32, (size, step), 0)
    stack = []
    for head in range(features // size):
        span = slice(head * size, (head + 1) * size)
        odd = head % 2
        inv = inverse[head // 2, odd : odd + 1, :]
        scaled = (d_mixed[span, :] * inv).astype(low)
        stack.append(scaled)
        centre = -column_sum(scaled.astype(full) * mixed[span, :].astype(full))
        one = centre.astype(low).astype(full)
        two = (centre - one).astype(low).astype(full)
        extra = jnp.where(
            row == 0,
            one,
            jnp.where(row == 1, two, jnp.where(row == 2, centre - one - two, 0.0)),
        ).astype(low)
        across = d_across[head // 2]
        across[odd, odd * size : (odd + 1) * size, :] = scaled
        across[odd, (1 - odd) * size : (2 - odd) * size, :] = extra
    for pair in range(pairs):
        d_down[pair][...] = jnp.concatenate(stack[2 * pair : 2 * pair + 2], axis=0).T

    @pl.when(pl.program_id(0) == pl.num_programs(0) - 1)
    def _():
        sums = column_sum(lanes[...].T)
        width = sums.shape[1]
        wide = up_to(width, LANES)
        sums = jnp.concatenate([sums, jnp.zeros((1, wide - width), full)], axis=1)
        add("head", sums)
        copies = [
            pltpu.make_async_copy(grads.at[side[SIDES]], keep, sems.at[0]),
            pltpu.make_async_copy(grads.at[1 - side[SIDES]], send, sems.at[1]),
        ]
        for copy in copies:
            copy.start()
        for copy in copies:
            copy.wait()


def middle(spans, height, group, side, lead, x, mixed, inverse, experts, upstream, tables):
    rows, features = x.shape
    size = features // HEADS
    channels = upstream.shape[0]
    step = ROWS
    pairs = features // LANES
    anywhere = pl.BlockSpec(memory_space=pl.ANY)
    return pl.pallas_call(
        functools.partial(middle_kernel, spans, size, group),
        grid=(rows // step,),
        in_specs=[
            SCALAR,
            SCALAR,
            pl.BlockSpec((step, features), lambda i: (i, 0)),
            pl.BlockSpec((features, step), lambda i: (0, i)),
            pl.BlockSpec((inverse.shape[0], 8, step), lambda i: (0, 0, i)),
            pl.BlockSpec((experts.shape[0], step), lambda i: (0, i)),
            pl.BlockSpec((channels, step), lambda i: (0, i)),
        ]
        + [whole(table.shape) for table in tables],
        out_specs=[
            pl.BlockSpec((channels, step), lambda i: (0, i)),
            pl.BlockSpec((step, features), lambda i: (i, 0)),
        ]
        + [pl.BlockSpec((2, LANES, step), lambda i: (0, 0, i))] * pairs
        + [pl.BlockSpec((step, LANES), lambda i: (i, 0))] * pairs
        + [anywhere, anywhere],
        out_shape=[
            jax.ShapeDtypeStruct((channels, rows), full),
            jax.ShapeDtypeStruct((rows, features), full),
        ]
        + [jax.ShapeDtypeStruct((2, LANES, rows), low)] * pairs
        + [jax.ShapeDtypeStruct((rows, LANES), low)] * pairs
        + [jax.ShapeDtypeStruct((height, LANES), full)] * 2,
        scratch_shapes=[
            pltpu.VMEM((2, height, LANES), full),
            pltpu.VMEM((4 * group, LANES), full),
            pltpu.VMEM((3 * group, features), low),
            pltpu.VMEM((3 * group, LANES), full),
            pltpu.SemaphoreType.DMA((2,)),
        ],
        compiler_params=params(1),
        name="middle",
    )(side, lead, x, mixed, inverse, experts, upstream, *tables)


def attend_back_kernel(size, pair, base, steps, last_part, token, *refs):
    if base == 0:
        projected, d_across, d_down, probs, d_query, d_pair, total, held, sems = refs
        carry = None
    else:
        projected, d_across, d_down, probs, carry, earlier, *refs = refs
        d_query, d_pair, total, held, sems = refs
        d_pair[:, : base * KEYS, :] = earlier[:, : base * KEYS, :]
    rows = d_down.shape[0]
    scaling = size ** (-0.5)
    lane = lax.broadcasted_iota(jnp.int32, (1, LANES), 1)

    def fetch(step, slot):
        return pltpu.make_async_copy(
            probs.at[pair, :, pl.ds((base + step) * KEYS, KEYS), :],
            held.at[slot],
            sems.at[slot],
        )

    fetch(0, 0).start()
    total[...] = jnp.zeros_like(total) if carry is None else carry[...]

    def one_step(step, unused):
        slot = lax.rem(step, 2)

        @pl.when(step + 1 < steps)
        def _():
            fetch(step + 1, 1 - slot).start()

        fetch(step, slot).wait()
        at = pl.ds(pl.multiple_of((base + step) * KEYS, KEYS), KEYS)
        v = projected[2, at, :]
        k_across = projected[1, at, :].T
        d_keys, d_values = [], []
        for head in range(2):
            other = (1 - head) * size
            data = jnp.where(lane // size == head, 1.0, 0.0).astype(low)
            ones = jnp.where((lane >= other) & (lane < other + 3), 1.0, 0.0)
            values = v * data + ones.astype(low)
            p = held[slot, head]
            d_p = mul(values, d_across[head])
            d_s = (p.astype(full) * d_p).astype(low)
            span = slice(head * size, (head + 1) * size)
            total[span, :] += mul(k_across[span, :], d_s)
            d_values.append(mul(p, d_down[...]))
            d_keys.append(mul(d_s, projected[0]))
        d_pair[0, at, :] = (jnp.where(lane < size, *d_keys) * scaling).astype(low)
        d_pair[1, at, :] = jnp.where(lane < size, *d_values).astype(low)
        return unused

    lax.fori_loop(0, steps, one_step, 0)
    if last_part:
        d_query[...] = (total[...].T * scaling).astype(low)
    else:
        d_query[...] = total[...]


def attend_back(
    pair, base, steps, token, projected, d_across, d_down, probs, carried
):
    rows = d_down.shape[0]
    size = LANES // 2
    all_steps = rows // KEYS
    last_part = base + steps == all_steps
    across = (rows, LANES) if last_part else (LANES, rows)
    vmem = pl.BlockSpec(memory_space=pltpu.VMEM)
    return pl.pallas_call(
        functools.partial(attend_back_kernel, size, pair, base, steps, last_part),
        in_specs=[SCALAR, vmem, vmem, vmem, pl.BlockSpec(memory_space=pl.ANY)]
        + [vmem] * len(carried),
        out_specs=[vmem, vmem],
        out_shape=[
            jax.ShapeDtypeStruct(across, low if last_part else full),
            jax.ShapeDtypeStruct((2, rows, LANES), low),
        ],
        scratch_shapes=[
            pltpu.VMEM((LANES, rows), full),
            pltpu.VMEM((2, 2, KEYS, rows), low),
            pltpu.SemaphoreType.DMA((2,)),
        ],
        compiler_params=pltpu.CompilerParams(vmem_limit_bytes=BACK_LIMIT),
        cost_estimate=pl.CostEstimate(
            flops=10 * rows * rows * 256 * steps // all_steps,
            bytes_accessed=rows * rows * 4 * steps // all_steps,
            transcendentals=0,
        ),
        name="attend_back",
    )(token, projected, d_across, d_down, probs, *carried)


def weigh_kernel(pairs, places, side, weight, first, *refs):
    d_query, d_pair = refs[:pairs], refs[pairs : 2 * pairs]
    keep, send, sums, grads, sems = refs[2 * pairs :]
    features = first.shape[0]
    grads[...] = jnp.zeros_like(grads)
    sums[...] = jnp.zeros_like(sums)
    parts = []
    for kind in range(3):
        for pair in range(pairs):
            values = d_query[pair][...] if kind == 0 else d_pair[pair][kind - 1]
            parts.append(values)
            if kind != 1:
                sums[
                    kind // 2 : kind // 2 + 1, pair * LANES : (pair + 1) * LANES
                ] = weight[0] * column_sum(values.astype(full))
    for start in range(0, len(parts), 2):
        some = parts[start : start + 2]
        product = mul(first[...], jnp.concatenate(some, axis=1)) * weight[0]
        for index in range(len(some)):
            half, base = places[start + index]
            grads[half, base : base + features, :] = product[
                :, index * LANES : (index + 1) * LANES
            ]
    copies = [
        pltpu.make_async_copy(grads.at[side[SIDES]], keep, sems.at[0]),
        pltpu.make_async_copy(grads.at[1 - side[SIDES]], send, sems.at[1]),
    ]
    for copy in copies:
        copy.start()
    for copy in copies:
        copy.wait()


def weigh(places, height, side, weight, first, d_query, d_pair):
    features = first.shape[0]
    vmem = pl.BlockSpec(memory_space=pltpu.VMEM)
    anywhere = pl.BlockSpec(memory_space=pl.ANY)
    pairs = len(d_query)
    return pl.pallas_call(
        functools.partial(weigh_kernel, pairs, places),
        in_specs=[SCALAR, SCALAR, vmem] + [vmem] * (2 * pairs),
        out_specs=[anywhere, anywhere, vmem],
        out_shape=[
            jax.ShapeDtypeStruct((height, LANES), full),
            jax.ShapeDtypeStruct((height, LANES), full),
            jax.ShapeDtypeStruct((8, features), full),
        ],
        scratch_shapes=[
            pltpu.VMEM((2, height, LANES), full),
            pltpu.SemaphoreType.DMA((2,)),
        ],
        compiler_params=pltpu.CompilerParams(vmem_limit_bytes=20 * 2**20),
        cost_estimate=pl.CostEstimate(
            flops=18 * d_query[0].shape[0] * features * features,
            bytes_accessed=d_query[0].shape[0] * features * 8,
            transcendentals=0,
        ),
        name="weigh",
    )(side, weight, first, *d_query, *d_pair)


def finish_kernel(pairs, last_part, lead, weight, x, embed, gain, wide, d_mid, *rest):
    d_query, d_pair, rest = rest[:pairs], rest[pairs : 2 * pairs], rest[2 * pairs :]
    if last_part:
        earlier, biases, _, grad_input, vectors, sums = rest
    else:
        grad_input, sums = rest
    step = pl.program_id(0)

    @pl.when(step == 0)
    def _():
        sums[...] = earlier[...] if last_part else jnp.zeros_like(sums)

    stream = x[...] + embed[pl.ds(lead[0], 1), :]
    unit, scale = normalize(stream)
    parts = []
    for kind in range(3):
        for pair in range(pairs):
            parts.append(d_query[pair][...] if kind == 0 else d_pair[pair][kind - 1])
    d_first = mul(jnp.concatenate(parts, axis=1), wide[...], NT)
    d_stream = (
        d_mid[...] + norm_back(d_first, unit, scale, gain[...][None, :])
    ) * weight[0]
    grad_input[...] = d_stream
    sums[0:1, :] += column_sum(d_first * unit) * weight[0]
    sums[1:2, :] += column_sum(d_first) * weight[0]
    sums[2:3, :] += column_sum(d_stream)

    if last_part:

        @pl.when(step == pl.num_programs(0) - 1)
        def _():
            vectors[...] = jnp.zeros_like(vectors)
            for index, (ref, at) in enumerate(
                ((sums, 0), (sums, 1), (biases, 0), (biases, 1), (sums, 2))
            ):
                for block in range(pairs):
                    row = index * pairs + block
                    vectors[row : row + 1, :] = ref[
                        at : at + 1, block * LANES : (block + 1) * LANES
                    ]


def finish(base, steps, lead, weight, x, embed, gain, wide, d_mid, d_query, d_pair, carried):
    rows, features = x.shape
    pairs = len(d_query)
    total = rows // ROWS
    last_part = base + steps == total
    height = up_to(5 * pairs, 8)
    row_spec = pl.BlockSpec((ROWS, features), lambda i: (base + i, 0))
    small = pl.BlockSpec((8, features), lambda i: (0, 0))
    return pl.pallas_call(
        functools.partial(finish_kernel, pairs, last_part),
        grid=(steps,),
        in_specs=[
            SCALAR,
            SCALAR,
            row_spec,
            whole(embed.shape),
            whole(gain.shape),
            whole(wide.shape),
            row_spec,
        ]
        + [pl.BlockSpec((ROWS, LANES), lambda i: (base + i, 0))] * pairs
        + [pl.BlockSpec((2, ROWS, LANES), lambda i: (0, base + i, 0))] * pairs
        + ([small, small, pl.BlockSpec(memory_space=pl.ANY)] if last_part else []),
        out_specs=[row_spec, whole((height, LANES)) if last_part else small],
        out_shape=[
            jax.ShapeDtypeStruct((rows, features), full),
            jax.ShapeDtypeStruct((height, LANES) if last_part else (8, features), full),
        ],
        scratch_shapes=[pltpu.VMEM((8, features), full)] if last_part else [],
        input_output_aliases={9 + 2 * pairs: 0} if last_part else {},
        compiler_params=params(1),
        cost_estimate=pl.CostEstimate(
            flops=6 * rows * features * features * steps // total,
            bytes_accessed=rows * features * 18 * steps // total,
            transcendentals=0,
        ),
        name="finish",
    )(lead, weight, x, embed, gain, wide, d_mid, *d_query, *d_pair, *carried)


def unpack_kernel(spans, group, channels, owners, *refs):
    chunks, expand, shrink, merge, router, vectors, grads, sems = refs
    chunk = chunks.shape[1]
    height = len(owners) * chunk // 2
    arrivals = [
        pltpu.make_async_copy(
            chunks.at[owner], grads.at[pl.ds(n * chunk, chunk)], sems.at[n]
        )
        for n, owner in enumerate(owners)
    ]
    for copy in arrivals:
        copy.start()
    for copy in arrivals:
        copy.wait()

    def block(name, rows, index):
        half, base = spans[name]
        start = half * height + base + index * rows
        return grads.at[pl.ds(start, rows)]

    features, hidden = expand.shape
    leaving = []
    for target, name in ((expand, "expand"), (merge, "merge")):
        for index in range(target.shape[1] // LANES):
            leaving.append(
                pltpu.make_async_copy(
                    block(name, features, index),
                    target.at[:, pl.ds(index * LANES, LANES)],
                    sems.at[len(owners) + len(leaving)],
                )
            )
    for copy in leaving:
        copy.start()
    for index in range(hidden // LANES):
        shrink[index * LANES : (index + 1) * LANES, :] = block("shrink", features, index)[
            ...
        ].T
    rows = 3 * group
    for index in range(features // LANES):
        values = block("router", rows, index)
        for e in range(3):
            router[
                e * channels : (e + 1) * channels, index * LANES : (index + 1) * LANES
            ] = values[e * group : e * group + channels, :]
    vectors[...] = block("expand_bias", vectors.shape[0], 0)[...]
    for copy in leaving:
        copy.wait()


def unpack(spans, group, channels, owners, features, hidden, tall, chunks):
    vmem = pl.BlockSpec(memory_space=pltpu.VMEM)
    anywhere = pl.BlockSpec(memory_space=pl.ANY)
    height = len(owners) * chunks.shape[1]
    return pl.pallas_call(
        functools.partial(unpack_kernel, spans, group, channels, owners),
        in_specs=[anywhere],
        out_specs=[anywhere, vmem, anywhere, vmem, vmem],
        out_shape=[
            jax.ShapeDtypeStruct((features, hidden), full),
            jax.ShapeDtypeStruct((hidden, features), full),
            jax.ShapeDtypeStruct((features, features), full),
            jax.ShapeDtypeStruct((3 * channels, features), full),
            jax.ShapeDtypeStruct((tall, LANES), full),
        ],
        scratch_shapes=[
            pltpu.VMEM((height, LANES), full),
            pltpu.SemaphoreType.DMA((len(owners) + (hidden + features) // LANES,)),
        ],
        compiler_params=pltpu.CompilerParams(vmem_limit_bytes=LIMIT),
        cost_estimate=pl.CostEstimate(
            flops=8 * 10**9, bytes_accessed=height * 1024, transcendentals=0
        ),
        name="unpack",
    )(chunks)


def join_kernel(group, spots, *refs):
    pieces, (out, sems) = refs[:-2], refs[-2:]
    height = pieces[0].shape[0]
    copies = []
    for mask, rows in enumerate(pieces):
        start = pl.multiple_of((spots[group] ^ mask) * height, 8)
        copies.append(
            pltpu.make_async_copy(rows, out.at[pl.ds(start, height)], sems.at[mask])
        )
    for copy in copies:
        copy.start()
    for copy in copies:
        copy.wait()


def join(group, spots, pieces):
    anywhere = pl.BlockSpec(memory_space=pl.ANY)
    return pl.pallas_call(
        functools.partial(join_kernel, group),
        in_specs=[SCALAR] + [anywhere] * len(pieces),
        out_specs=anywhere,
        out_shape=jax.ShapeDtypeStruct(
            (len(pieces) * pieces[0].shape[0], LANES), full
        ),
        scratch_shapes=[pltpu.SemaphoreType.DMA((len(pieces),))],
        compiler_params=pltpu.CompilerParams(vmem_limit_bytes=2**20),
        name="join",
    )(spots, *pieces)


def split_kernel(count, spots, *refs):
    outs = refs[-(len(refs) // (count + 1)) :]
    for mask, out in enumerate(outs):
        total = refs[mask * count][...]
        for index in range(1, count):
            total = total + refs[mask * count + index][...]
        out[...] = total


def split(group, fan, spots, terms):
    height = terms[0].shape[0] // fan

    def spec(mask):
        if fan == 1:
            return pl.BlockSpec((height, LANES), lambda i, spots: (0, 0))
        return pl.BlockSpec((height, LANES), lambda i, spots: (spots[group] ^ mask, 0))

    return pl.pallas_call(
        functools.partial(split_kernel, len(terms)),
        grid_spec=pltpu.PrefetchScalarGridSpec(
            num_scalar_prefetch=1,
            grid=(1,),
            in_specs=[spec(mask) for mask in range(fan) for _ in terms],
            out_specs=[pl.BlockSpec((height, LANES), lambda i, spots: (0, 0))] * fan,
        ),
        out_shape=[jax.ShapeDtypeStruct((height, LANES), full)] * fan,
        compiler_params=pltpu.CompilerParams(
            dimension_semantics=("arbitrary",), vmem_limit_bytes=16 * 2**20
        ),
        name="split",
    )(spots, *(list(terms) * fan))


def settle_kernel(
    places,
    owners,
    chunk,
    extra,
    side,
    leads,
    mine,
    got,
    attend,
    embed,
    vectors,
    held,
    table,
    sems,
):
    features = attend.shape[0]
    pairs = features // LANES
    arrivals = [
        pltpu.make_async_copy(mine, held.at[side[SIDES]], sems.at[0]),
        pltpu.make_async_copy(got, held.at[1 - side[SIDES]], sems.at[1]),
    ]
    for copy in arrivals:
        copy.start()
    table[...] = jnp.zeros_like(table)
    for copy in arrivals:
        copy.wait()
    stride = chunk + extra
    count = mine.shape[0] // stride
    leaving = []
    for index, (half, base) in enumerate(places):
        done = 0
        while done < features:
            at = base + done
            inside = at % chunk
            size = min(features - done, chunk - inside)
            leaving.append(
                pltpu.make_async_copy(
                    held.at[half, pl.ds(at // chunk * stride + inside, size)],
                    attend.at[pl.ds(done, size), pl.ds(index * LANES, LANES)],
                    sems.at[2 + len(leaving)],
                )
            )
            done += size
    for copy in leaving:
        copy.start()
    total = jnp.zeros((extra, LANES), full)
    row = lax.broadcasted_iota(jnp.int32, (table.shape[1], LANES), 0).astype(full)
    for half in range(2):
        for n in range(count):
            rows = held[half, n * stride + chunk : (n + 1) * stride, :]
            total = total + rows
            owner = owners[half * count + n]
            here = row == leads[owner : owner + 1, :]
            for block in range(pairs):
                at = 4 * pairs + block
                table[block] += jnp.where(here, rows[at : at + 1, :], 0.0)
    vectors[...] = total
    for block in range(pairs):
        embed[:, block * LANES : (block + 1) * LANES] = table[block]
    for copy in leaving:
        copy.wait()


def settle(places, owners, chunk, extra, leads, features, side, seen, mine, got):
    vmem = pl.BlockSpec(memory_space=pltpu.VMEM)
    anywhere = pl.BlockSpec(memory_space=pl.ANY)
    moves = 0
    for _, base in places:
        moves += (base + features - 1) // chunk - base // chunk + 1
    return pl.pallas_call(
        functools.partial(settle_kernel, places, owners, chunk, extra),
        in_specs=[SCALAR, vmem, anywhere, anywhere],
        out_specs=[anywhere, vmem, vmem],
        out_shape=[
            jax.ShapeDtypeStruct((features, 3 * features), full),
            jax.ShapeDtypeStruct((leads, features), full),
            jax.ShapeDtypeStruct((extra, LANES), full),
        ],
        scratch_shapes=[
            pltpu.VMEM((2, mine.shape[0], LANES), full),
            pltpu.VMEM((features // LANES, leads, LANES), full),
            pltpu.SemaphoreType.DMA((2 + moves,)),
        ],
        compiler_params=pltpu.CompilerParams(vmem_limit_bytes=32 * 2**20),
        name="settle",
    )(side, seen, mine, got)


def fold_kernel(count, sides, factors, *refs):
    total = refs[0][...] * factors[0]
    for index in range(1, count):
        total = total + refs[index][...] * factors[min(index, 2)]
    refs[count][...] = total


def fold(hop, hops, sides, factors, unit, terms):
    def spec(made):
        def index(i, sides, factors):
            at = i
            for step in range(made + 1, hop):
                at = at + sides[SIDES + step] * 2 ** (hops - 1 - step)
            if hop < hops:
                at = at + (1 - sides[SIDES + hop]) * 2 ** (hops - 1 - hop)
            return at, 0

        return pl.BlockSpec((unit, LANES), index)

    length = 2 ** (hops - 1 - hop) if hop < hops else 1
    return pl.pallas_call(
        functools.partial(fold_kernel, len(terms)),
        grid_spec=pltpu.PrefetchScalarGridSpec(
            num_scalar_prefetch=2,
            grid=(length,),
            in_specs=[spec(max(index - 1, 0)) for index in range(len(terms))],
            out_specs=pl.BlockSpec((unit, LANES), lambda i, *tables: (i, 0)),
        ),
        out_shape=jax.ShapeDtypeStruct((length * unit, LANES), full),
        compiler_params=pltpu.CompilerParams(
            dimension_semantics=("arbitrary",), vmem_limit_bytes=8 * 2**20
        ),
        name="fold",
    )(sides, factors, *terms)


def weights_kernel(index, frames, seen, weights, leads, held, sem):
    copy = pltpu.make_async_copy(seen.at[:, pl.ds(0, 8), :], held, sem)
    copy.start()
    total = lax.fori_loop(
        0, frames.shape[0], lambda n, sofar: sofar + frames[n], jnp.int32(0)
    ).astype(full)
    copy.wait()
    count = held.shape[0]
    rows = held[:, 0, :]
    leads[...] = rows
    device = lax.broadcasted_iota(jnp.int32, rows.shape, 0)
    for side in range(2):
        lead = jnp.max(jnp.where(device == index[side], rows, 0.0))
        same = jnp.sum(jnp.where(rows == lead, 1.0, 0.0)) / LANES
        chosen = frames[lead.astype(jnp.int32)].astype(full)
        weights[side] = chosen * count / (same * total)
    weights[2] = jnp.float32(1.0)


def weights_of(index, frames, seen):
    count = seen.shape[0]
    smem = pl.BlockSpec(memory_space=pltpu.SMEM)
    return pl.pallas_call(
        weights_kernel,
        in_specs=[smem, smem, pl.BlockSpec(memory_space=pl.ANY)],
        out_specs=[smem, pl.BlockSpec(memory_space=pltpu.VMEM)],
        out_shape=[
            jax.ShapeDtypeStruct((3,), full),
            jax.ShapeDtypeStruct((count, LANES), full),
        ],
        scratch_shapes=[
            pltpu.VMEM((count, 8, LANES), full),
            pltpu.SemaphoreType.DMA,
        ],
        compiler_params=pltpu.CompilerParams(vmem_limit_bytes=8 * 2**20),
        name="weights",
    )(index, frames, seen)


def up_to(value, step):
    return -(-value // step) * step


def tie(value, *others):
    return lax.optimization_barrier((value,) + others)[0]


def routes(sizes):
    inner = sizes["rep"]
    outer = sizes["dp"]
    if outer % 2:
        return 0, ((), ())
    far = [inner << n for n in range(1, outer.bit_length() - 1)]
    near = [1 << n for n in range(inner.bit_length() - 1)]
    even = []
    for n in range(max(len(far), len(near))):
        even += far[n : n + 1] + near[n : n + 1]
    odd = even[1:3] + even[:1] + even[3:]
    return inner, (tuple(even), tuple(odd))


SIDES = 2


class Ring:
    def __init__(self, sizes):
        self.count = sizes["dp"] * sizes["rep"]
        self.core_bit, self.orders = routes(sizes)
        self.hops = len(self.orders[0]) + 1 if self.core_bit else 0
        self.index = lax.axis_index(("dp", "rep"))

    def bits(self, hop):
        if hop == 0:
            return self.core_bit, self.core_bit
        return self.orders[0][hop - 1], self.orders[1][hop - 1]

    def swap(self, values, hop):
        pair = self.bits(hop)
        moves = [
            (i, i ^ pair[(i // self.core_bit) % 2]) for i in range(self.count)
        ]
        return lax.ppermute(values, ("dp", "rep"), moves)

    def sides(self, device):
        core = 1 if device & self.core_bit else 0
        return [
            1 if device & self.bits(hop)[core] else 0 for hop in range(self.hops)
        ]

    def scatter(self, where, factors, keep, send):
        unit = keep.shape[0] >> (self.hops - 1)
        terms = [keep]
        for hop in range(self.hops):
            if hop:
                send = fold(hop, self.hops, where, factors, unit, terms)
            got = self.swap(send, hop)
            beside = yield send
            terms.append(got if beside is None else tie(got, beside))
        return fold(self.hops, self.hops, where, factors, unit, terms)

    def owners(self):
        found = [0] * self.count
        for device in range(self.count):
            core = (device // self.core_bit) % 2
            chunk = 0
            for hop in range(self.hops):
                chunk = 2 * chunk + (1 if device & self.bits(hop)[core] else 0)
            found[chunk] = device
        return tuple(found)


class Wide:
    def __init__(self, ring):
        self.ring = ring
        order = ring.orders[0]
        even = [order[n : n + 2] for n in range(0, len(order), 2)]
        odd = list(even)
        if len(even) > 1 and len(even[1]) == 2:
            odd[0], odd[1] = even[1], even[0]
        self.groups = list(zip(even, odd))

    def place(self, device, group):
        core = 1 if device & self.ring.core_bit else 0
        spot = 0
        for bit in self.groups[group][core]:
            spot = 2 * spot + (1 if device & bit else 0)
        return spot

    def table(self):
        ring = self.ring
        rows = []
        for device in range(ring.count):
            rows.append(
                [device, device ^ ring.core_bit]
                + ring.sides(device)
                + [self.place(device, n) for n in range(len(self.groups))]
            )
        table = jnp.array(rows, jnp.int32)
        return lax.dynamic_index_in_dim(table, ring.index, 0, keepdims=False)

    def owners(self):
        found = [0] * self.ring.count
        for device in range(self.ring.count):
            chunk = 1 if device & self.ring.core_bit else 0
            for group, pair in enumerate(self.groups):
                chunk = chunk * 2 ** len(pair[0]) + self.place(device, group)
            found[chunk] = device
        return tuple(found)

    def swap(self, values, group, mask):
        ring = self.ring
        jumps = []
        for bits in self.groups[group]:
            jump = 0
            for n, bit in enumerate(reversed(bits)):
                jump |= bit if mask >> n & 1 else 0
            jumps.append(jump)
        moves = [
            (i, i ^ jumps[1 if i & ring.core_bit else 0]) for i in range(ring.count)
        ]
        return lax.ppermute(values, ("dp", "rep"), moves)

    def scatter(self, where, keep, send):
        ring = self.ring
        got = ring.swap(send, 0)
        beside = yield send
        terms = [keep, got if beside is None else tie(got, beside)]
        for group, pair in enumerate(self.groups):
            fan = 2 ** len(pair[0])
            own, *sends = split(SIDES + ring.hops + group, fan, where, terms)
            gots = [
                self.swap(values, group, mask + 1) for mask, values in enumerate(sends)
            ]
            beside = yield own
            if beside is not None:
                gots = [tie(got, beside) for got in gots]
            terms = [own] + gots
        return split(0, 1, where, terms)[0]


class Flow:
    def __init__(self, steps):
        self.steps = steps
        self.done = False
        self.sent = None
        self.result = None
        self.push(None)

    def push(self, beside):
        if self.done:
            return
        try:
            self.sent = self.steps.send(beside)
        except StopIteration as stop:
            self.done, self.sent, self.result = True, None, stop.value

    def drain(self):
        while not self.done:
            self.push(None)
        return self.result


def body(sizes, *args):
    (
        block_input,
        expert_out,
        upstream,
        lead_index,
        lead_frames,
        lead_embed,
        first_gain,
        first_shift,
        attend_weight,
        query_bias,
        value_bias,
        merge_weight,
        merge_bias,
        second_gain,
        second_shift,
        expand_weight,
        expand_bias,
        shrink_weight,
        shrink_bias,
        router_weight,
        router_bias,
        correction,
    ) = args
    rows, features = block_input.shape
    channels = correction.shape[0]
    leads = lead_embed.shape[0]
    hidden = expand_bias.shape[0]
    devices = sizes["dp"] * sizes["rep"]
    pairs = features // LANES
    grain = 4 * devices
    ring = Ring(sizes)
    wide = Wide(ring)
    where = wide.table()
    first_group = SIDES + ring.hops

    tall = max(8, 2048 // devices)
    mine = lead_index[0].astype(full)
    seen = lax.optimization_barrier(
        lax.all_gather(
            lax.optimization_barrier(jnp.full((tall, LANES), mine)), ("dp", "rep")
        )
    )
    weight, leads_seen = weights_of(
        where,
        lead_frames,
        seen,
    )

    first, projected, *own = project(
        lead_index,
        block_input,
        lead_embed,
        first_gain,
        first_shift,
        attend_weight,
        query_bias,
        value_bias,
    )
    probs, mixed, inverse = attend(projected)

    group = up_to(channels, 16)
    spans, heights = {}, [0, 0]
    for name, half, height in (
        ("expand", 0, features * hidden // LANES),
        ("merge", 0, features * features // LANES),
        ("shrink", 1, features * hidden // LANES),
        ("router", 1, features * 3 * group // LANES),
        ("expand_bias", 1, hidden // LANES),
        ("shrink_bias", 1, pairs),
        ("merge_bias", 1, pairs),
        ("second_gain", 1, pairs),
        ("second_shift", 1, pairs),
        ("head", 1, up_to(4 * group, LANES) // LANES),
    ):
        spans[name] = (half, heights[half])
        heights[half] += height
    vector_rows = up_to(heights[1] - spans["expand_bias"][1], 8)
    height = up_to(max(heights[0], spans["expand_bias"][1] + vector_rows), grain)
    tables = (
        lead_embed,
        merge_weight,
        merge_bias,
        second_gain,
        second_shift,
        expand_weight,
        expand_bias,
        shrink_weight,
        shrink_bias,
        router_weight.T,
        router_bias,
        correction,
    )
    blended, d_mid, *rest = middle(
        spans,
        height,
        group,
        where,
        lead_index,
        block_input,
        mixed,
        inverse,
        expert_out.T,
        upstream.T,
        tables,
    )
    d_across, d_down = rest[:pairs], rest[pairs : 2 * pairs]
    keep, send = rest[2 * pairs :]
    flow = None
    if ring.hops:
        flow = Flow(ring.scatter(where, weight, keep, tie(send, seen)))
        flow.push(weight)
    plan = ((4,), (2, 1, 1), (4,))
    d_query, d_pair = [], []
    for pair in range(pairs):
        carried = ()
        base = 0
        for steps in plan[pair]:
            token = where if flow is None or flow.done else tie(where, flow.sent)
            carried = attend_back(
                pair,
                base,
                steps,
                token,
                own[pair],
                d_across[pair],
                d_down[pair],
                probs,
                carried,
            )
            base += steps
            if flow is not None:
                flow.push(carried[0])
        d_query.append(carried[0])
        d_pair.append(carried[1])
    places = tuple(
        (n // 5, (n % 5) * features) for n in range(3 * pairs)
    )
    tail_height = up_to(5 * features, grain)
    now = weight if flow is None else tie(weight, flow.drain())
    tail_keep, tail_send, biases = weigh(
        places, tail_height, where, now, first, d_query, d_pair
    )
    late = None
    if ring.hops:
        late = Flow(wide.scatter(where, tail_keep, tail_send))
    carried = ()
    base = 0
    for steps in (rows // ROWS // 2,) * 2:
        now = weight if late is None else tie(weight, late.sent)
        grad_input, sums = finish(
            base,
            steps,
            lead_index,
            now,
            block_input,
            lead_embed,
            first_gain,
            attend_weight,
            d_mid,
            d_query,
            d_pair,
            carried,
        )
        base += steps
        carried = (sums, biases, grad_input)
        if late is not None:
            late.push(sums)
    extra = sums.shape[0]
    if ring.hops:
        owners = ring.owners()
        chunks = lax.all_gather(flow.result, ("dp", "rep"))
        piece = jnp.concatenate([late.drain(), sums])
        for stage in reversed(range(1, len(wide.groups))):
            fan = 2 ** len(wide.groups[stage][0])
            gots = [wide.swap(piece, stage, mask) for mask in range(1, fan)]
            piece = join(first_group + stage, where, [piece] + gots)
        gots = [
            wide.swap(piece, 0, mask) for mask in range(1, 2 ** len(wide.groups[0][0]))
        ]
        chunks = tie(chunks, piece)
        chunk = 2 * tail_height // devices
    else:
        owners = (0, 1)
        chunks = jnp.stack([keep, send]) * weight[0]
        chunk = tail_height
        piece = jnp.concatenate([tail_keep, sums])
        got = jnp.concatenate([tail_send, jnp.zeros_like(sums)])
        leads_seen = jnp.concatenate([leads_seen, leads_seen + leads])
    grad_expand, grad_shrink, grad_merge, grad_router, vectors = unpack(
        spans, group, channels, owners, features, hidden, vector_rows, chunks
    )
    first_vector = spans["expand_bias"][1]

    def take(name, length):
        start = spans[name][1] - first_vector
        return vectors[start : start + length // LANES].reshape(-1)

    head = take("head", up_to(4 * group, LANES))
    middle_vectors = (
        take("merge_bias", features),
        take("second_gain", features),
        take("second_shift", features),
        take("expand_bias", hidden),
        take("shrink_bias", features),
        head[: 3 * group].reshape(3, group)[:, :channels].reshape(-1),
        head[3 * group : 3 * group + channels],
    )
    if ring.hops:
        gots = [tie(got, vectors) for got in gots]
        piece = join(first_group, where, [piece] + gots)
        got = ring.swap(piece, 0)
        owners = wide.owners()
    grad_attend, grad_embed, small = settle(
        places,
        owners,
        chunk,
        extra,
        leads,
        features,
        where,
        leads_seen,
        piece,
        got,
    )
    small = small[: 4 * pairs].reshape(4, features)
    merge_b, gain_b, shift_b, expand_b, shrink_b, router_b, correct = middle_vectors
    return (
        blended.T,
        grad_input,
        grad_embed,
        small[0],
        small[1],
        grad_attend,
        small[2],
        small[3],
        grad_merge,
        merge_b,
        gain_b,
        shift_b,
        grad_expand,
        expand_b,
        grad_shrink,
        shrink_b,
        grad_router.T,
        router_b,
        correct,
    )


def solution(mesh):
    split = P(("dp", "rep"), None)
    sizes = dict(mesh.shape)
    return jax.shard_map(
        functools.partial(body, sizes),
        mesh=mesh,
        in_specs=(split, split, split, P(("dp", "rep"))) + (P(),) * 18,
        out_specs=(split, split) + (P(),) * 17,
        check_vma=False,
    )
```

```python
import functools

import jax
import jax.numpy as jnp
from jax import lax
from jax.experimental import pallas as pl
from jax.experimental.pallas import tpu as pltpu
from jax.sharding import PartitionSpec as P

HEADS = 6
EPSILON = 1e-05
PENALTY = 1.0
GELU_COEF = 0.7978845608028654
GELU_CUBE = 0.044715
LOG2E = 1.4426950408889634
LANES = 128
ROWS = 512
KEYS = 512
LIMIT = 56 * 2**20
BACK_LIMIT = 26 * 2**20
NORM_ROWS = 1024

low = jnp.bfloat16
full = jnp.float32


def mul(left, right, dims=((1,), (0,))):
    return lax.dot_general(left, right, (dims, ((), ())), preferred_element_type=full)


NT = ((1,), (1,))
TN = ((0,), (0,))


def params(count, limit=LIMIT):
    return pltpu.CompilerParams(
        dimension_semantics=("arbitrary",) * count, vmem_limit_bytes=limit
    )


def whole(shape):
    return pl.BlockSpec(shape, lambda *step: (0,) * len(shape))


SCALAR = pl.BlockSpec(memory_space=pltpu.SMEM)


def normalize(values):
    centre = jnp.mean(values, axis=-1, keepdims=True)
    centred = values - centre
    spread = jnp.mean(centred * centred, axis=-1, keepdims=True)
    scale = lax.rsqrt(spread + EPSILON)
    return centred * scale, scale


def norm_back(grad, unit, scale, gain):
    e = grad * gain
    first = jnp.mean(e, axis=-1, keepdims=True)
    second = jnp.mean(e * unit, axis=-1, keepdims=True)
    return scale * (e - first - unit * second)


def column_sum(values):
    return jnp.sum(values, axis=0, keepdims=True)


def project_kernel(
    lead, x, embed, gain, shift, weight, query_b, value_b, first, projected, *own
):
    stream = x[...] + embed[pl.ds(lead[0], 1), :]
    unit, _ = normalize(stream)
    rounded = (unit * gain[...][None, :] + shift[...][None, :]).astype(low)
    first[...] = rounded.T
    features = x.shape[1]
    query_row = query_b[...][None, :]
    bias = jnp.concatenate(
        [query_row, jnp.zeros_like(query_row), value_b[...][None, :]], axis=1
    )
    product = (mul(rounded, weight[...]) + bias).astype(low)
    pairs = projected.shape[0]
    for pair in range(pairs):
        for kind in range(3):
            block = kind * pairs + pair
            values = product[:, block * LANES : (block + 1) * LANES]
            projected[pair, kind] = values
            own[pair][kind] = values


def project(lead, x, embed, gain, shift, weight, query_b, value_b):
    rows, features = x.shape
    tables = (embed, gain, shift, weight, query_b, value_b)
    return pl.pallas_call(
        project_kernel,
        grid=(rows // NORM_ROWS,),
        in_specs=[SCALAR, pl.BlockSpec((NORM_ROWS, features), lambda i: (i, 0))]
        + [whole(table.shape) for table in tables],
        out_specs=[
            pl.BlockSpec((features, NORM_ROWS), lambda i: (0, i)),
            pl.BlockSpec((features // LANES, 3, NORM_ROWS, LANES), lambda i: (0, 0, i, 0)),
        ]
        + [pl.BlockSpec((3, NORM_ROWS, LANES), lambda i: (0, i, 0))] * (features // LANES),
        out_shape=[
            jax.ShapeDtypeStruct((features, rows), low),
            jax.ShapeDtypeStruct((features // LANES, 3, rows, LANES), low),
        ]
        + [jax.ShapeDtypeStruct((3, rows, LANES), low)] * (features // LANES),
        compiler_params=params(1),
        name="project",
    )(lead, x, *tables)


def attend_kernel(size, q, k, v, probs, mixed, inverse, turned):
    keys = k.shape[2]
    count = q.shape[2]
    scaling = size ** (-0.5) * LOG2E

    @pl.when(pl.program_id(1) == 0)
    def _():
        across = v[0, 0].T
        tail = lax.broadcasted_iota(jnp.int32, (16, keys), 0)
        ones = jnp.where(tail == 0, 1.0, 0.0).astype(low)
        for head in range(2):
            turned[head, 0:size, :] = across[head * size : (head + 1) * size, :]
            turned[head, size : size + 16, :] = ones

    lane = lax.broadcasted_iota(jnp.int32, (1, LANES), 1)

    def scores(head, start):
        mask = jnp.where(lane // size == head, 1.0, 0.0).astype(low)
        return mul(k[0, 0, start : start + keys, :], q[0, 0] * mask, NT) * scaling

    def finish(head, total):
        spread = total[size : size + 1, :]
        inv = 1.0 / spread
        inverse[0, head : head + 1, :] = inv
        mixed[head * size : (head + 1) * size, :] = (total[0:size, :] * inv).astype(low)
        return spread

    extremes = []
    for head in range(2):
        total = jnp.zeros((size + 16, count), full)
        for start in (0,):
            p = jnp.exp2(scores(head, start)).astype(low)
            probs[0, head, start : start + keys, :] = p
            total = total + mul(turned[head, :, start : start + keys], p)
        spread = finish(head, total)
        extremes.append(spread)

    both = jnp.concatenate(extremes, axis=0)
    inside = jnp.where((both > 1e-18) & (both < 1e18), 1.0, 0.0)

    @pl.when(jnp.min(inside) < 0.5)
    def _():
        for head in range(2):
            top = jnp.full((1, count), -jnp.inf, full)
            for start in (0,):
                top = jnp.maximum(
                    top, jnp.max(scores(head, start), axis=0, keepdims=True)
                )
            total = jnp.zeros((size + 16, count), full)
            for start in (0,):
                p = jnp.exp2(scores(head, start) - top).astype(low)
                probs[0, head, start : start + keys, :] = p
                total = total + mul(turned[head, :, start : start + keys], p)
            finish(head, total)


def attend(projected):
    pairs, _, rows, _ = projected.shape
    features = pairs * LANES
    size = features // HEADS
    return pl.pallas_call(
        functools.partial(attend_kernel, size),
        grid=(pairs, rows // ROWS),
        in_specs=[
            pl.BlockSpec((1, 1, ROWS, LANES), lambda p, i: (p, 0, i, 0)),
            pl.BlockSpec((1, 1, rows, LANES), lambda p, i: (p, 1, 0, 0)),
            pl.BlockSpec((1, 1, rows, LANES), lambda p, i: (p, 2, 0, 0)),
        ],
        out_specs=[
            pl.BlockSpec((1, 2, rows, ROWS), lambda p, i: (p, 0, 0, i)),
            pl.BlockSpec((LANES, ROWS), lambda p, i: (p, i)),
            pl.BlockSpec((1, 8, ROWS), lambda p, i: (p, 0, i)),
        ],
        out_shape=[
            jax.ShapeDtypeStruct((pairs, 2, rows, rows), low),
            jax.ShapeDtypeStruct((features, rows), low),
            jax.ShapeDtypeStruct((pairs, 8, rows), full),
        ],
        scratch_shapes=[pltpu.VMEM((2, size + 16, rows), low)],
        compiler_params=params(2),
        name="attend",
    )(projected, projected, projected)


def middle_kernel(
    spans,
    size,
    group,
    side,
    lead,
    x,
    mixed,
    inverse,
    experts,
    upstream,
    embed,
    merge_w,
    merge_b,
    gain,
    shift,
    expand_w,
    expand_b,
    shrink_w,
    shrink_b,
    router_in,
    router_b,
    correct,
    blended,
    d_mid,
    *rest,
):
    pairs = x.shape[1] // LANES
    d_across, d_down = rest[:pairs], rest[pairs : 2 * pairs]
    keep, send, grads, lanes, router_w, columns, sems = rest[2 * pairs :]
    features = x.shape[1]
    step = x.shape[0]
    hidden_size = expand_w.shape[1]
    channels = upstream.shape[0]
    chunk = hidden_size // 2

    @pl.when(pl.program_id(0) == 0)
    def _():
        grads[...] = jnp.zeros_like(grads)
        lanes[...] = jnp.zeros_like(lanes)
        weights = router_in[...].astype(full)
        wide = up_to(3 * channels, LANES)

        def down(row, width):
            row = jnp.concatenate(
                [row, jnp.zeros((1, width - row.shape[1]), full)], axis=1
            )
            return jnp.broadcast_to(row, (8, width)).T

        biases = down(router_b[...][None, :], wide)
        columns[...] = jnp.zeros_like(columns)
        for e in range(3):
            rows = slice(e * channels, (e + 1) * channels)
            router_w[e * group : (e + 1) * group, :] = jnp.concatenate(
                [weights[rows, :], jnp.zeros((group - channels, features), full)],
                axis=0,
            ).astype(low)
            columns[e * group : e * group + channels, 0:8] = biases[rows, :]
        columns[0:channels, 8:16] = down(correct[...][None, :], LANES)[:channels, :]

    def add(name, values, part=0):
        half, base = spans[name]
        height = values.shape[0]
        for block in range(values.shape[1] // LANES):
            start = base + (part + block) * height
            grads[half, start : start + height, :] += values[
                :, block * LANES : (block + 1) * LANES
            ]

    stream = x[...] + embed[pl.ds(lead[0], 1), :]
    mid = stream + mul(mixed[...], merge_w[...], TN) + merge_b[...][None, :]
    unit, scale = normalize(mid)
    gain_row = gain[...][None, :]
    second = (unit * gain_row + shift[...][None, :]).astype(low)
    output = mid + shrink_b[...][None, :]
    bias = expand_b[...][None, :]
    hidden, slope = [], []
    for start in range(0, hidden_size, chunk):
        part = slice(start, start + chunk)
        u = mul(second, expand_w[:, part]) + bias[:, part]
        square = u * u
        t = jnp.tanh(u * (GELU_COEF + GELU_COEF * GELU_CUBE * square))
        half = 0.5 + 0.5 * t
        act = u * half
        slope.append(
            half
            + act
            * (1.0 - half)
            * (2.0 * GELU_COEF + 6.0 * GELU_COEF * GELU_CUBE * square)
        )
        act = act.astype(low)
        hidden.append(act)
        output = output + mul(act, shrink_w[part, :])
    output_low = output.astype(low)
    logits = mul(router_w[...], output_low, NT) + columns[:, 0:1]
    valid = lax.broadcasted_iota(jnp.int32, (group, 1), 0) < channels
    parts = [logits[e * group : (e + 1) * group, :] for e in range(3)]
    largest = jnp.maximum(jnp.maximum(parts[0], parts[1]), parts[2])
    parts = [part - largest for part in parts]
    raised = [jnp.exp(part) for part in parts]
    total = raised[0] + raised[1] + raised[2]
    shared = jnp.log(total)
    logs = [part - shared for part in parts]
    share = 1.0 / total
    gates = [value * share for value in raised]

    def widen(values):
        return jnp.concatenate(
            [values, jnp.zeros((group - channels, step), full)], axis=0
        )

    frames = [
        widen(experts[e * channels : (e + 1) * channels, :]) for e in range(3)
    ]
    up = widen(upstream[...])
    mix = gates[0] * frames[0] + gates[1] * frames[1] + gates[2] * frames[2]
    entropy = -(gates[0] * logs[0] + gates[1] * logs[1] + gates[2] * logs[2])
    blended[...] = mix[:channels, :] + columns[:channels, 8:9]
    d_parts = [
        jnp.where(
            valid,
            gates[e] * (up * (frames[e] - mix) - PENALTY * (logs[e] + entropy)),
            0.0,
        )
        for e in range(3)
    ]
    for index, values in enumerate(d_parts + [up]):
        for start in range(0, step, LANES):
            lanes[index * group : (index + 1) * group, :] += values[
                :, start : start + LANES
            ]
    d_logits_low = jnp.concatenate(d_parts, axis=0).astype(low)
    add("router", mul(d_logits_low, output_low))
    d_output = mul(d_logits_low, router_w[...], TN)
    add("shrink_bias", column_sum(d_output))
    d_output_low = d_output.astype(low)
    d_turned = d_output_low.T
    second_turned = second.T
    d_second = jnp.zeros_like(d_output)
    for index, start in enumerate(range(0, hidden_size, chunk)):
        part = slice(start, start + chunk)
        d_pre = mul(d_output_low, shrink_w[part, :], NT) * slope[index]
        add("expand_bias", column_sum(d_pre), start // LANES)
        d_pre_low = d_pre.astype(low)
        d_second = d_second + mul(d_pre_low, expand_w[:, part], NT)
        add("expand", mul(second_turned, d_pre_low), start // LANES)
        add("shrink", mul(d_turned, hidden[index]), start // LANES)
    add("second_gain", column_sum(d_second * unit))
    add("second_shift", column_sum(d_second))
    grad_mid = d_output + norm_back(d_second, unit, scale, gain_row)
    d_mid[...] = grad_mid
    add("merge_bias", column_sum(grad_mid))
    d_mid_low = grad_mid.astype(low)
    add("merge", mul(mixed[...], d_mid_low))
    d_mixed = mul(merge_w[...], d_mid_low, NT).astype(low).astype(full)
    row = lax.broadcasted_iota(jnp.int32, (size, step), 0)
    stack = []
    for head in range(features // size):
        span = slice(head * size, (head + 1) * size)
        odd = head % 2
        inv = inverse[head // 2, odd : odd + 1, :]
        scaled = (d_mixed[span, :] * inv).astype(low)
        stack.append(scaled)
        centre = -column_sum(scaled.astype(full) * mixed[span, :].astype(full))
        one = centre.astype(low).astype(full)
        two = (centre - one).astype(low).astype(full)
        extra = jnp.where(
            row == 0,
            one,
            jnp.where(row == 1, two, jnp.where(row == 2, centre - one - two, 0.0)),
        ).astype(low)
        across = d_across[head // 2]
        across[odd, odd * size : (odd + 1) * size, :] = scaled
        across[odd, (1 - odd) * size : (2 - odd) * size, :] = extra
    for pair in range(pairs):
        d_down[pair][...] = jnp.concatenate(stack[2 * pair : 2 * pair + 2], axis=0).T

    @pl.when(pl.program_id(0) == pl.num_programs(0) - 1)
    def _():
        sums = column_sum(lanes[...].T)
        width = sums.shape[1]
        wide = up_to(width, LANES)
        sums = jnp.concatenate([sums, jnp.zeros((1, wide - width), full)], axis=1)
        add("head", sums)
        copies = [
            pltpu.make_async_copy(grads.at[side[SIDES]], keep, sems.at[0]),
            pltpu.make_async_copy(grads.at[1 - side[SIDES]], send, sems.at[1]),
        ]
        for copy in copies:
            copy.start()
        for copy in copies:
            copy.wait()


def middle(spans, height, group, side, lead, x, mixed, inverse, experts, upstream, tables):
    rows, features = x.shape
    size = features // HEADS
    channels = upstream.shape[0]
    step = ROWS
    pairs = features // LANES
    anywhere = pl.BlockSpec(memory_space=pl.ANY)
    return pl.pallas_call(
        functools.partial(middle_kernel, spans, size, group),
        grid=(rows // step,),
        in_specs=[
            SCALAR,
            SCALAR,
            pl.BlockSpec((step, features), lambda i: (i, 0)),
            pl.BlockSpec((features, step), lambda i: (0, i)),
            pl.BlockSpec((inverse.shape[0], 8, step), lambda i: (0, 0, i)),
            pl.BlockSpec((experts.shape[0], step), lambda i: (0, i)),
            pl.BlockSpec((channels, step), lambda i: (0, i)),
        ]
        + [whole(table.shape) for table in tables],
        out_specs=[
            pl.BlockSpec((channels, step), lambda i: (0, i)),
            pl.BlockSpec((step, features), lambda i: (i, 0)),
        ]
        + [pl.BlockSpec((2, LANES, step), lambda i: (0, 0, i))] * pairs
        + [pl.BlockSpec((step, LANES), lambda i: (i, 0))] * pairs
        + [anywhere, anywhere],
        out_shape=[
            jax.ShapeDtypeStruct((channels, rows), full),
            jax.ShapeDtypeStruct((rows, features), full),
        ]
        + [jax.ShapeDtypeStruct((2, LANES, rows), low)] * pairs
        + [jax.ShapeDtypeStruct((rows, LANES), low)] * pairs
        + [jax.ShapeDtypeStruct((height, LANES), full)] * 2,
        scratch_shapes=[
            pltpu.VMEM((2, height, LANES), full),
            pltpu.VMEM((4 * group, LANES), full),
            pltpu.VMEM((3 * group, features), low),
            pltpu.VMEM((3 * group, LANES), full),
            pltpu.SemaphoreType.DMA((2,)),
        ],
        compiler_params=params(1),
        name="middle",
    )(side, lead, x, mixed, inverse, experts, upstream, *tables)


def attend_back_kernel(size, pair, base, steps, last_part, ahead, token, *refs):
    refs = refs[ahead:]
    if base == 0:
        projected, d_across, d_down, probs, d_query, d_pair, total, held, sems = refs
        carry = None
    else:
        projected, d_across, d_down, probs, carry, earlier, *refs = refs
        d_query, d_pair, total, held, sems = refs
        d_pair[:, : base * KEYS, :] = earlier[:, : base * KEYS, :]
    rows = d_down.shape[0]
    scaling = size ** (-0.5)
    lane = lax.broadcasted_iota(jnp.int32, (1, LANES), 1)

    def fetch(step, slot):
        return pltpu.make_async_copy(
            probs.at[pair, :, pl.ds((base + step) * KEYS, KEYS), :],
            held.at[slot],
            sems.at[slot],
        )

    fetch(0, 0).start()
    total[...] = jnp.zeros_like(total) if carry is None else carry[...]

    def one_step(step, unused):
        slot = lax.rem(step, 2)

        @pl.when(step + 1 < steps)
        def _():
            fetch(step + 1, 1 - slot).start()

        fetch(step, slot).wait()
        at = pl.ds(pl.multiple_of((base + step) * KEYS, KEYS), KEYS)
        v = projected[2, at, :]
        k_across = projected[1, at, :].T
        d_keys, d_values = [], []
        for head in range(2):
            other = (1 - head) * size
            data = jnp.where(lane // size == head, 1.0, 0.0).astype(low)
            ones = jnp.where((lane >= other) & (lane < other + 3), 1.0, 0.0)
            values = v * data + ones.astype(low)
            p = held[slot, head]
            d_p = mul(values, d_across[head])
            d_s = (p.astype(full) * d_p).astype(low)
            span = slice(head * size, (head + 1) * size)
            total[span, :] += mul(k_across[span, :], d_s)
            d_values.append(mul(p, d_down[...]))
            d_keys.append(mul(d_s, projected[0]))
        d_pair[0, at, :] = (jnp.where(lane < size, *d_keys) * scaling).astype(low)
        d_pair[1, at, :] = jnp.where(lane < size, *d_values).astype(low)
        return unused

    lax.fori_loop(0, steps, one_step, 0)
    if last_part:
        d_query[...] = (total[...].T * scaling).astype(low)
    else:
        d_query[...] = total[...]


def attend_back(
    pair, base, steps, token, ahead, projected, d_across, d_down, probs, carried
):
    rows = d_down.shape[0]
    size = LANES // 2
    all_steps = rows // KEYS
    last_part = base + steps == all_steps
    across = (rows, LANES) if last_part else (LANES, rows)
    vmem = pl.BlockSpec(memory_space=pltpu.VMEM)
    return pl.pallas_call(
        functools.partial(
            attend_back_kernel, size, pair, base, steps, last_part, len(ahead)
        ),
        in_specs=[SCALAR]
        + [vmem] * len(ahead)
        + [vmem, vmem, vmem, pl.BlockSpec(memory_space=pl.ANY)]
        + [vmem] * len(carried),
        out_specs=[vmem, vmem],
        out_shape=[
            jax.ShapeDtypeStruct(across, low if last_part else full),
            jax.ShapeDtypeStruct((2, rows, LANES), low),
        ],
        scratch_shapes=[
            pltpu.VMEM((LANES, rows), full),
            pltpu.VMEM((2, 2, KEYS, rows), low),
            pltpu.SemaphoreType.DMA((2,)),
        ],
        compiler_params=pltpu.CompilerParams(vmem_limit_bytes=BACK_LIMIT),
        cost_estimate=pl.CostEstimate(
            flops=10 * rows * rows * 256 * steps // all_steps,
            bytes_accessed=rows * rows * 4 * steps // all_steps,
            transcendentals=0,
        ),
        name="attend_back",
    )(token, *ahead, projected, d_across, d_down, probs, *carried)


def weigh_kernel(pairs, places, side, weight, first, *refs):
    d_query, d_pair = refs[:pairs], refs[pairs : 2 * pairs]
    keep, send, sums, grads, sems = refs[2 * pairs :]
    features = first.shape[0]
    grads[...] = jnp.zeros_like(grads)
    sums[...] = jnp.zeros_like(sums)
    parts = []
    for kind in range(3):
        for pair in range(pairs):
            values = d_query[pair][...] if kind == 0 else d_pair[pair][kind - 1]
            parts.append(values)
            if kind != 1:
                sums[
                    kind // 2 : kind // 2 + 1, pair * LANES : (pair + 1) * LANES
                ] = weight[0] * column_sum(values.astype(full))
    for start in range(0, len(parts), 2):
        some = parts[start : start + 2]
        product = mul(first[...], jnp.concatenate(some, axis=1)) * weight[0]
        for index in range(len(some)):
            half, base = places[start + index]
            grads[half, base : base + features, :] = product[
                :, index * LANES : (index + 1) * LANES
            ]
    copies = [
        pltpu.make_async_copy(grads.at[side[SIDES]], keep, sems.at[0]),
        pltpu.make_async_copy(grads.at[1 - side[SIDES]], send, sems.at[1]),
    ]
    for copy in copies:
        copy.start()
    for copy in copies:
        copy.wait()


def weigh(places, height, side, weight, first, d_query, d_pair):
    features = first.shape[0]
    vmem = pl.BlockSpec(memory_space=pltpu.VMEM)
    anywhere = pl.BlockSpec(memory_space=pl.ANY)
    pairs = len(d_query)
    return pl.pallas_call(
        functools.partial(weigh_kernel, pairs, places),
        in_specs=[SCALAR, SCALAR, vmem] + [vmem] * (2 * pairs),
        out_specs=[anywhere, anywhere, vmem],
        out_shape=[
            jax.ShapeDtypeStruct((height, LANES), full),
            jax.ShapeDtypeStruct((height, LANES), full),
            jax.ShapeDtypeStruct((8, features), full),
        ],
        scratch_shapes=[
            pltpu.VMEM((2, height, LANES), full),
            pltpu.SemaphoreType.DMA((2,)),
        ],
        compiler_params=pltpu.CompilerParams(vmem_limit_bytes=20 * 2**20),
        cost_estimate=pl.CostEstimate(
            flops=18 * d_query[0].shape[0] * features * features,
            bytes_accessed=d_query[0].shape[0] * features * 8,
            transcendentals=0,
        ),
        name="weigh",
    )(side, weight, first, *d_query, *d_pair)


def finish_kernel(pairs, last_part, lead, weight, x, embed, gain, wide, d_mid, *rest):
    d_query, d_pair, rest = rest[:pairs], rest[pairs : 2 * pairs], rest[2 * pairs :]
    if last_part:
        earlier, biases, _, grad_input, vectors, sums = rest
    else:
        grad_input, sums = rest
    step = pl.program_id(0)

    @pl.when(step == 0)
    def _():
        sums[...] = earlier[...] if last_part else jnp.zeros_like(sums)

    stream = x[...] + embed[pl.ds(lead[0], 1), :]
    unit, scale = normalize(stream)
    parts = []
    for kind in range(3):
        for pair in range(pairs):
            parts.append(d_query[pair][...] if kind == 0 else d_pair[pair][kind - 1])
    d_first = mul(jnp.concatenate(parts, axis=1), wide[...], NT)
    d_stream = (
        d_mid[...] + norm_back(d_first, unit, scale, gain[...][None, :])
    ) * weight[0]
    grad_input[...] = d_stream
    sums[0:1, :] += column_sum(d_first * unit) * weight[0]
    sums[1:2, :] += column_sum(d_first) * weight[0]
    sums[2:3, :] += column_sum(d_stream)

    if last_part:

        @pl.when(step == pl.num_programs(0) - 1)
        def _():
            vectors[...] = jnp.zeros_like(vectors)
            for index, (ref, at) in enumerate(
                ((sums, 0), (sums, 1), (biases, 0), (biases, 1), (sums, 2))
            ):
                for block in range(pairs):
                    row = index * pairs + block
                    vectors[row : row + 1, :] = ref[
                        at : at + 1, block * LANES : (block + 1) * LANES
                    ]


def finish(base, steps, lead, weight, x, embed, gain, wide, d_mid, d_query, d_pair, carried):
    rows, features = x.shape
    pairs = len(d_query)
    total = rows // ROWS
    last_part = base + steps == total
    height = up_to(5 * pairs, 8)
    row_spec = pl.BlockSpec((ROWS, features), lambda i: (base + i, 0))
    small = pl.BlockSpec((8, features), lambda i: (0, 0))
    return pl.pallas_call(
        functools.partial(finish_kernel, pairs, last_part),
        grid=(steps,),
        in_specs=[
            SCALAR,
            SCALAR,
            row_spec,
            whole(embed.shape),
            whole(gain.shape),
            whole(wide.shape),
            row_spec,
        ]
        + [pl.BlockSpec((ROWS, LANES), lambda i: (base + i, 0))] * pairs
        + [pl.BlockSpec((2, ROWS, LANES), lambda i: (0, base + i, 0))] * pairs
        + ([small, small, pl.BlockSpec(memory_space=pl.ANY)] if last_part else []),
        out_specs=[row_spec, whole((height, LANES)) if last_part else small],
        out_shape=[
            jax.ShapeDtypeStruct((rows, features), full),
            jax.ShapeDtypeStruct((height, LANES) if last_part else (8, features), full),
        ],
        scratch_shapes=[pltpu.VMEM((8, features), full)] if last_part else [],
        input_output_aliases={9 + 2 * pairs: 0} if last_part else {},
        compiler_params=params(1),
        cost_estimate=pl.CostEstimate(
            flops=6 * rows * features * features * steps // total,
            bytes_accessed=rows * features * 18 * steps // total,
            transcendentals=0,
        ),
        name="finish",
    )(lead, weight, x, embed, gain, wide, d_mid, *d_query, *d_pair, *carried)


def pieces_of(start, height, chunk):
    found = []
    done = 0
    while done < height:
        at = start + done
        inside = at % chunk
        size = min(height - done, chunk - inside)
        found.append((at // chunk, inside, done, size))
        done += size
    return found


def unpack_kernel(spans, group, channels, owners, *refs):
    chunks, expand, shrink, merge, router, vectors, grads, turned, sems = refs
    chunk = chunks.shape[1]
    half = len(owners) // 2
    features, hidden = expand.shape
    copies = []

    def copy(source, target):
        copies.append(pltpu.make_async_copy(source, target, sems.at[len(copies)]))
        copies[-1].start()
        return copies[-1]

    arrivals = [
        copy(chunks.at[owner], grads.at[pl.ds(n * chunk, chunk)])
        for n, owner in enumerate(owners)
    ]
    here = 0
    for target, name in ((expand, "expand"), (merge, "merge")):
        for index in range(target.shape[1] // LANES):
            base = spans[name][1] + index * features
            while here * chunk < base + features:
                arrivals[here].wait()
                here += 1
            copy(
                grads.at[pl.ds(base, features)],
                target.at[:, pl.ds(index * LANES, LANES)],
            )
    for index in range(hidden // LANES):
        base = half * chunk + spans["shrink"][1] + index * features
        while here * chunk < base + features:
            arrivals[here].wait()
            here += 1
        rows = pl.ds(index * LANES, LANES)
        turned[rows, :] = grads[base : base + features, :].T
        copy(turned.at[rows], shrink.at[rows])
    for arrival in arrivals[here:]:
        arrival.wait()
    rows = 3 * group
    for index in range(features // LANES):
        base = half * chunk + spans["router"][1] + index * rows
        for e in range(3):
            start = base + e * group
            router[
                e * channels : (e + 1) * channels, index * LANES : (index + 1) * LANES
            ] = grads[start : start + channels, :]
    first = half * chunk + spans["expand_bias"][1]
    vectors[...] = grads[first : first + vectors.shape[0], :]
    for last in copies[len(owners) :]:
        last.wait()


def unpack(spans, group, channels, owners, features, hidden, tall, chunks):
    vmem = pl.BlockSpec(memory_space=pltpu.VMEM)
    anywhere = pl.BlockSpec(memory_space=pl.ANY)
    chunk = chunks.shape[1]
    half = len(owners) // 2
    moves = len(owners) + (2 * hidden + features) // LANES
    return pl.pallas_call(
        functools.partial(unpack_kernel, spans, group, channels, owners),
        in_specs=[anywhere],
        out_specs=[anywhere, anywhere, anywhere, vmem, vmem],
        out_shape=[
            jax.ShapeDtypeStruct((features, hidden), full),
            jax.ShapeDtypeStruct((hidden, features), full),
            jax.ShapeDtypeStruct((features, features), full),
            jax.ShapeDtypeStruct((3 * channels, features), full),
            jax.ShapeDtypeStruct((tall, LANES), full),
        ],
        scratch_shapes=[
            pltpu.VMEM((2 * half * chunk, LANES), full),
            pltpu.VMEM((hidden, features), full),
            pltpu.SemaphoreType.DMA((moves,)),
        ],
        compiler_params=pltpu.CompilerParams(vmem_limit_bytes=LIMIT),
        cost_estimate=pl.CostEstimate(
            flops=8 * 10**9, bytes_accessed=half * chunk * 2048, transcendentals=0
        ),
        name="unpack",
    )(chunks)


def join_kernel(group, spots, *refs):
    pieces, (out, sems) = refs[:-2], refs[-2:]
    height = pieces[0].shape[0]
    copies = []
    for mask, rows in enumerate(pieces):
        start = pl.multiple_of((spots[group] ^ mask) * height, 8)
        copies.append(
            pltpu.make_async_copy(rows, out.at[pl.ds(start, height)], sems.at[mask])
        )
    for copy in copies:
        copy.start()
    for copy in copies:
        copy.wait()


def join(group, spots, pieces):
    anywhere = pl.BlockSpec(memory_space=pl.ANY)
    return pl.pallas_call(
        functools.partial(join_kernel, group),
        in_specs=[SCALAR] + [anywhere] * len(pieces),
        out_specs=anywhere,
        out_shape=jax.ShapeDtypeStruct(
            (len(pieces) * pieces[0].shape[0], LANES), full
        ),
        scratch_shapes=[pltpu.SemaphoreType.DMA((len(pieces),))],
        compiler_params=pltpu.CompilerParams(vmem_limit_bytes=2**20),
        name="join",
    )(spots, *pieces)


def split_kernel(count, spots, *refs):
    outs = refs[-(len(refs) // (count + 1)) :]
    for mask, out in enumerate(outs):
        total = refs[mask * count][...]
        for index in range(1, count):
            total = total + refs[mask * count + index][...]
        out[...] = total


def split(group, fan, spots, terms):
    height = terms[0].shape[0] // fan

    def spec(mask):
        if fan == 1:
            return pl.BlockSpec((height, LANES), lambda i, spots: (0, 0))
        return pl.BlockSpec((height, LANES), lambda i, spots: (spots[group] ^ mask, 0))

    return pl.pallas_call(
        functools.partial(split_kernel, len(terms)),
        grid_spec=pltpu.PrefetchScalarGridSpec(
            num_scalar_prefetch=1,
            grid=(1,),
            in_specs=[spec(mask) for mask in range(fan) for _ in terms],
            out_specs=[pl.BlockSpec((height, LANES), lambda i, spots: (0, 0))] * fan,
        ),
        out_shape=[jax.ShapeDtypeStruct((height, LANES), full)] * fan,
        compiler_params=pltpu.CompilerParams(
            dimension_semantics=("arbitrary",), vmem_limit_bytes=16 * 2**20
        ),
        name="split",
    )(spots, *(list(terms) * fan))


def settle_kernel(places, owners, extra, side, leads, mine, got, *refs):
    attend, embed, vectors, held, table, sems = refs
    features = attend.shape[0]
    pairs = features // LANES
    count, stride, _ = mine.shape
    chunk = stride - extra

    def run(halves):
        arrivals = []
        for half in range(2):
            arrivals.append(
                pltpu.make_async_copy(
                    halves[half].at[:, pl.ds(chunk, extra), :],
                    held.at[half],
                    sems.at[half],
                )
            )
        leaving = []
        for index, (half, base) in enumerate(places):
            for n, inside, done, size in pieces_of(base, features, chunk):
                leaving.append(
                    pltpu.make_async_copy(
                        halves[half].at[n, pl.ds(inside, size)],
                        attend.at[pl.ds(done, size), pl.ds(index * LANES, LANES)],
                        sems.at[2 + len(leaving)],
                    )
                )
        for copy in arrivals + leaving:
            copy.start()
        table[...] = jnp.zeros_like(table)
        for copy in arrivals:
            copy.wait()
        total = jnp.zeros((extra, LANES), full)
        row = lax.broadcasted_iota(jnp.int32, (table.shape[1], LANES), 0).astype(full)
        for half in range(2):
            for n in range(count):
                rows = held[half, n]
                total = total + rows
                owner = owners[half * count + n]
                here = row == leads[owner : owner + 1, :]
                for block in range(pairs):
                    at = 4 * pairs + block
                    table[block] += jnp.where(here, rows[at : at + 1, :], 0.0)
        vectors[...] = total
        for block in range(pairs):
            embed[:, block * LANES : (block + 1) * LANES] = table[block]
        for copy in leaving:
            copy.wait()

    @pl.when(side[SIDES] == 0)
    def _():
        run((mine, got))

    @pl.when(side[SIDES] != 0)
    def _():
        run((got, mine))


def settle(places, owners, chunk, extra, leads, features, side, seen, mine, got):
    vmem = pl.BlockSpec(memory_space=pltpu.VMEM)
    anywhere = pl.BlockSpec(memory_space=pl.ANY)
    count = mine.shape[0] // (chunk + extra)
    moves = sum(len(pieces_of(base, features, chunk)) for _, base in places)
    return pl.pallas_call(
        functools.partial(settle_kernel, places, owners, extra),
        in_specs=[SCALAR, vmem, anywhere, anywhere],
        out_specs=[anywhere, vmem, vmem],
        out_shape=[
            jax.ShapeDtypeStruct((features, 3 * features), full),
            jax.ShapeDtypeStruct((leads, features), full),
            jax.ShapeDtypeStruct((extra, LANES), full),
        ],
        scratch_shapes=[
            pltpu.VMEM((2, count, extra, LANES), full),
            pltpu.VMEM((features // LANES, leads, LANES), full),
            pltpu.SemaphoreType.DMA((2 + moves,)),
        ],
        compiler_params=pltpu.CompilerParams(vmem_limit_bytes=32 * 2**20),
        name="settle",
    )(
        side,
        seen,
        mine.reshape(count, chunk + extra, LANES),
        got.reshape(count, chunk + extra, LANES),
    )


def fold_kernel(count, sides, factors, *refs):
    total = refs[0][...] * factors[0]
    for index in range(1, count):
        total = total + refs[index][...] * factors[min(index, 2)]
    refs[count][...] = total


def fold(hop, hops, sides, factors, unit, terms):
    def spec(made):
        def index(i, sides, factors):
            at = i
            for step in range(made + 1, hop):
                at = at + sides[SIDES + step] * 2 ** (hops - 1 - step)
            if hop < hops:
                at = at + (1 - sides[SIDES + hop]) * 2 ** (hops - 1 - hop)
            return at, 0

        return pl.BlockSpec((unit, LANES), index)

    length = 2 ** (hops - 1 - hop) if hop < hops else 1
    return pl.pallas_call(
        functools.partial(fold_kernel, len(terms)),
        grid_spec=pltpu.PrefetchScalarGridSpec(
            num_scalar_prefetch=2,
            grid=(length,),
            in_specs=[spec(max(index - 1, 0)) for index in range(len(terms))],
            out_specs=pl.BlockSpec((unit, LANES), lambda i, *tables: (i, 0)),
        ),
        out_shape=jax.ShapeDtypeStruct((length * unit, LANES), full),
        compiler_params=pltpu.CompilerParams(
            dimension_semantics=("arbitrary",), vmem_limit_bytes=8 * 2**20
        ),
        name="fold",
    )(sides, factors, *terms)


def weights_kernel(index, frames, near, seen, weights, leads, held, sem):
    copy = pltpu.make_async_copy(seen.at[:, pl.ds(0, 8), :], held, sem)
    copy.start()
    total = lax.fori_loop(
        0, frames.shape[0], lambda n, sofar: sofar + frames[n], jnp.int32(0)
    ).astype(full)
    copy.wait()
    count = held.shape[0]
    rows = held[:, 0, :]
    leads[...] = rows
    device = lax.broadcasted_iota(jnp.int32, rows.shape, 0)
    for side in range(2):
        lead = jnp.max(jnp.where(device == index[side], rows, 0.0))
        same = jnp.sum(jnp.where(rows == lead, 1.0, 0.0)) / LANES
        chosen = frames[lead.astype(jnp.int32)].astype(full)
        weights[side] = chosen * count / (same * total)
    weights[2] = jnp.float32(1.0)


def weights_of(index, frames, near, seen):
    count = seen.shape[0]
    smem = pl.BlockSpec(memory_space=pltpu.SMEM)
    return pl.pallas_call(
        weights_kernel,
        in_specs=[
            smem,
            smem,
            pl.BlockSpec(memory_space=pltpu.VMEM),
            pl.BlockSpec(memory_space=pl.ANY),
        ],
        out_specs=[smem, pl.BlockSpec(memory_space=pltpu.VMEM)],
        out_shape=[
            jax.ShapeDtypeStruct((3,), full),
            jax.ShapeDtypeStruct((count, LANES), full),
        ],
        scratch_shapes=[
            pltpu.VMEM((count, 8, LANES), full),
            pltpu.SemaphoreType.DMA,
        ],
        compiler_params=pltpu.CompilerParams(vmem_limit_bytes=8 * 2**20),
        name="weights",
    )(index, frames, near, seen)


def up_to(value, step):
    return -(-value // step) * step


def tie(value, *others):
    return lax.optimization_barrier((value,) + others)[0]


def routes(sizes):
    inner = sizes["rep"]
    outer = sizes["dp"]
    if outer % 2:
        return 0, ((), ())
    far = [inner << n for n in range(1, outer.bit_length() - 1)]
    near = [1 << n for n in range(inner.bit_length() - 1)]
    even = []
    for n in range(max(len(far), len(near))):
        even += far[n : n + 1] + near[n : n + 1]
    odd = even[1:3] + even[:1] + even[3:]
    return inner, (tuple(even), tuple(odd))


SIDES = 2


class Ring:
    def __init__(self, sizes):
        self.count = sizes["dp"] * sizes["rep"]
        self.core_bit, self.orders = routes(sizes)
        self.hops = len(self.orders[0]) + 1 if self.core_bit else 0
        self.index = lax.axis_index(("dp", "rep"))

    def bits(self, hop):
        if hop == 0:
            return self.core_bit, self.core_bit
        return self.orders[0][hop - 1], self.orders[1][hop - 1]

    def swap(self, values, hop):
        pair = self.bits(hop)
        moves = [
            (i, i ^ pair[(i // self.core_bit) % 2]) for i in range(self.count)
        ]
        return lax.ppermute(values, ("dp", "rep"), moves)

    def sides(self, device):
        core = 1 if device & self.core_bit else 0
        return [
            1 if device & self.bits(hop)[core] else 0 for hop in range(self.hops)
        ]

    def scatter(self, where, factors, keep, send):
        unit = keep.shape[0] >> (self.hops - 1)
        terms = [keep]
        for hop in range(self.hops):
            if hop:
                send = fold(hop, self.hops, where, factors, unit, terms)
            got = self.swap(send, hop)
            beside = yield send
            terms.append(got if beside is None else tie(got, beside))
        return fold(self.hops, self.hops, where, factors, unit, terms)

    def owners(self):
        found = [0] * self.count
        for device in range(self.count):
            core = (device // self.core_bit) % 2
            chunk = 0
            for hop in range(self.hops):
                chunk = 2 * chunk + (1 if device & self.bits(hop)[core] else 0)
            found[chunk] = device
        return tuple(found)


class Wide:
    def __init__(self, ring):
        self.ring = ring
        order = ring.orders[0]
        even = [order[n : n + 2] for n in range(0, len(order), 2)]
        odd = list(even)
        if len(even) > 1 and len(even[1]) == 2:
            odd[0], odd[1] = even[1], even[0]
        self.groups = list(zip(even, odd))

    def place(self, device, group):
        core = 1 if device & self.ring.core_bit else 0
        spot = 0
        for bit in self.groups[group][core]:
            spot = 2 * spot + (1 if device & bit else 0)
        return spot

    def table(self):
        ring = self.ring
        rows = []
        for device in range(ring.count):
            rows.append(
                [device, device ^ ring.core_bit]
                + ring.sides(device)
                + [self.place(device, n) for n in range(len(self.groups))]
            )
        table = jnp.array(rows, jnp.int32)
        return lax.dynamic_index_in_dim(table, ring.index, 0, keepdims=False)

    def owners(self):
        found = [0] * self.ring.count
        for device in range(self.ring.count):
            chunk = 1 if device & self.ring.core_bit else 0
            for group, pair in enumerate(self.groups):
                chunk = chunk * 2 ** len(pair[0]) + self.place(device, group)
            found[chunk] = device
        return tuple(found)

    def swap(self, values, group, mask):
        ring = self.ring
        jumps = []
        for bits in self.groups[group]:
            jump = 0
            for n, bit in enumerate(reversed(bits)):
                jump |= bit if mask >> n & 1 else 0
            jumps.append(jump)
        moves = [
            (i, i ^ jumps[1 if i & ring.core_bit else 0]) for i in range(ring.count)
        ]
        return lax.ppermute(values, ("dp", "rep"), moves)

    def scatter(self, where, keep, send):
        ring = self.ring
        got = ring.swap(send, 0)
        beside = yield send
        terms = [keep, got if beside is None else tie(got, beside)]
        for group, pair in enumerate(self.groups):
            fan = 2 ** len(pair[0])
            own, *sends = split(SIDES + ring.hops + group, fan, where, terms)
            gots = [
                self.swap(values, group, mask + 1) for mask, values in enumerate(sends)
            ]
            beside = yield own
            if beside is not None:
                gots = [tie(got, beside) for got in gots]
            terms = [own] + gots
        return split(0, 1, where, terms)[0]


class Flow:
    def __init__(self, steps):
        self.steps = steps
        self.done = False
        self.sent = None
        self.result = None
        self.push(None)

    def push(self, beside):
        if self.done:
            return
        try:
            self.sent = self.steps.send(beside)
        except StopIteration as stop:
            self.done, self.sent, self.result = True, None, stop.value

    def drain(self):
        while not self.done:
            self.push(None)
        return self.result


def body(sizes, *args):
    (
        block_input,
        expert_out,
        upstream,
        lead_index,
        lead_frames,
        lead_embed,
        first_gain,
        first_shift,
        attend_weight,
        query_bias,
        value_bias,
        merge_weight,
        merge_bias,
        second_gain,
        second_shift,
        expand_weight,
        expand_bias,
        shrink_weight,
        shrink_bias,
        router_weight,
        router_bias,
        correction,
    ) = args
    rows, features = block_input.shape
    channels = correction.shape[0]
    leads = lead_embed.shape[0]
    hidden = expand_bias.shape[0]
    devices = sizes["dp"] * sizes["rep"]
    pairs = features // LANES
    grain = 4 * devices
    ring = Ring(sizes)
    wide = Wide(ring)
    where = wide.table()
    first_group = SIDES + ring.hops

    tall = max(8, 2048 // devices)
    mine = lead_index[0].astype(full)
    seen = lax.optimization_barrier(
        lax.all_gather(
            lax.optimization_barrier(jnp.full((tall, LANES), mine)), ("dp", "rep")
        )
    )
    first, projected, *own = project(
        lead_index,
        block_input,
        lead_embed,
        first_gain,
        first_shift,
        attend_weight,
        query_bias,
        value_bias,
    )
    probs, mixed, inverse = attend(projected)

    group = up_to(channels, 16)
    spans, heights = {}, [0, 0]
    for name, half, height in (
        ("expand", 0, features * hidden // LANES),
        ("merge", 0, features * features // LANES),
        ("shrink", 1, features * hidden // LANES),
        ("router", 1, features * 3 * group // LANES),
        ("expand_bias", 1, hidden // LANES),
        ("shrink_bias", 1, pairs),
        ("merge_bias", 1, pairs),
        ("second_gain", 1, pairs),
        ("second_shift", 1, pairs),
        ("head", 1, up_to(4 * group, LANES) // LANES),
    ):
        spans[name] = (half, heights[half])
        heights[half] += height
    vector_rows = up_to(heights[1] - spans["expand_bias"][1], 8)
    height = up_to(max(heights[0], spans["expand_bias"][1] + vector_rows), grain)
    tables = (
        lead_embed,
        merge_weight,
        merge_bias,
        second_gain,
        second_shift,
        expand_weight,
        expand_bias,
        shrink_weight,
        shrink_bias,
        router_weight.T,
        router_bias,
        correction,
    )
    blended, d_mid, *rest = middle(
        spans,
        height,
        group,
        where,
        lead_index,
        block_input,
        mixed,
        inverse,
        expert_out.T,
        upstream.T,
        tables,
    )
    d_across, d_down = rest[:pairs], rest[pairs : 2 * pairs]
    keep, send = rest[2 * pairs :]
    weight, leads_seen = weights_of(
        where,
        lead_frames,
        keep,
        seen,
    )

    flow = None
    if ring.hops:
        flow = Flow(ring.scatter(where, weight, keep, tie(send, seen)))
        flow.push(weight)
    plan = ((4,), (2, 1, 1), (4,))
    d_query, d_pair = [], []
    for pair in range(pairs):
        carried = ()
        base = 0
        for steps in plan[pair]:
            ahead = ()
            if base + steps == sum(plan[pair]) and pair + 1 < pairs:
                ahead = (own[pair + 1], d_across[pair + 1], d_down[pair + 1])
            token = where if flow is None or flow.done else tie(where, flow.sent)
            carried = attend_back(
                pair,
                base,
                steps,
                token,
                ahead,
                own[pair],
                d_across[pair],
                d_down[pair],
                probs,
                carried,
            )
            base += steps
            if flow is not None:
                flow.push(carried[0])
        d_query.append(carried[0])
        d_pair.append(carried[1])
    places = tuple(
        (n // 5, (n % 5) * features) for n in range(3 * pairs)
    )
    tail_height = up_to(5 * features, grain)
    now = weight if flow is None else tie(weight, flow.drain())
    tail_keep, tail_send, biases = weigh(
        places, tail_height, where, now, first, d_query, d_pair
    )
    late = None
    if ring.hops:
        late = Flow(wide.scatter(where, tail_keep, tail_send))
    carried = ()
    base = 0
    for steps in (rows // ROWS // 2,) * 2:
        now = weight if late is None else tie(weight, late.sent)
        grad_input, sums = finish(
            base,
            steps,
            lead_index,
            now,
            block_input,
            lead_embed,
            first_gain,
            attend_weight,
            d_mid,
            d_query,
            d_pair,
            carried,
        )
        base += steps
        carried = (sums, biases, grad_input)
        if late is not None:
            late.push(sums)
    extra = sums.shape[0]
    if ring.hops:
        owners = ring.owners()
        chunks = lax.all_gather(flow.result, ("dp", "rep"))
        piece = jnp.concatenate([late.drain(), sums])
        for stage in reversed(range(1, len(wide.groups))):
            fan = 2 ** len(wide.groups[stage][0])
            gots = [wide.swap(piece, stage, mask) for mask in range(1, fan)]
            piece = join(first_group + stage, where, [piece] + gots)
        gots = [
            wide.swap(piece, 0, mask) for mask in range(1, 2 ** len(wide.groups[0][0]))
        ]
        chunks = tie(chunks, piece)
        chunk = 2 * tail_height // devices
    else:
        owners = (0, 1)
        chunks = jnp.stack([keep, send]) * weight[0]
        chunk = tail_height
        piece = jnp.concatenate([tail_keep, sums])
        got = jnp.concatenate([tail_send, jnp.zeros_like(sums)])
        leads_seen = jnp.concatenate([leads_seen, leads_seen + leads])
    grad_expand, grad_shrink, grad_merge, grad_router, vectors = unpack(
        spans, group, channels, owners, features, hidden, vector_rows, chunks
    )
    first_vector = spans["expand_bias"][1]

    def take(name, length):
        start = spans[name][1] - first_vector
        return vectors[start : start + length // LANES].reshape(-1)

    head = take("head", up_to(4 * group, LANES))
    middle_vectors = (
        take("merge_bias", features),
        take("second_gain", features),
        take("second_shift", features),
        take("expand_bias", hidden),
        take("shrink_bias", features),
        head[: 3 * group].reshape(3, group)[:, :channels].reshape(-1),
        head[3 * group : 3 * group + channels],
    )
    if ring.hops:
        gots = [tie(got, vectors) for got in gots]
        piece = join(first_group, where, [piece] + gots)
        got = ring.swap(piece, 0)
        owners = wide.owners()
    grad_attend, grad_embed, small = settle(
        places,
        owners,
        chunk,
        extra,
        leads,
        features,
        where,
        leads_seen,
        piece,
        got,
    )
    small = small[: 4 * pairs].reshape(4, features)
    merge_b, gain_b, shift_b, expand_b, shrink_b, router_b, correct = middle_vectors
    return (
        blended.T,
        grad_input,
        grad_embed,
        small[0],
        small[1],
        grad_attend,
        small[2],
        small[3],
        grad_merge,
        merge_b,
        gain_b,
        shift_b,
        grad_expand,
        expand_b,
        grad_shrink,
        shrink_b,
        grad_router.T,
        router_b,
        correct,
    )


def solution(mesh):
    split = P(("dp", "rep"), None)
    sizes = dict(mesh.shape)
    return jax.shard_map(
        functools.partial(body, sizes),
        mesh=mesh,
        in_specs=(split, split, split, P(("dp", "rep"))) + (P(),) * 18,
        out_specs=(split, split) + (P(),) * 17,
        check_vma=False,
    )
```

```python
import functools

import jax
import jax.numpy as jnp
from jax import lax
from jax.experimental import pallas as pl
from jax.experimental.pallas import tpu as pltpu
from jax.sharding import PartitionSpec as P

HEADS = 6
EPSILON = 1e-05
PENALTY = 1.0
GELU_COEF = 0.7978845608028654
GELU_CUBE = 0.044715
LOG2E = 1.4426950408889634
LANES = 128
ROWS = 512
KEYS = 512
LIMIT = 56 * 2**20
BACK_LIMIT = 26 * 2**20
NORM_ROWS = 1024

low = jnp.bfloat16
full = jnp.float32


def mul(left, right, dims=((1,), (0,))):
    return lax.dot_general(left, right, (dims, ((), ())), preferred_element_type=full)


NT = ((1,), (1,))
TN = ((0,), (0,))


def params(count, limit=LIMIT):
    return pltpu.CompilerParams(
        dimension_semantics=("arbitrary",) * count, vmem_limit_bytes=limit
    )


def whole(shape):
    return pl.BlockSpec(shape, lambda *step: (0,) * len(shape))


SCALAR = pl.BlockSpec(memory_space=pltpu.SMEM)


def normalize(values):
    centre = jnp.mean(values, axis=-1, keepdims=True)
    centred = values - centre
    spread = jnp.mean(centred * centred, axis=-1, keepdims=True)
    scale = lax.rsqrt(spread + EPSILON)
    return centred * scale, scale


def norm_back(grad, unit, scale, gain):
    e = grad * gain
    first = jnp.mean(e, axis=-1, keepdims=True)
    second = jnp.mean(e * unit, axis=-1, keepdims=True)
    return scale * (e - first - unit * second)


def column_sum(values):
    return jnp.sum(values, axis=0, keepdims=True)


def project_kernel(
    lead, x, embed, gain, shift, weight, query_b, value_b, first, projected, *own
):
    stream = x[...] + embed[pl.ds(lead[0], 1), :]
    unit, _ = normalize(stream)
    rounded = (unit * gain[...][None, :] + shift[...][None, :]).astype(low)
    first[...] = rounded.T
    features = x.shape[1]
    query_row = query_b[...][None, :]
    bias = jnp.concatenate(
        [query_row, jnp.zeros_like(query_row), value_b[...][None, :]], axis=1
    )
    product = (mul(rounded, weight[...]) + bias).astype(low)
    pairs = projected.shape[0]
    for pair in range(pairs):
        for kind in range(3):
            block = kind * pairs + pair
            values = product[:, block * LANES : (block + 1) * LANES]
            projected[pair, kind] = values
            own[pair][kind] = values


def project(lead, x, embed, gain, shift, weight, query_b, value_b):
    rows, features = x.shape
    tables = (embed, gain, shift, weight, query_b, value_b)
    return pl.pallas_call(
        project_kernel,
        grid=(rows // NORM_ROWS,),
        in_specs=[SCALAR, pl.BlockSpec((NORM_ROWS, features), lambda i: (i, 0))]
        + [whole(table.shape) for table in tables],
        out_specs=[
            pl.BlockSpec((features, NORM_ROWS), lambda i: (0, i)),
            pl.BlockSpec((features // LANES, 3, NORM_ROWS, LANES), lambda i: (0, 0, i, 0)),
        ]
        + [pl.BlockSpec((3, NORM_ROWS, LANES), lambda i: (0, i, 0))] * (features // LANES),
        out_shape=[
            jax.ShapeDtypeStruct((features, rows), low),
            jax.ShapeDtypeStruct((features // LANES, 3, rows, LANES), low),
        ]
        + [jax.ShapeDtypeStruct((3, rows, LANES), low)] * (features // LANES),
        compiler_params=params(1),
        name="project",
    )(lead, x, *tables)


def attend_kernel(size, q, k, v, probs, mixed, inverse, turned):
    keys = k.shape[2]
    count = q.shape[2]
    scaling = size ** (-0.5) * LOG2E

    @pl.when(pl.program_id(1) == 0)
    def _():
        across = v[0, 0].T
        tail = lax.broadcasted_iota(jnp.int32, (16, keys), 0)
        ones = jnp.where(tail == 0, 1.0, 0.0).astype(low)
        for head in range(2):
            turned[head, 0:size, :] = across[head * size : (head + 1) * size, :]
            turned[head, size : size + 16, :] = ones

    lane = lax.broadcasted_iota(jnp.int32, (1, LANES), 1)

    def scores(head, start):
        mask = jnp.where(lane // size == head, 1.0, 0.0).astype(low)
        return mul(k[0, 0, start : start + keys, :], q[0, 0] * mask, NT) * scaling

    def finish(head, total):
        spread = total[size : size + 1, :]
        inv = 1.0 / spread
        inverse[0, head : head + 1, :] = inv
        mixed[head * size : (head + 1) * size, :] = (total[0:size, :] * inv).astype(low)
        return spread

    extremes = []
    for head in range(2):
        total = jnp.zeros((size + 16, count), full)
        for start in (0,):
            p = jnp.exp2(scores(head, start)).astype(low)
            probs[0, head, start : start + keys, :] = p
            total = total + mul(turned[head, :, start : start + keys], p)
        spread = finish(head, total)
        extremes.append(spread)

    both = jnp.concatenate(extremes, axis=0)
    inside = jnp.where((both > 1e-18) & (both < 1e18), 1.0, 0.0)

    @pl.when(jnp.min(inside) < 0.5)
    def _():
        for head in range(2):
            top = jnp.full((1, count), -jnp.inf, full)
            for start in (0,):
                top = jnp.maximum(
                    top, jnp.max(scores(head, start), axis=0, keepdims=True)
                )
            total = jnp.zeros((size + 16, count), full)
            for start in (0,):
                p = jnp.exp2(scores(head, start) - top).astype(low)
                probs[0, head, start : start + keys, :] = p
                total = total + mul(turned[head, :, start : start + keys], p)
            finish(head, total)


def attend(projected):
    pairs, _, rows, _ = projected.shape
    features = pairs * LANES
    size = features // HEADS
    return pl.pallas_call(
        functools.partial(attend_kernel, size),
        grid=(pairs, rows // ROWS),
        in_specs=[
            pl.BlockSpec((1, 1, ROWS, LANES), lambda p, i: (p, 0, i, 0)),
            pl.BlockSpec((1, 1, rows, LANES), lambda p, i: (p, 1, 0, 0)),
            pl.BlockSpec((1, 1, rows, LANES), lambda p, i: (p, 2, 0, 0)),
        ],
        out_specs=[
            pl.BlockSpec((1, 2, rows, ROWS), lambda p, i: (p, 0, 0, i)),
            pl.BlockSpec((LANES, ROWS), lambda p, i: (p, i)),
            pl.BlockSpec((1, 8, ROWS), lambda p, i: (p, 0, i)),
        ],
        out_shape=[
            jax.ShapeDtypeStruct((pairs, 2, rows, rows), low),
            jax.ShapeDtypeStruct((features, rows), low),
            jax.ShapeDtypeStruct((pairs, 8, rows), full),
        ],
        scratch_shapes=[pltpu.VMEM((2, size + 16, rows), low)],
        compiler_params=params(2),
        name="attend",
    )(projected, projected, projected)


def middle_kernel(
    spans,
    size,
    group,
    side,
    lead,
    x,
    mixed,
    inverse,
    experts,
    upstream,
    embed,
    merge_w,
    merge_b,
    gain,
    shift,
    expand_w,
    expand_b,
    shrink_w,
    shrink_b,
    router_in,
    router_b,
    correct,
    blended,
    d_mid,
    *rest,
):
    pairs = x.shape[1] // LANES
    d_across, d_down = rest[:pairs], rest[pairs : 2 * pairs]
    keep, send, grads, lanes, router_w, columns, sems = rest[2 * pairs :]
    features = x.shape[1]
    step = x.shape[0]
    hidden_size = expand_w.shape[1]
    channels = upstream.shape[0]
    chunk = hidden_size // 2

    @pl.when(pl.program_id(0) == 0)
    def _():
        grads[...] = jnp.zeros_like(grads)
        lanes[...] = jnp.zeros_like(lanes)
        weights = router_in[...].astype(full)
        wide = up_to(3 * channels, LANES)

        def down(row, width):
            row = jnp.concatenate(
                [row, jnp.zeros((1, width - row.shape[1]), full)], axis=1
            )
            return jnp.broadcast_to(row, (8, width)).T

        biases = down(router_b[...][None, :], wide)
        columns[...] = jnp.zeros_like(columns)
        for e in range(3):
            rows = slice(e * channels, (e + 1) * channels)
            router_w[e * group : (e + 1) * group, :] = jnp.concatenate(
                [weights[rows, :], jnp.zeros((group - channels, features), full)],
                axis=0,
            ).astype(low)
            columns[e * group : e * group + channels, 0:8] = biases[rows, :]
        columns[0:channels, 8:16] = down(correct[...][None, :], LANES)[:channels, :]

    def add(name, values, part=0):
        half, base = spans[name]
        height = values.shape[0]
        for block in range(values.shape[1] // LANES):
            start = base + (part + block) * height
            grads[half, start : start + height, :] += values[
                :, block * LANES : (block + 1) * LANES
            ]

    stream = x[...] + embed[pl.ds(lead[0], 1), :]
    mid = stream + mul(mixed[...], merge_w[...], TN) + merge_b[...][None, :]
    unit, scale = normalize(mid)
    gain_row = gain[...][None, :]
    second = (unit * gain_row + shift[...][None, :]).astype(low)
    output = mid + shrink_b[...][None, :]
    bias = expand_b[...][None, :]
    hidden, slope = [], []
    for start in range(0, hidden_size, chunk):
        part = slice(start, start + chunk)
        u = mul(second, expand_w[:, part]) + bias[:, part]
        square = u * u
        t = jnp.tanh(u * (GELU_COEF + GELU_COEF * GELU_CUBE * square))
        half = 0.5 + 0.5 * t
        act = u * half
        slope.append(
            half
            + act
            * (1.0 - half)
            * (2.0 * GELU_COEF + 6.0 * GELU_COEF * GELU_CUBE * square)
        )
        act = act.astype(low)
        hidden.append(act)
        output = output + mul(act, shrink_w[part, :])
    output_low = output.astype(low)
    logits = mul(router_w[...], output_low, NT) + columns[:, 0:1]
    valid = lax.broadcasted_iota(jnp.int32, (group, 1), 0) < channels
    parts = [logits[e * group : (e + 1) * group, :] for e in range(3)]
    largest = jnp.maximum(jnp.maximum(parts[0], parts[1]), parts[2])
    parts = [part - largest for part in parts]
    raised = [jnp.exp(part) for part in parts]
    total = raised[0] + raised[1] + raised[2]
    shared = jnp.log(total)
    logs = [part - shared for part in parts]
    share = 1.0 / total
    gates = [value * share for value in raised]

    def widen(values):
        return jnp.concatenate(
            [values, jnp.zeros((group - channels, step), full)], axis=0
        )

    frames = [
        widen(experts[e * channels : (e + 1) * channels, :]) for e in range(3)
    ]
    up = widen(upstream[...])
    mix = gates[0] * frames[0] + gates[1] * frames[1] + gates[2] * frames[2]
    entropy = -(gates[0] * logs[0] + gates[1] * logs[1] + gates[2] * logs[2])
    blended[...] = mix[:channels, :] + columns[:channels, 8:9]
    d_parts = [
        jnp.where(
            valid,
            gates[e] * (up * (frames[e] - mix) - PENALTY * (logs[e] + entropy)),
            0.0,
        )
        for e in range(3)
    ]
    for index, values in enumerate(d_parts + [up]):
        for start in range(0, step, LANES):
            lanes[index * group : (index + 1) * group, :] += values[
                :, start : start + LANES
            ]
    d_logits_low = jnp.concatenate(d_parts, axis=0).astype(low)
    add("router", mul(d_logits_low, output_low))
    d_output = mul(d_logits_low, router_w[...], TN)
    add("shrink_bias", column_sum(d_output))
    d_output_low = d_output.astype(low)
    d_turned = d_output_low.T
    second_turned = second.T
    d_second = jnp.zeros_like(d_output)
    for index, start in enumerate(range(0, hidden_size, chunk)):
        part = slice(start, start + chunk)
        d_pre = mul(d_output_low, shrink_w[part, :], NT) * slope[index]
        add("expand_bias", column_sum(d_pre), start // LANES)
        d_pre_low = d_pre.astype(low)
        d_second = d_second + mul(d_pre_low, expand_w[:, part], NT)
        add("expand", mul(second_turned, d_pre_low), start // LANES)
        add("shrink", mul(d_turned, hidden[index]), start // LANES)
    add("second_gain", column_sum(d_second * unit))
    add("second_shift", column_sum(d_second))
    grad_mid = d_output + norm_back(d_second, unit, scale, gain_row)
    d_mid[...] = grad_mid
    add("merge_bias", column_sum(grad_mid))
    d_mid_low = grad_mid.astype(low)
    add("merge", mul(mixed[...], d_mid_low))
    d_mixed = mul(merge_w[...], d_mid_low, NT).astype(low).astype(full)
    row = lax.broadcasted_iota(jnp.int32, (size, step), 0)
    stack = []
    for head in range(features // size):
        span = slice(head * size, (head + 1) * size)
        odd = head % 2
        inv = inverse[head // 2, odd : odd + 1, :]
        scaled = (d_mixed[span, :] * inv).astype(low)
        stack.append(scaled)
        centre = -column_sum(scaled.astype(full) * mixed[span, :].astype(full))
        one = centre.astype(low).astype(full)
        two = (centre - one).astype(low).astype(full)
        extra = jnp.where(
            row == 0,
            one,
            jnp.where(row == 1, two, jnp.where(row == 2, centre - one - two, 0.0)),
        ).astype(low)
        across = d_across[head // 2]
        across[odd, odd * size : (odd + 1) * size, :] = scaled
        across[odd, (1 - odd) * size : (2 - odd) * size, :] = extra
    for pair in range(pairs):
        d_down[pair][...] = jnp.concatenate(stack[2 * pair : 2 * pair + 2], axis=0).T

    @pl.when(pl.program_id(0) == pl.num_programs(0) - 1)
    def _():
        sums = column_sum(lanes[...].T)
        width = sums.shape[1]
        wide = up_to(width, LANES)
        sums = jnp.concatenate([sums, jnp.zeros((1, wide - width), full)], axis=1)
        add("head", sums)
        copies = [
            pltpu.make_async_copy(grads.at[side[SIDES]], keep, sems.at[0]),
            pltpu.make_async_copy(grads.at[1 - side[SIDES]], send, sems.at[1]),
        ]
        for copy in copies:
            copy.start()
        for copy in copies:
            copy.wait()


def middle(spans, height, group, side, lead, x, mixed, inverse, experts, upstream, tables):
    rows, features = x.shape
    size = features // HEADS
    channels = upstream.shape[0]
    step = ROWS
    pairs = features // LANES
    anywhere = pl.BlockSpec(memory_space=pl.ANY)
    return pl.pallas_call(
        functools.partial(middle_kernel, spans, size, group),
        grid=(rows // step,),
        in_specs=[
            SCALAR,
            SCALAR,
            pl.BlockSpec((step, features), lambda i: (i, 0)),
            pl.BlockSpec((features, step), lambda i: (0, i)),
            pl.BlockSpec((inverse.shape[0], 8, step), lambda i: (0, 0, i)),
            pl.BlockSpec((experts.shape[0], step), lambda i: (0, i)),
            pl.BlockSpec((channels, step), lambda i: (0, i)),
        ]
        + [whole(table.shape) for table in tables],
        out_specs=[
            pl.BlockSpec((channels, step), lambda i: (0, i)),
            pl.BlockSpec((step, features), lambda i: (i, 0)),
        ]
        + [pl.BlockSpec((2, LANES, step), lambda i: (0, 0, i))] * pairs
        + [pl.BlockSpec((step, LANES), lambda i: (i, 0))] * pairs
        + [anywhere, anywhere],
        out_shape=[
            jax.ShapeDtypeStruct((channels, rows), full),
            jax.ShapeDtypeStruct((rows, features), full),
        ]
        + [jax.ShapeDtypeStruct((2, LANES, rows), low)] * pairs
        + [jax.ShapeDtypeStruct((rows, LANES), low)] * pairs
        + [jax.ShapeDtypeStruct((height, LANES), full)] * 2,
        scratch_shapes=[
            pltpu.VMEM((2, height, LANES), full),
            pltpu.VMEM((4 * group, LANES), full),
            pltpu.VMEM((3 * group, features), low),
            pltpu.VMEM((3 * group, LANES), full),
            pltpu.SemaphoreType.DMA((2,)),
        ],
        compiler_params=params(1),
        name="middle",
    )(side, lead, x, mixed, inverse, experts, upstream, *tables)


def attend_back_kernel(size, pair, base, steps, last_part, ahead, token, *refs):
    refs = refs[ahead:]
    if base == 0:
        projected, d_across, d_down, probs, d_query, d_pair, total, held, sems = refs
        carry = None
    else:
        projected, d_across, d_down, probs, carry, earlier, *refs = refs
        d_query, d_pair, total, held, sems = refs
        d_pair[:, : base * KEYS, :] = earlier[:, : base * KEYS, :]
    rows = d_down.shape[0]
    scaling = size ** (-0.5)
    lane = lax.broadcasted_iota(jnp.int32, (1, LANES), 1)

    def fetch(step, slot):
        return pltpu.make_async_copy(
            probs.at[pair, :, pl.ds((base + step) * KEYS, KEYS), :],
            held.at[slot],
            sems.at[slot],
        )

    fetch(0, 0).start()
    total[...] = jnp.zeros_like(total) if carry is None else carry[...]

    def one_step(step, unused):
        slot = lax.rem(step, 2)

        @pl.when(step + 1 < steps)
        def _():
            fetch(step + 1, 1 - slot).start()

        fetch(step, slot).wait()
        at = pl.ds(pl.multiple_of((base + step) * KEYS, KEYS), KEYS)
        v = projected[2, at, :]
        k_across = projected[1, at, :].T
        d_keys, d_values = [], []
        for head in range(2):
            other = (1 - head) * size
            data = jnp.where(lane // size == head, 1.0, 0.0).astype(low)
            ones = jnp.where((lane >= other) & (lane < other + 3), 1.0, 0.0)
            values = v * data + ones.astype(low)
            p = held[slot, head]
            d_p = mul(values, d_across[head])
            d_s = (p.astype(full) * d_p).astype(low)
            span = slice(head * size, (head + 1) * size)
            total[span, :] += mul(k_across[span, :], d_s)
            d_values.append(mul(p, d_down[...]))
            d_keys.append(mul(d_s, projected[0]))
        d_pair[0, at, :] = (jnp.where(lane < size, *d_keys) * scaling).astype(low)
        d_pair[1, at, :] = jnp.where(lane < size, *d_values).astype(low)
        return unused

    lax.fori_loop(0, steps, one_step, 0)
    if last_part:
        d_query[...] = (total[...].T * scaling).astype(low)
    else:
        d_query[...] = total[...]


def attend_back(
    pair, base, steps, token, ahead, projected, d_across, d_down, probs, carried
):
    rows = d_down.shape[0]
    size = LANES // 2
    all_steps = rows // KEYS
    last_part = base + steps == all_steps
    across = (rows, LANES) if last_part else (LANES, rows)
    vmem = pl.BlockSpec(memory_space=pltpu.VMEM)
    return pl.pallas_call(
        functools.partial(
            attend_back_kernel, size, pair, base, steps, last_part, len(ahead)
        ),
        in_specs=[SCALAR]
        + [vmem] * len(ahead)
        + [vmem, vmem, vmem, pl.BlockSpec(memory_space=pl.ANY)]
        + [vmem] * len(carried),
        out_specs=[vmem, vmem],
        out_shape=[
            jax.ShapeDtypeStruct(across, low if last_part else full),
            jax.ShapeDtypeStruct((2, rows, LANES), low),
        ],
        scratch_shapes=[
            pltpu.VMEM((LANES, rows), full),
            pltpu.VMEM((2, 2, KEYS, rows), low),
            pltpu.SemaphoreType.DMA((2,)),
        ],
        compiler_params=pltpu.CompilerParams(vmem_limit_bytes=BACK_LIMIT),
        cost_estimate=pl.CostEstimate(
            flops=10 * rows * rows * 256 * steps // all_steps,
            bytes_accessed=rows * rows * 4 * steps // all_steps,
            transcendentals=0,
        ),
        name="attend_back",
    )(token, *ahead, projected, d_across, d_down, probs, *carried)


def weigh_kernel(pairs, places, side, weight, first, *refs):
    d_query, d_pair = refs[:pairs], refs[pairs : 2 * pairs]
    keep, send, sums, grads, sems = refs[2 * pairs :]
    features = first.shape[0]
    grads[...] = jnp.zeros_like(grads)
    sums[...] = jnp.zeros_like(sums)
    parts = []
    for kind in range(3):
        for pair in range(pairs):
            values = d_query[pair][...] if kind == 0 else d_pair[pair][kind - 1]
            parts.append(values)
            if kind != 1:
                sums[
                    kind // 2 : kind // 2 + 1, pair * LANES : (pair + 1) * LANES
                ] = weight[0] * column_sum(values.astype(full))
    for start in range(0, len(parts), 2):
        some = parts[start : start + 2]
        product = mul(first[...], jnp.concatenate(some, axis=1)) * weight[0]
        for index in range(len(some)):
            half, base = places[start + index]
            grads[half, base : base + features, :] = product[
                :, index * LANES : (index + 1) * LANES
            ]
    copies = [
        pltpu.make_async_copy(grads.at[side[SIDES]], keep, sems.at[0]),
        pltpu.make_async_copy(grads.at[1 - side[SIDES]], send, sems.at[1]),
    ]
    for copy in copies:
        copy.start()
    for copy in copies:
        copy.wait()


def weigh(places, height, side, weight, first, d_query, d_pair):
    features = first.shape[0]
    vmem = pl.BlockSpec(memory_space=pltpu.VMEM)
    anywhere = pl.BlockSpec(memory_space=pl.ANY)
    pairs = len(d_query)
    return pl.pallas_call(
        functools.partial(weigh_kernel, pairs, places),
        in_specs=[SCALAR, SCALAR, vmem] + [vmem] * (2 * pairs),
        out_specs=[anywhere, anywhere, vmem],
        out_shape=[
            jax.ShapeDtypeStruct((height, LANES), full),
            jax.ShapeDtypeStruct((height, LANES), full),
            jax.ShapeDtypeStruct((8, features), full),
        ],
        scratch_shapes=[
            pltpu.VMEM((2, height, LANES), full),
            pltpu.SemaphoreType.DMA((2,)),
        ],
        compiler_params=pltpu.CompilerParams(vmem_limit_bytes=20 * 2**20),
        cost_estimate=pl.CostEstimate(
            flops=18 * d_query[0].shape[0] * features * features,
            bytes_accessed=d_query[0].shape[0] * features * 8,
            transcendentals=0,
        ),
        name="weigh",
    )(side, weight, first, *d_query, *d_pair)


def finish_kernel(pairs, last_part, lead, weight, x, embed, gain, wide, d_mid, *rest):
    d_query, d_pair, rest = rest[:pairs], rest[pairs : 2 * pairs], rest[2 * pairs :]
    if last_part:
        earlier, biases, _, grad_input, vectors, sums = rest
    else:
        grad_input, sums = rest
    step = pl.program_id(0)

    @pl.when(step == 0)
    def _():
        sums[...] = earlier[...] if last_part else jnp.zeros_like(sums)

    stream = x[...] + embed[pl.ds(lead[0], 1), :]
    unit, scale = normalize(stream)
    parts = []
    for kind in range(3):
        for pair in range(pairs):
            parts.append(d_query[pair][...] if kind == 0 else d_pair[pair][kind - 1])
    d_first = mul(jnp.concatenate(parts, axis=1), wide[...], NT)
    d_stream = (
        d_mid[...] + norm_back(d_first, unit, scale, gain[...][None, :])
    ) * weight[0]
    grad_input[...] = d_stream
    sums[0:1, :] += column_sum(d_first * unit) * weight[0]
    sums[1:2, :] += column_sum(d_first) * weight[0]
    sums[2:3, :] += column_sum(d_stream)

    if last_part:

        @pl.when(step == pl.num_programs(0) - 1)
        def _():
            vectors[...] = jnp.zeros_like(vectors)
            for index, (ref, at) in enumerate(
                ((sums, 0), (sums, 1), (biases, 0), (biases, 1), (sums, 2))
            ):
                for block in range(pairs):
                    row = index * pairs + block
                    vectors[row : row + 1, :] = ref[
                        at : at + 1, block * LANES : (block + 1) * LANES
                    ]


def finish(base, steps, lead, weight, x, embed, gain, wide, d_mid, d_query, d_pair, carried):
    rows, features = x.shape
    pairs = len(d_query)
    total = rows // ROWS
    last_part = base + steps == total
    height = up_to(5 * pairs, 8)
    row_spec = pl.BlockSpec((ROWS, features), lambda i: (base + i, 0))
    small = pl.BlockSpec((8, features), lambda i: (0, 0))
    return pl.pallas_call(
        functools.partial(finish_kernel, pairs, last_part),
        grid=(steps,),
        in_specs=[
            SCALAR,
            SCALAR,
            row_spec,
            whole(embed.shape),
            whole(gain.shape),
            whole(wide.shape),
            row_spec,
        ]
        + [pl.BlockSpec((ROWS, LANES), lambda i: (base + i, 0))] * pairs
        + [pl.BlockSpec((2, ROWS, LANES), lambda i: (0, base + i, 0))] * pairs
        + ([small, small, pl.BlockSpec(memory_space=pl.ANY)] if last_part else []),
        out_specs=[row_spec, whole((height, LANES)) if last_part else small],
        out_shape=[
            jax.ShapeDtypeStruct((rows, features), full),
            jax.ShapeDtypeStruct((height, LANES) if last_part else (8, features), full),
        ],
        scratch_shapes=[pltpu.VMEM((8, features), full)] if last_part else [],
        input_output_aliases={9 + 2 * pairs: 0} if last_part else {},
        compiler_params=params(1, 24 * 2**20),
        cost_estimate=pl.CostEstimate(
            flops=6 * rows * features * features * steps // total,
            bytes_accessed=rows * features * 18 * steps // total,
            transcendentals=0,
        ),
        name="finish",
    )(lead, weight, x, embed, gain, wide, d_mid, *d_query, *d_pair, *carried)


def pieces_of(start, height, chunk):
    found = []
    done = 0
    while done < height:
        at = start + done
        inside = at % chunk
        size = min(height - done, chunk - inside)
        found.append((at // chunk, inside, done, size))
        done += size
    return found


def unpack_kernel(spans, group, channels, owners, *refs):
    chunks, expand, shrink, merge, router, vectors, grads, turned, sems = refs
    chunk = chunks.shape[1]
    half = len(owners) // 2
    features, hidden = expand.shape
    copies = []

    def copy(source, target):
        copies.append(pltpu.make_async_copy(source, target, sems.at[len(copies)]))
        copies[-1].start()
        return copies[-1]

    arrivals = [
        copy(chunks.at[owner], grads.at[pl.ds(n * chunk, chunk)])
        for n, owner in enumerate(owners)
    ]
    here = 0
    for target, name in ((expand, "expand"), (merge, "merge")):
        for index in range(target.shape[1] // LANES):
            base = spans[name][1] + index * features
            while here * chunk < base + features:
                arrivals[here].wait()
                here += 1
            copy(
                grads.at[pl.ds(base, features)],
                target.at[:, pl.ds(index * LANES, LANES)],
            )
    for index in range(hidden // LANES):
        base = half * chunk + spans["shrink"][1] + index * features
        while here * chunk < base + features:
            arrivals[here].wait()
            here += 1
        rows = pl.ds(index * LANES, LANES)
        turned[rows, :] = grads[base : base + features, :].T
        copy(turned.at[rows], shrink.at[rows])
    for arrival in arrivals[here:]:
        arrival.wait()
    rows = 3 * group
    for index in range(features // LANES):
        base = half * chunk + spans["router"][1] + index * rows
        for e in range(3):
            start = base + e * group
            router[
                e * channels : (e + 1) * channels, index * LANES : (index + 1) * LANES
            ] = grads[start : start + channels, :]
    first = half * chunk + spans["expand_bias"][1]
    vectors[...] = grads[first : first + vectors.shape[0], :]
    for last in copies[len(owners) :]:
        last.wait()


def unpack(spans, group, channels, owners, features, hidden, tall, chunks):
    vmem = pl.BlockSpec(memory_space=pltpu.VMEM)
    anywhere = pl.BlockSpec(memory_space=pl.ANY)
    chunk = chunks.shape[1]
    half = len(owners) // 2
    moves = len(owners) + (2 * hidden + features) // LANES
    return pl.pallas_call(
        functools.partial(unpack_kernel, spans, group, channels, owners),
        in_specs=[anywhere],
        out_specs=[anywhere, anywhere, anywhere, vmem, vmem],
        out_shape=[
            jax.ShapeDtypeStruct((features, hidden), full),
            jax.ShapeDtypeStruct((hidden, features), full),
            jax.ShapeDtypeStruct((features, features), full),
            jax.ShapeDtypeStruct((3 * channels, features), full),
            jax.ShapeDtypeStruct((tall, LANES), full),
        ],
        scratch_shapes=[
            pltpu.VMEM((2 * half * chunk, LANES), full),
            pltpu.VMEM((hidden, features), full),
            pltpu.SemaphoreType.DMA((moves,)),
        ],
        compiler_params=pltpu.CompilerParams(vmem_limit_bytes=LIMIT),
        cost_estimate=pl.CostEstimate(
            flops=8 * 10**9, bytes_accessed=half * chunk * 2048, transcendentals=0
        ),
        name="unpack",
    )(chunks)


def join_kernel(group, spots, *refs):
    pieces, (out, sems) = refs[:-2], refs[-2:]
    height = pieces[0].shape[0]
    copies = []
    for mask, rows in enumerate(pieces):
        start = pl.multiple_of((spots[group] ^ mask) * height, 8)
        copies.append(
            pltpu.make_async_copy(rows, out.at[pl.ds(start, height)], sems.at[mask])
        )
    for copy in copies:
        copy.start()
    for copy in copies:
        copy.wait()


def join(group, spots, pieces):
    anywhere = pl.BlockSpec(memory_space=pl.ANY)
    return pl.pallas_call(
        functools.partial(join_kernel, group),
        in_specs=[SCALAR] + [anywhere] * len(pieces),
        out_specs=anywhere,
        out_shape=jax.ShapeDtypeStruct(
            (len(pieces) * pieces[0].shape[0], LANES), full
        ),
        scratch_shapes=[pltpu.SemaphoreType.DMA((len(pieces),))],
        compiler_params=pltpu.CompilerParams(vmem_limit_bytes=2**20),
        name="join",
    )(spots, *pieces)


def split_kernel(count, spots, *refs):
    outs = refs[-(len(refs) // (count + 1)) :]
    for mask, out in enumerate(outs):
        total = refs[mask * count][...]
        for index in range(1, count):
            total = total + refs[mask * count + index][...]
        out[...] = total


def split(group, fan, spots, terms):
    height = terms[0].shape[0] // fan

    def spec(mask):
        if fan == 1:
            return pl.BlockSpec((height, LANES), lambda i, spots: (0, 0))
        return pl.BlockSpec((height, LANES), lambda i, spots: (spots[group] ^ mask, 0))

    return pl.pallas_call(
        functools.partial(split_kernel, len(terms)),
        grid_spec=pltpu.PrefetchScalarGridSpec(
            num_scalar_prefetch=1,
            grid=(1,),
            in_specs=[spec(mask) for mask in range(fan) for _ in terms],
            out_specs=[pl.BlockSpec((height, LANES), lambda i, spots: (0, 0))] * fan,
        ),
        out_shape=[jax.ShapeDtypeStruct((height, LANES), full)] * fan,
        compiler_params=pltpu.CompilerParams(
            dimension_semantics=("arbitrary",), vmem_limit_bytes=16 * 2**20
        ),
        name="split",
    )(spots, *(list(terms) * fan))


def settle_kernel(places, owners, extra, side, leads, mine, got, *refs):
    attend, embed, vectors, held, table, sems = refs
    features = attend.shape[0]
    pairs = features // LANES
    count, stride, _ = mine.shape
    chunk = stride - extra

    def run(halves):
        arrivals = []
        for half in range(2):
            arrivals.append(
                pltpu.make_async_copy(
                    halves[half].at[:, pl.ds(chunk, extra), :],
                    held.at[half],
                    sems.at[half],
                )
            )
        leaving = []
        for index, (half, base) in enumerate(places):
            for n, inside, done, size in pieces_of(base, features, chunk):
                leaving.append(
                    pltpu.make_async_copy(
                        halves[half].at[n, pl.ds(inside, size)],
                        attend.at[pl.ds(done, size), pl.ds(index * LANES, LANES)],
                        sems.at[2 + len(leaving)],
                    )
                )
        for copy in arrivals + leaving:
            copy.start()
        table[...] = jnp.zeros_like(table)
        for copy in arrivals:
            copy.wait()
        total = jnp.zeros((extra, LANES), full)
        row = lax.broadcasted_iota(jnp.int32, (table.shape[1], LANES), 0).astype(full)
        for half in range(2):
            for n in range(count):
                rows = held[half, n]
                total = total + rows
                owner = owners[half * count + n]
                here = row == leads[owner : owner + 1, :]
                for block in range(pairs):
                    at = 4 * pairs + block
                    table[block] += jnp.where(here, rows[at : at + 1, :], 0.0)
        vectors[...] = total
        for block in range(pairs):
            embed[:, block * LANES : (block + 1) * LANES] = table[block]
        for copy in leaving:
            copy.wait()

    @pl.when(side[SIDES] == 0)
    def _():
        run((mine, got))

    @pl.when(side[SIDES] != 0)
    def _():
        run((got, mine))


def settle(places, owners, chunk, extra, leads, features, side, seen, mine, got):
    vmem = pl.BlockSpec(memory_space=pltpu.VMEM)
    anywhere = pl.BlockSpec(memory_space=pl.ANY)
    count = mine.shape[0] // (chunk + extra)
    moves = sum(len(pieces_of(base, features, chunk)) for _, base in places)
    return pl.pallas_call(
        functools.partial(settle_kernel, places, owners, extra),
        in_specs=[SCALAR, vmem, anywhere, anywhere],
        out_specs=[anywhere, vmem, vmem],
        out_shape=[
            jax.ShapeDtypeStruct((features, 3 * features), full),
            jax.ShapeDtypeStruct((leads, features), full),
            jax.ShapeDtypeStruct((extra, LANES), full),
        ],
        scratch_shapes=[
            pltpu.VMEM((2, count, extra, LANES), full),
            pltpu.VMEM((features // LANES, leads, LANES), full),
            pltpu.SemaphoreType.DMA((2 + moves,)),
        ],
        compiler_params=pltpu.CompilerParams(vmem_limit_bytes=32 * 2**20),
        name="settle",
    )(
        side,
        seen,
        mine.reshape(count, chunk + extra, LANES),
        got.reshape(count, chunk + extra, LANES),
    )


def fold_kernel(count, sides, factors, *refs):
    total = refs[0][...] * factors[0]
    for index in range(1, count):
        total = total + refs[index][...] * factors[min(index, 2)]
    refs[count][...] = total


def fold(hop, hops, sides, factors, unit, terms):
    def spec(made):
        def index(i, sides, factors):
            at = i
            for step in range(made + 1, hop):
                at = at + sides[SIDES + step] * 2 ** (hops - 1 - step)
            if hop < hops:
                at = at + (1 - sides[SIDES + hop]) * 2 ** (hops - 1 - hop)
            return at, 0

        return pl.BlockSpec((unit, LANES), index)

    length = 2 ** (hops - 1 - hop) if hop < hops else 1
    return pl.pallas_call(
        functools.partial(fold_kernel, len(terms)),
        grid_spec=pltpu.PrefetchScalarGridSpec(
            num_scalar_prefetch=2,
            grid=(length,),
            in_specs=[spec(max(index - 1, 0)) for index in range(len(terms))],
            out_specs=pl.BlockSpec((unit, LANES), lambda i, *tables: (i, 0)),
        ),
        out_shape=jax.ShapeDtypeStruct((length * unit, LANES), full),
        compiler_params=pltpu.CompilerParams(
            dimension_semantics=("arbitrary",), vmem_limit_bytes=8 * 2**20
        ),
        name="fold",
    )(sides, factors, *terms)


def weights_kernel(index, frames, near, seen, weights, leads, held, sem):
    copy = pltpu.make_async_copy(seen.at[:, pl.ds(0, 8), :], held, sem)
    copy.start()
    total = lax.fori_loop(
        0, frames.shape[0], lambda n, sofar: sofar + frames[n], jnp.int32(0)
    ).astype(full)
    copy.wait()
    count = held.shape[0]
    rows = held[:, 0, :]
    leads[...] = rows
    device = lax.broadcasted_iota(jnp.int32, rows.shape, 0)
    for side in range(2):
        lead = jnp.max(jnp.where(device == index[side], rows, 0.0))
        same = jnp.sum(jnp.where(rows == lead, 1.0, 0.0)) / LANES
        chosen = frames[lead.astype(jnp.int32)].astype(full)
        weights[side] = chosen * count / (same * total)
    weights[2] = jnp.float32(1.0)


def weights_of(index, frames, near, seen):
    count = seen.shape[0]
    smem = pl.BlockSpec(memory_space=pltpu.SMEM)
    return pl.pallas_call(
        weights_kernel,
        in_specs=[
            smem,
            smem,
            pl.BlockSpec(memory_space=pltpu.VMEM),
            pl.BlockSpec(memory_space=pl.ANY),
        ],
        out_specs=[smem, pl.BlockSpec(memory_space=pltpu.VMEM)],
        out_shape=[
            jax.ShapeDtypeStruct((3,), full),
            jax.ShapeDtypeStruct((count, LANES), full),
        ],
        scratch_shapes=[
            pltpu.VMEM((count, 8, LANES), full),
            pltpu.SemaphoreType.DMA,
        ],
        compiler_params=pltpu.CompilerParams(vmem_limit_bytes=8 * 2**20),
        name="weights",
    )(index, frames, near, seen)


def up_to(value, step):
    return -(-value // step) * step


def tie(value, *others):
    return lax.optimization_barrier((value,) + others)[0]


def routes(sizes):
    inner = sizes["rep"]
    outer = sizes["dp"]
    if outer % 2:
        return 0, ((), ())
    far = [inner << n for n in range(1, outer.bit_length() - 1)]
    near = [1 << n for n in range(inner.bit_length() - 1)]
    even = []
    for n in range(max(len(far), len(near))):
        even += far[n : n + 1] + near[n : n + 1]
    odd = even[1:3] + even[:1] + even[3:]
    return inner, (tuple(even), tuple(odd))


SIDES = 2


class Ring:
    def __init__(self, sizes):
        self.count = sizes["dp"] * sizes["rep"]
        self.core_bit, self.orders = routes(sizes)
        self.hops = len(self.orders[0]) + 1 if self.core_bit else 0
        self.index = lax.axis_index(("dp", "rep"))

    def bits(self, hop):
        if hop == 0:
            return self.core_bit, self.core_bit
        return self.orders[0][hop - 1], self.orders[1][hop - 1]

    def swap(self, values, hop):
        pair = self.bits(hop)
        moves = [
            (i, i ^ pair[(i // self.core_bit) % 2]) for i in range(self.count)
        ]
        return lax.ppermute(values, ("dp", "rep"), moves)

    def sides(self, device):
        core = 1 if device & self.core_bit else 0
        return [
            1 if device & self.bits(hop)[core] else 0 for hop in range(self.hops)
        ]

    def scatter(self, where, factors, keep, send):
        unit = keep.shape[0] >> (self.hops - 1)
        terms = [keep]
        for hop in range(self.hops):
            if hop:
                send = fold(hop, self.hops, where, factors, unit, terms)
            got = self.swap(send, hop)
            beside = yield send
            terms.append(got if beside is None else tie(got, beside))
        return fold(self.hops, self.hops, where, factors, unit, terms)

    def owners(self):
        found = [0] * self.count
        for device in range(self.count):
            core = (device // self.core_bit) % 2
            chunk = 0
            for hop in range(self.hops):
                chunk = 2 * chunk + (1 if device & self.bits(hop)[core] else 0)
            found[chunk] = device
        return tuple(found)


class Wide:
    def __init__(self, ring):
        self.ring = ring
        order = ring.orders[0]
        even = [order[n : n + 2] for n in range(0, len(order), 2)]
        odd = list(even)
        if len(even) > 1 and len(even[1]) == 2:
            odd[0], odd[1] = even[1], even[0]
        self.groups = list(zip(even, odd))

    def place(self, device, group):
        core = 1 if device & self.ring.core_bit else 0
        spot = 0
        for bit in self.groups[group][core]:
            spot = 2 * spot + (1 if device & bit else 0)
        return spot

    def table(self):
        ring = self.ring
        rows = []
        for device in range(ring.count):
            rows.append(
                [device, device ^ ring.core_bit]
                + ring.sides(device)
                + [self.place(device, n) for n in range(len(self.groups))]
            )
        table = jnp.array(rows, jnp.int32)
        return lax.dynamic_index_in_dim(table, ring.index, 0, keepdims=False)

    def owners(self):
        found = [0] * self.ring.count
        for device in range(self.ring.count):
            chunk = 1 if device & self.ring.core_bit else 0
            for group, pair in enumerate(self.groups):
                chunk = chunk * 2 ** len(pair[0]) + self.place(device, group)
            found[chunk] = device
        return tuple(found)

    def swap(self, values, group, mask):
        ring = self.ring
        jumps = []
        for bits in self.groups[group]:
            jump = 0
            for n, bit in enumerate(reversed(bits)):
                jump |= bit if mask >> n & 1 else 0
            jumps.append(jump)
        moves = [
            (i, i ^ jumps[1 if i & ring.core_bit else 0]) for i in range(ring.count)
        ]
        return lax.ppermute(values, ("dp", "rep"), moves)

    def scatter(self, where, keep, send):
        ring = self.ring
        got = ring.swap(send, 0)
        beside = yield send
        terms = [keep, got if beside is None else tie(got, beside)]
        for group, pair in enumerate(self.groups):
            fan = 2 ** len(pair[0])
            own, *sends = split(SIDES + ring.hops + group, fan, where, terms)
            gots = [
                self.swap(values, group, mask + 1) for mask, values in enumerate(sends)
            ]
            beside = yield own
            if beside is not None:
                gots = [tie(got, beside) for got in gots]
            terms = [own] + gots
        return split(0, 1, where, terms)[0]


class Flow:
    def __init__(self, steps):
        self.steps = steps
        self.done = False
        self.sent = None
        self.result = None
        self.push(None)

    def push(self, beside):
        if self.done:
            return
        try:
            self.sent = self.steps.send(beside)
        except StopIteration as stop:
            self.done, self.sent, self.result = True, None, stop.value

    def drain(self):
        while not self.done:
            self.push(None)
        return self.result


def body(sizes, *args):
    (
        block_input,
        expert_out,
        upstream,
        lead_index,
        lead_frames,
        lead_embed,
        first_gain,
        first_shift,
        attend_weight,
        query_bias,
        value_bias,
        merge_weight,
        merge_bias,
        second_gain,
        second_shift,
        expand_weight,
        expand_bias,
        shrink_weight,
        shrink_bias,
        router_weight,
        router_bias,
        correction,
    ) = args
    rows, features = block_input.shape
    channels = correction.shape[0]
    leads = lead_embed.shape[0]
    hidden = expand_bias.shape[0]
    devices = sizes["dp"] * sizes["rep"]
    pairs = features // LANES
    grain = 4 * devices
    ring = Ring(sizes)
    wide = Wide(ring)
    where = wide.table()
    first_group = SIDES + ring.hops

    tall = max(8, 2048 // devices)
    mine = lead_index[0].astype(full)
    seen = lax.optimization_barrier(
        lax.all_gather(
            lax.optimization_barrier(jnp.full((tall, LANES), mine)), ("dp", "rep")
        )
    )
    first, projected, *own = project(
        lead_index,
        block_input,
        lead_embed,
        first_gain,
        first_shift,
        attend_weight,
        query_bias,
        value_bias,
    )
    probs, mixed, inverse = attend(projected)

    group = up_to(channels, 16)
    spans, heights = {}, [0, 0]
    for name, half, height in (
        ("expand", 0, features * hidden // LANES),
        ("merge", 0, features * features // LANES),
        ("shrink", 1, features * hidden // LANES),
        ("router", 1, features * 3 * group // LANES),
        ("expand_bias", 1, hidden // LANES),
        ("shrink_bias", 1, pairs),
        ("merge_bias", 1, pairs),
        ("second_gain", 1, pairs),
        ("second_shift", 1, pairs),
        ("head", 1, up_to(4 * group, LANES) // LANES),
    ):
        spans[name] = (half, heights[half])
        heights[half] += height
    vector_rows = up_to(heights[1] - spans["expand_bias"][1], 8)
    height = up_to(max(heights[0], spans["expand_bias"][1] + vector_rows), grain)
    tables = (
        lead_embed,
        merge_weight,
        merge_bias,
        second_gain,
        second_shift,
        expand_weight,
        expand_bias,
        shrink_weight,
        shrink_bias,
        router_weight.T,
        router_bias,
        correction,
    )
    blended, d_mid, *rest = middle(
        spans,
        height,
        group,
        where,
        lead_index,
        block_input,
        mixed,
        inverse,
        expert_out.T,
        upstream.T,
        tables,
    )
    d_across, d_down = rest[:pairs], rest[pairs : 2 * pairs]
    keep, send = rest[2 * pairs :]
    weight, leads_seen = weights_of(
        where,
        lead_frames,
        keep,
        seen,
    )

    flow = None
    if ring.hops:
        flow = Flow(ring.scatter(where, weight, keep, tie(send, seen)))
        flow.push(weight)
    plan = ((4,), (2, 1, 1), (4,))
    d_query, d_pair = [], []
    for pair in range(pairs):
        carried = ()
        base = 0
        for steps in plan[pair]:
            ahead = ()
            if base + steps == sum(plan[pair]) and pair + 1 < pairs:
                ahead = (own[pair + 1], d_across[pair + 1], d_down[pair + 1])
            token = where if flow is None or flow.done else tie(where, flow.sent)
            carried = attend_back(
                pair,
                base,
                steps,
                token,
                ahead,
                own[pair],
                d_across[pair],
                d_down[pair],
                probs,
                carried,
            )
            base += steps
            if flow is not None:
                flow.push(carried[0])
        d_query.append(carried[0])
        d_pair.append(carried[1])
    places = tuple(
        (n // 5, (n % 5) * features) for n in range(3 * pairs)
    )
    tail_height = up_to(5 * features, grain)
    now = weight if flow is None else tie(weight, flow.drain())
    tail_keep, tail_send, biases = weigh(
        places, tail_height, where, now, first, d_query, d_pair
    )
    late = None
    if ring.hops:
        late = Flow(wide.scatter(where, tail_keep, tail_send))
    carried = ()
    base = 0
    for steps in (rows // ROWS // 2,) * 2:
        now = weight if late is None else tie(weight, late.sent)
        grad_input, sums = finish(
            base,
            steps,
            lead_index,
            now,
            block_input,
            lead_embed,
            first_gain,
            attend_weight,
            d_mid,
            d_query,
            d_pair,
            carried,
        )
        base += steps
        carried = (sums, biases, grad_input)
        if late is not None:
            late.push(sums)
    extra = sums.shape[0]
    if ring.hops:
        owners = ring.owners()
        chunks = lax.all_gather(flow.result, ("dp", "rep"))
        piece = jnp.concatenate([late.drain(), sums])
        for stage in reversed(range(1, len(wide.groups))):
            fan = 2 ** len(wide.groups[stage][0])
            gots = [wide.swap(piece, stage, mask) for mask in range(1, fan)]
            piece = join(first_group + stage, where, [piece] + gots)
        gots = [
            wide.swap(piece, 0, mask) for mask in range(1, 2 ** len(wide.groups[0][0]))
        ]
        chunks = tie(chunks, piece)
        chunk = 2 * tail_height // devices
    else:
        owners = (0, 1)
        chunks = jnp.stack([keep, send]) * weight[0]
        chunk = tail_height
        piece = jnp.concatenate([tail_keep, sums])
        got = jnp.concatenate([tail_send, jnp.zeros_like(sums)])
        leads_seen = jnp.concatenate([leads_seen, leads_seen + leads])
    grad_expand, grad_shrink, grad_merge, grad_router, vectors = unpack(
        spans, group, channels, owners, features, hidden, vector_rows, chunks
    )
    first_vector = spans["expand_bias"][1]

    def take(name, length):
        start = spans[name][1] - first_vector
        return vectors[start : start + length // LANES].reshape(-1)

    head = take("head", up_to(4 * group, LANES))
    middle_vectors = (
        take("merge_bias", features),
        take("second_gain", features),
        take("second_shift", features),
        take("expand_bias", hidden),
        take("shrink_bias", features),
        head[: 3 * group].reshape(3, group)[:, :channels].reshape(-1),
        head[3 * group : 3 * group + channels],
    )
    if ring.hops:
        gots = [tie(got, vectors) for got in gots]
        piece = join(first_group, where, [piece] + gots)
        got = ring.swap(piece, 0)
        owners = wide.owners()
    grad_attend, grad_embed, small = settle(
        places,
        owners,
        chunk,
        extra,
        leads,
        features,
        where,
        leads_seen,
        piece,
        got,
    )
    small = small[: 4 * pairs].reshape(4, features)
    merge_b, gain_b, shift_b, expand_b, shrink_b, router_b, correct = middle_vectors
    return (
        blended.T,
        grad_input,
        grad_embed,
        small[0],
        small[1],
        grad_attend,
        small[2],
        small[3],
        grad_merge,
        merge_b,
        gain_b,
        shift_b,
        grad_expand,
        expand_b,
        grad_shrink,
        shrink_b,
        grad_router.T,
        router_b,
        correct,
    )


def solution(mesh):
    split = P(("dp", "rep"), None)
    sizes = dict(mesh.shape)
    return jax.shard_map(
        functools.partial(body, sizes),
        mesh=mesh,
        in_specs=(split, split, split, P(("dp", "rep"))) + (P(),) * 18,
        out_specs=(split, split) + (P(),) * 17,
        check_vma=False,
    )
```
